256 devices in a mesh: dp: 16 (over x, y), zero: 16 (over z, core).
Axes of the slice: x: 4, y: 4, z: 8, core: 2. Of those that a mesh axis runs over, the one named last changes fastest.
Arguments:
- frames: bfloat16 [16, 16, 768, 1536], P('dp', 'zero')
- segments: int32 [16, 16, 768], P('dp', 'zero'), may hold values from 0 to 2, never falling along the last dimension, each value on 1 to 384 neighbouring positions
- targets: int32 [16, 16, 12], P('dp', 'zero'), may hold values from -1 to 15, as said below
- cotangent: bfloat16 [16, 16, 512, 1536], P('dp', 'zero'), may hold values from -6 to 6
- w_out: bfloat16 [1536, 1536], P(None, 'zero'), may hold values from -0.15625 to 0.15625
- kernel: bfloat16 [32, 1536], P(None, 'zero'), may hold values from -1 to 1
- norm_params: bfloat16 [2, 1536], P(None, 'zero'), may hold values from 0.29882812 to 1.5
Outputs:
- module_out: bfloat16 [16, 16, 512, 1536], P('dp', 'zero')
- grad_out_weight: float32 [1536, 1536], P(None, 'zero')
- grad_kernel: float32 [32, 1536], P(None, 'zero')
- grad_norm: float32 [2, 1536], P(None, 'zero')
The draws below stay inside these ranges and needn't reach their ends.
Inputs may be any that keep to these rules, and one draw needn't show every extreme that they name: `targets`: within each device's slots the padding blocks come after the live ones. For each zero index, counting the live blocks in order of dp index and then block, the n-th goes to data group n mod 16; every data group receives exactly 8 blocks; a device sends at most 1 block to one data group.
All inputs are finite; a program needn't handle non-finite values.
Results may differ from the reference program's by a relative error of at most 0.005.
Values may be sent and summed in bfloat16 or wider, within the bound.
No kernel may reach another device: no remote copies, remote signals or barrier semaphores. Data moves between devices by JAX's collectives and lax.ppermute only.
A program may use at most 128 MiB of HBM per device.

```python
import math
import jax
import jax.numpy as jnp
import numpy as np
from jax import lax

MODEL_WIDTH = 1536
KER = 32
BLOCK_FRAMES = 64
BLOCKS_PER_DEVICE = 8
NB = 12
UTT = 3
LEFT = 16
SPAN = 95
UMAX = 384
NR = 131072
N_DP = 16
N_ZERO = 16


def draw_frames(key, part):
    key = jax.random.fold_in(key, 11)
    base_key, row_key, col_key = jax.random.split(key, 3)
    shape = (N_DP, N_ZERO, NB * BLOCK_FRAMES, MODEL_WIDTH)
    row_scale = 10.0 ** jax.random.uniform(row_key, (N_DP, N_ZERO, NB * BLOCK_FRAMES, 1), jnp.float32)
    col_scale = 10.0 ** jax.random.uniform(col_key, (1, 1, 1, MODEL_WIDTH), jnp.float32)
    trend = 0.5 + jnp.arange(N_DP * N_ZERO, dtype=jnp.float32).reshape(N_DP, N_ZERO, 1, 1) / (N_DP * N_ZERO)
    base = jnp.clip(jax.random.normal(base_key, shape, jnp.float32), -4.0, 4.0)
    return (0.3 * base * row_scale * col_scale * trend).astype(jnp.bfloat16)


def draw_targets(key, part):
    key = jax.random.fold_in(key, 23)
    keys = jax.random.split(key, N_ZERO)

    def column(sub):
        order_key, shift_key = jax.random.split(sub)
        order = jax.random.permutation(order_key, N_DP)
        shift = jax.random.randint(shift_key, (N_DP // 2,), 0, 5).astype(jnp.int32)
        shift = shift.at[0].set(4)
        signed = jnp.concatenate([shift, -shift])
        counts = jnp.zeros((N_DP,), jnp.int32).at[order].set(BLOCKS_PER_DEVICE + signed)
        live = jnp.arange(NB, dtype=jnp.int32)[None, :] < counts[:, None]
        flat = live.reshape(-1)
        rank = jnp.cumsum(flat.astype(jnp.int32)) - 1
        dest = jnp.where(flat, rank % N_DP, -1)
        return dest.reshape(N_DP, NB)
    cols = jax.vmap(column)(keys)
    return jnp.transpose(cols, (1, 0, 2)).astype(jnp.int32)


def strengthened(entries, rng, source, target, shards_of, factor):
    owner, partner = [(jnp.arange(entries.shape[dim]) // (entries.shape[dim] // shards_of)).reshape([-1 if axis == dim else 1 for axis in range(entries.ndim)]) for dim in (source, target)]
    chosen = jax.random.permutation(rng, shards_of)[partner]
    strong = (owner == chosen) | (owner == (partner + shards_of // 2) % shards_of)
    return jnp.where(strong, factor * entries, entries)


def block_levels(key, extent, pieces, low, largest):
    gain, own = 1.0, jax.random.fold_in(key, 6)
    for position, parts in pieces:
        steps = jnp.exp(jax.random.uniform(jax.random.fold_in(own, position), (parts,), jnp.float32, low / len(pieces), largest / len(pieces)))
        gain = gain * jnp.repeat(steps, extent[position] // parts).reshape([-1 if axis == position else 1 for axis in range(len(extent))])
    return gain


def profile(number_of, total, reach, lean):
    loads = [(1 << 20) // math.isqrt(grade ** lean) + 1 for grade in range(2, number_of + 1)]
    spare, given = total - reach - (number_of - 1), [1] * (number_of - 1)
    while spare > 0:
        movable = [i for i in range(number_of - 1) if given[i] < reach]
        mass, budget = sum([loads[i] for i in movable]), spare
        for i in movable:
            more = min(reach - given[i], max(1, budget * loads[i] // mass), spare)
            given[i] = given[i] + more
            spare = spare - more
    return np.array([reach] + given)


def uneven_parts(stream_key, amount, total, limit, lean):
    if amount == 2:
        one = jax.random.randint(stream_key, (), max(1, total - limit), min(limit, total - 1) + 1)
        return jnp.stack([one, total - one])
    tallies = jnp.asarray(profile(amount, total, limit, lean), jnp.int32)
    pairs = (amount - 1) // 2
    giver, taker = tallies[1:1 + 2 * pairs:2], tallies[2:2 + 2 * pairs:2]
    room = jnp.minimum(giver - 1, limit - taker)
    shifted = jax.random.randint(jax.random.fold_in(stream_key, 1), (pairs,), 0, 1 << 20) % (room + 1)
    tallies = tallies.at[1:1 + 2 * pairs:2].set(giver - shifted).at[2:2 + 2 * pairs:2].set(taker + shifted)
    return tallies[jax.random.permutation(jax.random.fold_in(stream_key, 2), amount)]


def centred(rng, dims, scale, bound, cuts=(), kind=jnp.bfloat16):
    result = scale * jax.random.normal(rng, dims, jnp.float32)
    if cuts:
        result = result * block_levels(rng, dims, cuts, -0.22, 0.18)
    return jnp.clip(result, -bound, bound).astype(kind)


def gaussian_with(stream_key, extent, scale, limit, pieces, heavy, kind=jnp.bfloat16):
    entries = scale * jax.random.normal(stream_key, extent, jnp.float32)
    if pieces:
        entries = entries * block_levels(stream_key, extent, pieces, -0.22, 0.18)
    return jnp.clip(strengthened(entries, jax.random.fold_in(stream_key, 3), *heavy), -limit, limit).astype(kind)


def setup_inputs(seed: int = 0) -> dict:
    streams_of = jax.random.split(jax.random.key(seed), 8)
    frames = draw_frames(jax.random.fold_in(streams_of[7], 71), 0)
    segments = jax.vmap(lambda own: jnp.searchsorted(jnp.cumsum(uneven_parts(own, UTT, NB * BLOCK_FRAMES, UMAX, 2)), jnp.arange(NB * BLOCK_FRAMES), side="right"))(jax.random.split(streams_of[1], N_DP * N_ZERO)).reshape((N_DP, N_ZERO, NB * BLOCK_FRAMES)).astype(jnp.int32)
    targets = draw_targets(jax.random.fold_in(streams_of[7], 71), 0)
    cotangent = gaussian_with(streams_of[3], (N_DP, N_ZERO, BLOCKS_PER_DEVICE * BLOCK_FRAMES, MODEL_WIDTH), 1.0, 6.0, ((0, 16), (1, 16)), (1, 3, 16, 2.0))
    w_out = centred(streams_of[4], (MODEL_WIDTH, MODEL_WIDTH), MODEL_WIDTH ** -0.5, 0.15625, ((1, 16),))
    kernel = centred(streams_of[5], (KER, MODEL_WIDTH), KER ** -0.5, 1.0, ((1, 16),))
    norm_params = jnp.clip(0.29882812 + 1.2011719 * jax.random.uniform(streams_of[6], (2, MODEL_WIDTH), jnp.float32) ** block_levels(streams_of[6], (2, MODEL_WIDTH), ((1, 16),), -0.2, 0.2), 0.29882812, 1.5).astype(jnp.bfloat16)
    return {"frames": frames, "segments": segments, "targets": targets, "cotangent": cotangent, "w_out": w_out, "kernel": kernel, "norm_params": norm_params}


EPS = 1e-05

def column_blocks(frames_col, segs_col, tgt_col):
    live = tgt_col >= 0
    row_live = jnp.repeat(live, BLOCK_FRAMES, axis=1)
    row_seg = jnp.where(row_live, segs_col, -1).astype(jnp.int32)
    after = KER - 1 - LEFT
    pad_frames = jnp.pad(frames_col, ((0, 0), (LEFT, after), (0, 0)))
    pad_segs = jnp.pad(row_seg, ((0, 0), (LEFT, after)), constant_values=-1)
    flat = tgt_col.reshape(-1)
    groups = jnp.arange(N_DP, dtype=jnp.int32)
    hit = (flat[None, :] == groups[:, None]).astype(jnp.int32)
    rank = jnp.cumsum(hit, axis=1).astype(jnp.int32) - 1
    places = jnp.arange(BLOCKS_PER_DEVICE, dtype=jnp.int32)
    chosen = hit[:, None, :] * (rank[:, None, :] == places[None, :, None]).astype(jnp.int32)
    where_q = jnp.arange(N_DP * NB, dtype=jnp.int32)
    pick = lax.optimization_barrier(jnp.sum(chosen * where_q[None, None, :], axis=2)).astype(jnp.int32)
    source = (pick // NB).astype(jnp.int32)
    block = (pick % NB).astype(jnp.int32)

    def cut(src, blk):
        start = (blk * BLOCK_FRAMES).astype(jnp.int32)
        zero_value = jnp.zeros((), jnp.int32)
        piece = lax.dynamic_slice(pad_frames, (src, start, zero_value), (1, SPAN, MODEL_WIDTH))[0]
        label = lax.dynamic_slice(pad_segs, (src, start), (1, SPAN))[0]
        return (piece, label)
    return jax.vmap(jax.vmap(cut))(source, block)

def depthwise(block_pieces, frame_labels, kernel):
    centre = frame_labels[..., LEFT:LEFT + BLOCK_FRAMES]
    total = jnp.zeros(block_pieces.shape[:-2] + (BLOCK_FRAMES, block_pieces.shape[-1]), jnp.float32)
    for tap in range(KER):
        same = (frame_labels[..., tap:tap + BLOCK_FRAMES] == centre).astype(jnp.float32)
        total = total + block_pieces[..., tap:tap + BLOCK_FRAMES, :].astype(jnp.float32) * (same[..., None] * kernel[tap].astype(jnp.float32))
    return total

def kernel_terms(hidden_gradient, block_pieces, frame_labels):
    centre = frame_labels[..., LEFT:LEFT + BLOCK_FRAMES]
    rows_out = []
    for tap in range(KER):
        same = (frame_labels[..., tap:tap + BLOCK_FRAMES] == centre).astype(jnp.float32)
        term = hidden_gradient * block_pieces[..., tap:tap + BLOCK_FRAMES, :].astype(jnp.float32) * same[..., None]
        rows_out.append(lax.optimization_barrier(jnp.sum(term.reshape(-1, term.shape[-1]), axis=0)))
    return jnp.stack(rows_out)

def reference(frames, segments, targets, cotangent, w_out, kernel, norm_params):
    frame_count = jnp.float32(NR)
    columns = jnp.arange(N_ZERO, dtype=jnp.int32)

    def conv_col(block_index):
        block_pieces, frame_labels = column_blocks(frames[:, block_index], segments[:, block_index], targets[:, block_index])
        return (depthwise(block_pieces, frame_labels, kernel), block_pieces, frame_labels)

    def stats(loop_carry, block_index):
        hidden_rows = conv_col(block_index)[0].reshape(-1, MODEL_WIDTH)
        return ((loop_carry[0] + lax.optimization_barrier(jnp.sum(hidden_rows, axis=0)), loop_carry[1] + lax.optimization_barrier(jnp.sum(hidden_rows * hidden_rows, axis=0))), None)
    zeros_d = jnp.zeros((MODEL_WIDTH,), jnp.float32)
    (sum_h, sum_sq), _ = lax.scan(stats, (zeros_d, zeros_d), columns)
    channel_mean = sum_h / frame_count
    var = sum_sq / frame_count - channel_mean * channel_mean
    inverse_deviation = lax.rsqrt(var + EPS)
    norm_scale = norm_params[0].astype(jnp.float32)
    norm_shift = norm_params[1].astype(jnp.float32)

    def forward_pass(block_index):
        hidden_rows, block_pieces, frame_labels = conv_col(block_index)
        normalized_input = (hidden_rows.reshape(-1, MODEL_WIDTH) - channel_mean) * inverse_deviation
        swish_input = normalized_input * norm_scale + norm_shift
        sig = jax.nn.sigmoid(swish_input)
        swish_output = (swish_input * sig).astype(jnp.bfloat16)
        row_gradients = cotangent[:, block_index].reshape(-1, MODEL_WIDTH)
        back = jnp.dot(row_gradients, w_out.T, preferred_element_type=jnp.float32)
        swish_input_gradient = back * (sig * (1.0 + swish_input * (1.0 - sig)))
        return (normalized_input, swish_output, row_gradients, swish_input_gradient, block_pieces, frame_labels)

    def second(loop_carry, block_index):
        normalized_input, swish_output, row_gradients, swish_input_gradient, block_pieces, frame_labels = forward_pass(block_index)
        projected_output = jnp.dot(swish_output, w_out, preferred_element_type=jnp.float32).astype(jnp.bfloat16)
        weight_term = loop_carry[0] + jnp.dot(swish_output.T, row_gradients, preferred_element_type=jnp.float32)
        return ((weight_term, loop_carry[1] + lax.optimization_barrier(jnp.sum(swish_input_gradient, axis=0)), loop_carry[2] + lax.optimization_barrier(jnp.sum(swish_input_gradient * normalized_input, axis=0))), projected_output.reshape(N_DP, BLOCKS_PER_DEVICE * BLOCK_FRAMES, MODEL_WIDTH))
    init = (jnp.zeros((MODEL_WIDTH, MODEL_WIDTH), jnp.float32), zeros_d, zeros_d)
    (grad_w, gradient_sum, gradient_normed_sum), outs = lax.scan(second, init, columns)

    def third(loop_carry, block_index):
        normalized_input, swish_output, row_gradients, swish_input_gradient, block_pieces, frame_labels = forward_pass(block_index)
        hidden_gradient = norm_scale * inverse_deviation * (swish_input_gradient - gradient_sum / frame_count - normalized_input * gradient_normed_sum / frame_count)
        return (loop_carry + kernel_terms(hidden_gradient.reshape(N_DP, BLOCKS_PER_DEVICE, BLOCK_FRAMES, MODEL_WIDTH), block_pieces, frame_labels), None)
    grad_k, _ = lax.scan(third, jnp.zeros((KER, MODEL_WIDTH), jnp.float32), columns)
    module_out = jnp.transpose(outs, (1, 0, 2, 3))
    grad_norm = jnp.stack([gradient_normed_sum, gradient_sum])
    return (module_out, grad_w, grad_k, grad_norm)
```

```python
import jax
import jax.numpy as jnp
from jax import lax
from jax.experimental import pallas as pl
from jax.experimental.pallas import tpu as pltpu
from jax.sharding import PartitionSpec as P

KER = 32
BLOCK = 64
BLOCKS = 8
NB = 12
LEFT = 16
WIN = 96
CHUNK = 32
LANES = 128
EPS = 1e-05
F32 = jnp.float32
BF16 = jnp.bfloat16
SMEM_SPEC = pl.BlockSpec(memory_space=pltpu.SMEM)


def row_iota(rows):
    return lax.broadcasted_iota(jnp.int32, (rows, LANES), 0)


def spread_taps(kern_ref, taps):
    for k in range(KER):
        taps[pl.ds(8 * k, 8), :] = jnp.broadcast_to(kern_ref[pl.ds(k, 1), :], (8, LANES))


def shifted(window, p):
    return [window[pl.ds(p + 8 * i, 8), :] for i in range(7)]


def conv_chunk(window, taps):
    acc = [jnp.zeros((8, LANES), F32) for _ in range(4)]
    for p in range(8):
        xs = shifted(window, p)
        for q in range(4):
            tap = taps[pl.ds(8 * (8 * q + p), 8), :]
            for i in range(4):
                acc[i] = acc[i] + tap * xs[i + q]
    return acc


def pack_kernel(block_ref, x_ref, out_ref, sems):
    def copies(r):
        b = block_ref[r]
        before = pl.multiple_of(jnp.maximum(b * BLOCK - LEFT, 0), 16)
        start = pl.multiple_of(b * BLOCK, 16)
        after = pl.multiple_of(jnp.minimum((b + 1) * BLOCK, NB * BLOCK - 16), 16)
        return [
            pltpu.make_async_copy(
                x_ref.at[pl.ds(before, 16)], out_ref.at[r, pl.ds(0, 16)], sems.at[r, 0]
            ),
            pltpu.make_async_copy(
                x_ref.at[pl.ds(start, 64)], out_ref.at[r, pl.ds(16, 64)], sems.at[r, 1]
            ),
            pltpu.make_async_copy(
                x_ref.at[pl.ds(after, 16)], out_ref.at[r, pl.ds(80, 16)], sems.at[r, 2]
            ),
        ]

    for r in range(16):
        @pl.when(block_ref[r] >= 0)
        def _():
            for copy in copies(r):
                copy.start()

    for r in range(16):
        @pl.when(block_ref[r] >= 0)
        def _():
            for copy in copies(r):
                copy.wait()


def pack(block_of, x):
    return pl.pallas_call(
        pack_kernel,
        out_shape=jax.ShapeDtypeStruct((16, WIN, x.shape[1]), BF16),
        in_specs=[SMEM_SPEC, pl.BlockSpec(memory_space=pl.ANY)],
        out_specs=pl.BlockSpec(memory_space=pl.ANY),
        scratch_shapes=[pltpu.SemaphoreType.DMA((16, 3))],
        name="pack",
    )(block_of, x)


def stats_kernel(bounds_ref, x_ref, kern_ref, out_ref, full, window, taps, sums):
    spread_taps(kern_ref, taps)
    full[pl.ds(0, 16), :] = jnp.zeros((16, LANES), F32)
    full[pl.ds(16 + NB * BLOCK, 16), :] = jnp.zeros((16, LANES), F32)
    full[pl.ds(16, NB * BLOCK), :] = x_ref[...].astype(F32)
    sums[...] = jnp.zeros_like(sums)
    first, second, end = bounds_ref[1], bounds_ref[2], bounds_ref[3]

    def chunk(c, carry):
        row = c * CHUNK
        low = (first <= row).astype(jnp.int32) + (second <= row).astype(jnp.int32)
        top = row + CHUNK - 1
        high = (first <= top).astype(jnp.int32) + (second <= top).astype(jnp.int32)

        def part(u, inner):
            begin, stop = bounds_ref[u], bounds_ref[u + 1]
            rows = row_iota(64) + (row - LEFT)
            source = full[pl.ds(pl.multiple_of(row, 32), 64), :]
            window[...] = jnp.where((rows >= begin) & (rows < stop), source, 0.0)
            acc = conv_chunk(window, taps)
            total, square = sums[pl.ds(0, 8), :], sums[pl.ds(8, 8), :]
            for i in range(4):
                at = row_iota(8) + (row + 8 * i)
                h = jnp.where((at >= begin) & (at < stop), acc[i], 0.0)
                total = total + h
                square = square + h * h
            sums[pl.ds(0, 8), :] = total
            sums[pl.ds(8, 8), :] = square
            return inner

        return lax.fori_loop(low, high + 1, part, carry)

    lax.fori_loop(0, end // CHUNK, chunk, 0)
    out_ref[pl.ds(0, 1), :] = jnp.sum(sums[pl.ds(0, 8), :], axis=0, keepdims=True)
    out_ref[pl.ds(1, 1), :] = jnp.sum(sums[pl.ds(8, 8), :], axis=0, keepdims=True)


def stats(bounds, x, kern):
    width = x.shape[1]
    return pl.pallas_call(
        stats_kernel,
        grid=(width // LANES,),
        out_shape=jax.ShapeDtypeStruct((2, width), F32),
        in_specs=[
            SMEM_SPEC,
            pl.BlockSpec((NB * BLOCK, LANES), lambda c: (0, c)),
            pl.BlockSpec((KER, LANES), lambda c: (0, c)),
        ],
        out_specs=pl.BlockSpec((2, LANES), lambda c: (0, c)),
        scratch_shapes=[
            pltpu.VMEM((32 + NB * BLOCK, LANES), F32),
            pltpu.VMEM((64, LANES), F32),
            pltpu.VMEM((8 * KER, LANES), F32),
            pltpu.VMEM((16, LANES), F32),
        ],
        cost_estimate=pl.CostEstimate(flops=100_000_000, bytes_accessed=3_000_000, transcendentals=0),
        name="stats",
    )(bounds, x, kern)


def live_parts(info_ref, got_ref, window, per_part):
    def slot(s, n):
        valid = info_ref[8 * s] > 0

        @pl.when(valid)
        def _():
            for c in range(2):
                row = LEFT + CHUNK * c
                top = row + CHUNK - 1
                first, second = info_ref[8 * s + 2], info_ref[8 * s + 3]
                low = (first <= row).astype(jnp.int32) + (second <= row).astype(jnp.int32)
                high = (first <= top).astype(jnp.int32) + (second <= top).astype(jnp.int32)
                at = pl.multiple_of(n * BLOCK + c * CHUNK, CHUNK)

                def part(u, carry):
                    begin, stop = info_ref[8 * s + 1 + u], info_ref[8 * s + 2 + u]
                    rows = row_iota(64) + CHUNK * c
                    source = got_ref[s, pl.ds(CHUNK * c, 64), :].astype(F32)
                    window[...] = jnp.where((rows >= begin) & (rows < stop), source, 0.0)
                    per_part(row, at, begin, stop)
                    return carry

                lax.fori_loop(low, high + 1, part, 0)

        return n + valid.astype(jnp.int32)

    lax.fori_loop(0, 16, slot, 0)


def hidden_kernel(info_ref, got_ref, kern_ref, h_ref, window, taps):
    spread_taps(kern_ref, taps)

    def per_part(row, at, begin, stop):
        acc = conv_chunk(window, taps)
        for i in range(4):
            rows = row_iota(8) + (row + 8 * i)
            place = pl.ds(pl.multiple_of(at + 8 * i, 8), 8)
            h_ref[place, :] = jnp.where((rows >= begin) & (rows < stop), acc[i], h_ref[place, :])

    live_parts(info_ref, got_ref, window, per_part)


def hidden(info, got, kern):
    width = got.shape[2]
    return pl.pallas_call(
        hidden_kernel,
        grid=(width // LANES,),
        out_shape=jax.ShapeDtypeStruct((BLOCKS * BLOCK, width), F32),
        in_specs=[
            SMEM_SPEC,
            pl.BlockSpec((16, WIN, LANES), lambda c: (0, 0, c)),
            pl.BlockSpec((KER, LANES), lambda c: (0, c)),
        ],
        out_specs=pl.BlockSpec((BLOCKS * BLOCK, LANES), lambda c: (0, c)),
        scratch_shapes=[pltpu.VMEM((64, LANES), F32), pltpu.VMEM((8 * KER, LANES), F32)],
        cost_estimate=pl.CostEstimate(flops=60_000_000, bytes_accessed=8_000_000, transcendentals=0),
        name="hidden",
    )(info, got, kern)


def terms_kernel(info_ref, got_ref, h_ref, back_ref, norm_ref, out_ref, window, acc_a, acc_x, sums):
    acc_a[...] = jnp.zeros_like(acc_a)
    acc_x[...] = jnp.zeros_like(acc_x)
    sums[...] = jnp.zeros_like(sums)
    mean, inverse = norm_ref[pl.ds(0, 1), :], norm_ref[pl.ds(1, 1), :]
    scale, shift = norm_ref[pl.ds(2, 1), :], norm_ref[pl.ds(3, 1), :]

    def per_part(row, at, begin, stop):
        das, hats = [], []
        sum_x, sum_1 = sums[pl.ds(0, 8), :], sums[pl.ds(8, 8), :]
        for i in range(4):
            place = pl.ds(pl.multiple_of(at + 8 * i, 8), 8)
            rows = row_iota(8) + (row + 8 * i)
            keep = (rows >= begin) & (rows < stop)
            hat = (h_ref[place, :] - mean) * inverse
            a = hat * scale + shift
            sig = jax.nn.sigmoid(a)
            da = back_ref[place, :] * (sig * (1.0 + a * (1.0 - sig)))
            da = jnp.where(keep, da, 0.0)
            hat = jnp.where(keep, hat, 0.0)
            sum_x = sum_x + da * hat
            sum_1 = sum_1 + da
            das.append(da)
            hats.append(hat)
        sums[pl.ds(0, 8), :] = sum_x
        sums[pl.ds(8, 8), :] = sum_1
        for p in range(8):
            xs = shifted(window, p)
            for q in range(4):
                place = pl.ds(8 * (8 * q + p), 8)
                acc_a[place, :] += (das[0] * xs[q] + das[1] * xs[q + 1]) + (
                    das[2] * xs[q + 2] + das[3] * xs[q + 3]
                )
                acc_x[place, :] += (hats[0] * xs[q] + hats[1] * xs[q + 1]) + (
                    hats[2] * xs[q + 2] + hats[3] * xs[q + 3]
                )

    live_parts(info_ref, got_ref, window, per_part)
    out_ref[pl.ds(0, 32), :] = jnp.sum(acc_a[...].reshape(KER, 8, LANES), axis=1)
    out_ref[pl.ds(32, 32), :] = jnp.sum(acc_x[...].reshape(KER, 8, LANES), axis=1)
    out_ref[pl.ds(64, 1), :] = jnp.sum(sums[pl.ds(0, 8), :], axis=0, keepdims=True)
    out_ref[pl.ds(65, 1), :] = jnp.sum(sums[pl.ds(8, 8), :], axis=0, keepdims=True)
    out_ref[pl.ds(66, 6), :] = jnp.zeros((6, LANES), F32)


def terms(info, got, h, back, norm):
    width = got.shape[2]
    return pl.pallas_call(
        terms_kernel,
        grid=(width // LANES,),
        out_shape=jax.ShapeDtypeStruct((72, width), F32),
        in_specs=[
            SMEM_SPEC,
            pl.BlockSpec((16, WIN, LANES), lambda c: (0, 0, c)),
            pl.BlockSpec((BLOCKS * BLOCK, LANES), lambda c: (0, c)),
            pl.BlockSpec((BLOCKS * BLOCK, LANES), lambda c: (0, c)),
            pl.BlockSpec((4, LANES), lambda c: (0, c)),
        ],
        out_specs=pl.BlockSpec((72, LANES), lambda c: (0, c)),
        scratch_shapes=[
            pltpu.VMEM((64, LANES), F32),
            pltpu.VMEM((8 * KER, LANES), F32),
            pltpu.VMEM((8 * KER, LANES), F32),
            pltpu.VMEM((16, LANES), F32),
        ],
        cost_estimate=pl.CostEstimate(
            flops=110_000_000, bytes_accessed=12_000_000, transcendentals=800_000
        ),
        name="terms",
    )(info, got, h, back, norm)


def gather_sum(x, axis):
    copies = jnp.broadcast_to(x[None], (16,) + x.shape)
    return jnp.sum(lax.all_to_all(copies, axis, 0, 0, tiled=True), axis=0)


def per_device(frames, segments, targets, cotangent, w_out, kernel, norm_params):
    x, seg, target_row, cot = frames[0, 0], segments[0, 0], targets[0, 0], cotangent[0, 0]
    width = x.shape[1]
    share = width // 16
    zero_id = lax.axis_index("zero")
    core = lax.rem(zero_id, 2)

    groups = jnp.arange(16, dtype=jnp.int32)
    hit = target_row[None, :] == groups[:, None]
    valid = jnp.any(hit, axis=1)
    block_of = jnp.sum(jnp.where(hit, jnp.arange(NB, dtype=jnp.int32)[None, :], 0), axis=1)
    end = BLOCK * jnp.sum((target_row >= 0).astype(jnp.int32))
    ends = [jnp.minimum(jnp.sum((seg < u).astype(jnp.int32)), end) for u in (1, 2)]
    bounds = jnp.stack([jnp.int32(0), ends[0], ends[1], end])
    base = BLOCK * block_of - LEFT
    info = jnp.clip(bounds[None, :] - base[:, None], 0, WIN)
    info = jnp.concatenate(
        [valid.astype(jnp.int32)[:, None], info, jnp.zeros((16, 3), jnp.int32)], axis=1
    )

    small = jnp.concatenate([kernel, norm_params, jnp.zeros((14, share), BF16)], axis=0)
    small_full = lax.all_to_all(
        jnp.broadcast_to(small[None], (16,) + small.shape), "zero", 0, 0, tiled=True
    )
    small_full = jnp.transpose(small_full, (1, 0, 2)).reshape(48, width).astype(F32)
    kern_full = small_full[:KER]
    info = lax.all_to_all(info, "dp", 0, 0, tiled=True).reshape(128)

    send = pack(jnp.where(valid, block_of, -1), x)
    got = lax.all_to_all(send, "dp", 0, 0, tiled=True)

    w_t = lax.all_gather(w_out.T, "zero", axis=0, tiled=True)

    sums = stats(bounds, x, kern_full)
    sums = gather_sum(gather_sum(sums, "zero"), "dp")
    frame_count = jnp.float32(BLOCKS * BLOCK * 256)
    mean = sums[0] / frame_count
    var = sums[1] / frame_count - mean * mean
    inverse = lax.rsqrt(var + EPS)
    norm = jnp.stack([mean, inverse, small_full[KER], small_full[KER + 1]])

    label = jnp.where(jnp.arange(NB * BLOCK) < end, seg, -1)
    padded = jnp.pad(label, (KER - 1 - LEFT, LEFT), constant_values=-1)
    meets = jnp.stack(
        [
            (padded[KER - 1 - k : KER - 1 - k + NB * BLOCK] == label) & (label >= 0)
            for k in range(KER)
        ]
    )
    x_sums = jnp.dot(meets.astype(BF16), x, preferred_element_type=F32)

    halves = cot.reshape(BLOCKS * BLOCK, 8, 2, share)
    cot_own = lax.dynamic_index_in_dim(halves, core, 2, False).reshape(-1, width // 2)
    cot_send = lax.dynamic_index_in_dim(halves, 1 - core, 2, False).reshape(-1, width // 2)
    swap = [(i, i ^ 1) for i in range(16)]
    cot_other = lax.ppermute(cot_send, "zero", swap)
    back = jnp.dot(cot, w_t, preferred_element_type=F32)

    h = hidden(info, got, kern_full)
    a = (h - mean) * inverse * norm[2] + norm[3]
    sw = (a * jax.nn.sigmoid(a)).astype(BF16)
    sw_other = lax.ppermute(sw, "zero", swap)
    contract = (((0,), (0,)), ((), ()))
    term = lax.dot_general(sw, cot_own, contract, preferred_element_type=F32)
    term = term + lax.dot_general(sw_other, cot_other, contract, preferred_element_type=F32)
    term = term.astype(BF16).reshape(16, share, width // 2)
    term = lax.all_to_all(term, "dp", 0, 0, tiled=True)

    grads = terms(info, got, h, back, norm)
    out = lax.dot_general(
        sw, w_t, (((1,), (1,)), ((), ())), preferred_element_type=F32
    ).astype(BF16)

    grads = jnp.concatenate([grads, x_sums], axis=0)
    grads = jnp.transpose(grads.reshape(104, 16, share), (1, 0, 2))
    grads = jnp.sum(lax.all_to_all(grads, "zero", 0, 0, tiled=True), axis=0)

    term = jnp.sum(term.astype(F32), axis=0)
    term = jnp.transpose(term.reshape(share, 8, share), (1, 0, 2))
    term = lax.all_to_all(
        term,
        "zero",
        0,
        0,
        axis_index_groups=[[i for i in range(16) if i % 2 == c] for c in range(2)],
        tiled=True,
    )
    term = jnp.sum(term, axis=0)

    last = jnp.concatenate([term, grads], axis=0)
    last = lax.all_to_all(
        jnp.broadcast_to(last[None], (16,) + last.shape), "dp", 0, 0, tiled=True
    )
    part_w = last[:, :share].reshape(width, share)
    grads = jnp.sum(last[:, share:], axis=0)

    own = lax.dynamic_slice_in_dim(norm, zero_id * share, share, 1)
    da_x, hat_x, x_k = grads[:KER], grads[KER : 2 * KER], grads[72 : 72 + KER]
    sum_x, sum_1 = grads[64], grads[65]
    part_k = (own[2] * own[1]) * (da_x - (sum_1 / frame_count) * x_k - (sum_x / frame_count) * hat_x)
    return out[None, None], part_w, part_k, jnp.stack([sum_x, sum_1])


def solution(mesh):
    return jax.shard_map(
        per_device,
        mesh=mesh,
        in_specs=(
            P("dp", "zero", None, None),
            P("dp", "zero", None),
            P("dp", "zero", None),
            P("dp", "zero", None, None),
            P(None, "zero"),
            P(None, "zero"),
            P(None, "zero"),
        ),
        out_specs=(P("dp", "zero", None, None), P(None, "zero"), P(None, "zero"), P(None, "zero")),
        check_vma=False,
    )
```

```python
import jax
import jax.numpy as jnp
from jax import lax
from jax.experimental import pallas as pl
from jax.experimental.pallas import tpu as pltpu
from jax.sharding import PartitionSpec as P

KER = 32
BLOCK = 64
BLOCKS = 8
NB = 12
LEFT = 16
WIN = 96
CHUNK = 32
LANES = 128
EPS = 1e-05
F32 = jnp.float32
BF16 = jnp.bfloat16
SMEM_SPEC = pl.BlockSpec(memory_space=pltpu.SMEM)


def cost(microseconds):
    return pl.CostEstimate(
        flops=microseconds * 1_100_000_000, bytes_accessed=1_000_000, transcendentals=0
    )


def row_iota(rows):
    return lax.broadcasted_iota(jnp.int32, (rows, LANES), 0)


def spread_taps(kern_ref, taps):
    for k in range(KER):
        taps[pl.ds(8 * k, 8), :] = jnp.broadcast_to(kern_ref[pl.ds(k, 1), :], (8, LANES))


def shifted(window, p):
    return [window[pl.ds(p + 8 * i, 8), :] for i in range(7)]


def conv_chunk(window, taps):
    acc = [jnp.zeros((8, LANES), F32) for _ in range(4)]
    for p in range(8):
        xs = shifted(window, p)
        for q in range(4):
            tap = taps[pl.ds(8 * (8 * q + p), 8), :]
            for i in range(4):
                acc[i] = acc[i] + tap * xs[i + q]
    return acc


def pack_kernel(block_ref, x_ref, out_ref):
    for i in range(4):
        b = block_ref[4 * pl.program_id(0) + i]

        @pl.when(b >= 0)
        def _():
            before = pl.multiple_of(jnp.maximum(b * BLOCK - LEFT, 0), 16)
            start = pl.multiple_of(b * BLOCK, 16)
            after = pl.multiple_of(jnp.minimum((b + 1) * BLOCK, NB * BLOCK - 16), 16)
            out_ref[i, pl.ds(0, 16), :] = x_ref[pl.ds(before, 16), :]
            out_ref[i, pl.ds(16, 64), :] = x_ref[pl.ds(start, 64), :]
            out_ref[i, pl.ds(80, 16), :] = x_ref[pl.ds(after, 16), :]

        @pl.when(b < 0)
        def _():
            out_ref[i] = jnp.zeros_like(out_ref[i])


def pack(block_of, x):
    rows, width = x.shape
    return pl.pallas_call(
        pack_kernel,
        grid=(4,),
        out_shape=jax.ShapeDtypeStruct((16, WIN, width), BF16),
        in_specs=[SMEM_SPEC, pl.BlockSpec((rows, width), lambda r: (0, 0))],
        out_specs=pl.BlockSpec((4, WIN, width), lambda r: (r, 0, 0)),
        cost_estimate=cost(4),
        compiler_params=pltpu.CompilerParams(vmem_limit_bytes=32 * 1024 * 1024),
        name="pack",
    )(block_of, x)


def stats_kernel(bounds_ref, x_ref, kern_ref, _, out_ref, full, window, taps, sums):
    spread_taps(kern_ref, taps)
    full[pl.ds(0, 16), :] = jnp.zeros((16, LANES), F32)
    full[pl.ds(16 + NB * BLOCK, 16), :] = jnp.zeros((16, LANES), F32)
    full[pl.ds(16, NB * BLOCK), :] = x_ref[...].astype(F32)
    sums[...] = jnp.zeros_like(sums)
    first, second, end = bounds_ref[1], bounds_ref[2], bounds_ref[3]

    def chunk(c, carry):
        row = c * CHUNK
        low = (first <= row).astype(jnp.int32) + (second <= row).astype(jnp.int32)
        top = row + CHUNK - 1
        high = (first <= top).astype(jnp.int32) + (second <= top).astype(jnp.int32)

        def part(u, inner):
            begin, stop = bounds_ref[u], bounds_ref[u + 1]
            rows = row_iota(64) + (row - LEFT)
            source = full[pl.ds(pl.multiple_of(row, 32), 64), :]
            window[...] = jnp.where((rows >= begin) & (rows < stop), source, 0.0)
            acc = conv_chunk(window, taps)
            total, square = sums[pl.ds(0, 8), :], sums[pl.ds(8, 8), :]
            for i in range(4):
                at = row_iota(8) + (row + 8 * i)
                h = jnp.where((at >= begin) & (at < stop), acc[i], 0.0)
                total = total + h
                square = square + h * h
            sums[pl.ds(0, 8), :] = total
            sums[pl.ds(8, 8), :] = square
            return inner

        return lax.fori_loop(low, high + 1, part, carry)

    lax.fori_loop(0, end // CHUNK, chunk, 0)
    out_ref[pl.ds(0, 1), :] = jnp.sum(sums[pl.ds(0, 8), :], axis=0, keepdims=True)
    out_ref[pl.ds(1, 1), :] = jnp.sum(sums[pl.ds(8, 8), :], axis=0, keepdims=True)


def stats(bounds, x, kern, earlier):
    width = x.shape[1]
    return pl.pallas_call(
        stats_kernel,
        grid=(width // LANES,),
        out_shape=jax.ShapeDtypeStruct((2, width), F32),
        in_specs=[
            SMEM_SPEC,
            pl.BlockSpec((NB * BLOCK, LANES), lambda c: (0, c)),
            pl.BlockSpec((KER, LANES), lambda c: (0, c)),
            pl.BlockSpec(memory_space=pl.ANY),
        ],
        out_specs=pl.BlockSpec((2, LANES), lambda c: (0, c)),
        scratch_shapes=[
            pltpu.VMEM((32 + NB * BLOCK, LANES), F32),
            pltpu.VMEM((64, LANES), F32),
            pltpu.VMEM((8 * KER, LANES), F32),
            pltpu.VMEM((16, LANES), F32),
        ],
        cost_estimate=cost(15),
        name="stats",
    )(bounds, x, kern, earlier)


def live_parts(info_ref, got_ref, window, per_part):
    def slot(s, n):
        valid = info_ref[5 * s] > 0

        @pl.when(valid)
        def _():
            for c in range(2):
                row = LEFT + CHUNK * c
                top = row + CHUNK - 1
                first, second = info_ref[5 * s + 2], info_ref[5 * s + 3]
                low = (first <= row).astype(jnp.int32) + (second <= row).astype(jnp.int32)
                high = (first <= top).astype(jnp.int32) + (second <= top).astype(jnp.int32)
                at = pl.multiple_of(n * BLOCK + c * CHUNK, CHUNK)

                def part(u, carry):
                    begin, stop = info_ref[5 * s + 1 + u], info_ref[5 * s + 2 + u]
                    rows = row_iota(64) + CHUNK * c
                    source = got_ref[s, pl.ds(CHUNK * c, 64), :].astype(F32)
                    window[...] = jnp.where((rows >= begin) & (rows < stop), source, 0.0)
                    per_part(row, at, begin, stop)
                    return carry

                lax.fori_loop(low, high + 1, part, 0)

        return n + valid.astype(jnp.int32)

    lax.fori_loop(0, 16, slot, 0)


def hidden_kernel(info_ref, got_ref, kern_ref, *rest):
    h_ref, window, taps = rest[-3:]
    spread_taps(kern_ref, taps)

    def per_part(row, at, begin, stop):
        acc = conv_chunk(window, taps)
        for i in range(4):
            rows = row_iota(8) + (row + 8 * i)
            place = pl.ds(pl.multiple_of(at + 8 * i, 8), 8)
            h_ref[place, :] = jnp.where((rows >= begin) & (rows < stop), acc[i], h_ref[place, :])

    live_parts(info_ref, got_ref, window, per_part)


def hidden(info, got, kern, *earlier):
    width = got.shape[2]
    return pl.pallas_call(
        hidden_kernel,
        grid=(width // LANES,),
        out_shape=jax.ShapeDtypeStruct((BLOCKS * BLOCK, width), F32),
        in_specs=[
            SMEM_SPEC,
            pl.BlockSpec((16, WIN, LANES), lambda c: (0, 0, c)),
            pl.BlockSpec((KER, LANES), lambda c: (0, c)),
        ]
        + [pl.BlockSpec(memory_space=pl.ANY)] * len(earlier),
        out_specs=pl.BlockSpec((BLOCKS * BLOCK, LANES), lambda c: (0, c)),
        scratch_shapes=[pltpu.VMEM((64, LANES), F32), pltpu.VMEM((8 * KER, LANES), F32)],
        cost_estimate=cost(16),
        name="hidden",
    )(info, got, kern, *earlier)


def terms_kernel(info_ref, got_ref, h_ref, back_ref, norm_ref, out_ref, window, acc_a, acc_x, sums):
    acc_a[...] = jnp.zeros_like(acc_a)
    acc_x[...] = jnp.zeros_like(acc_x)
    sums[...] = jnp.zeros_like(sums)
    mean, inverse = norm_ref[pl.ds(0, 1), :], norm_ref[pl.ds(1, 1), :]
    scale, shift = norm_ref[pl.ds(2, 1), :], norm_ref[pl.ds(3, 1), :]

    def per_part(row, at, begin, stop):
        das, hats = [], []
        sum_x, sum_1 = sums[pl.ds(0, 8), :], sums[pl.ds(8, 8), :]
        for i in range(4):
            place = pl.ds(pl.multiple_of(at + 8 * i, 8), 8)
            rows = row_iota(8) + (row + 8 * i)
            keep = (rows >= begin) & (rows < stop)
            hat = (h_ref[place, :] - mean) * inverse
            a = hat * scale + shift
            sig = jax.nn.sigmoid(a)
            da = back_ref[place, :] * (sig * (1.0 + a * (1.0 - sig)))
            da = jnp.where(keep, da, 0.0)
            hat = jnp.where(keep, hat, 0.0)
            sum_x = sum_x + da * hat
            sum_1 = sum_1 + da
            das.append(da)
            hats.append(hat)
        sums[pl.ds(0, 8), :] = sum_x
        sums[pl.ds(8, 8), :] = sum_1
        for p in range(8):
            xs = shifted(window, p)
            for q in range(4):
                place = pl.ds(8 * (8 * q + p), 8)
                acc_a[place, :] += (das[0] * xs[q] + das[1] * xs[q + 1]) + (
                    das[2] * xs[q + 2] + das[3] * xs[q + 3]
                )
                acc_x[place, :] += (hats[0] * xs[q] + hats[1] * xs[q + 1]) + (
                    hats[2] * xs[q + 2] + hats[3] * xs[q + 3]
                )

    live_parts(info_ref, got_ref, window, per_part)
    out_ref[pl.ds(0, 32), :] = jnp.sum(acc_a[...].reshape(KER, 8, LANES), axis=1)
    out_ref[pl.ds(32, 32), :] = jnp.sum(acc_x[...].reshape(KER, 8, LANES), axis=1)
    out_ref[pl.ds(64, 1), :] = jnp.sum(sums[pl.ds(0, 8), :], axis=0, keepdims=True)
    out_ref[pl.ds(65, 1), :] = jnp.sum(sums[pl.ds(8, 8), :], axis=0, keepdims=True)
    out_ref[pl.ds(66, 6), :] = jnp.zeros((6, LANES), F32)


def terms(info, got, h, back, norm):
    width = got.shape[2]
    return pl.pallas_call(
        terms_kernel,
        grid=(width // LANES,),
        out_shape=jax.ShapeDtypeStruct((72, width), F32),
        in_specs=[
            SMEM_SPEC,
            pl.BlockSpec((16, WIN, LANES), lambda c: (0, 0, c)),
            pl.BlockSpec((BLOCKS * BLOCK, LANES), lambda c: (0, c)),
            pl.BlockSpec((BLOCKS * BLOCK, LANES), lambda c: (0, c)),
            pl.BlockSpec((4, LANES), lambda c: (0, c)),
        ],
        out_specs=pl.BlockSpec((72, LANES), lambda c: (0, c)),
        scratch_shapes=[
            pltpu.VMEM((64, LANES), F32),
            pltpu.VMEM((8 * KER, LANES), F32),
            pltpu.VMEM((8 * KER, LANES), F32),
            pltpu.VMEM((16, LANES), F32),
        ],
        cost_estimate=cost(25),
        name="terms",
    )(info, got, h, back, norm)


def zero_step(step):
    if step < 4:
        return [(i, i ^ step) for i in range(16)]
    return [(i, (i + step) % 16) for i in range(16)]


def dp_step(step, row):
    if row:
        return [(i, 4 * (i // 4) + (i + step) % 4) for i in range(16)]
    return [(i, (i + 4 * step) % 16) for i in range(16)]


def add_from(x, axis, steps):
    total = x
    for step in steps:
        total = total + lax.ppermute(x, axis, step)
    return total


def per_device(frames, segments, targets, cotangent, w_out, kernel, norm_params):
    x, seg, target_row, cot = frames[0, 0], segments[0, 0], targets[0, 0], cotangent[0, 0]
    width = x.shape[1]
    share = width // 16
    zero_id = lax.axis_index("zero")
    core = lax.rem(zero_id, 2)

    groups = jnp.arange(16, dtype=jnp.int32)
    hit = target_row[None, :] == groups[:, None]
    valid = jnp.any(hit, axis=1)
    block_of = jnp.sum(jnp.where(hit, jnp.arange(NB, dtype=jnp.int32)[None, :], 0), axis=1)
    end = BLOCK * jnp.sum((target_row >= 0).astype(jnp.int32))
    ends = [jnp.minimum(jnp.sum((seg < u).astype(jnp.int32)), end) for u in (1, 2)]
    bounds = jnp.stack([jnp.int32(0), ends[0], ends[1], end])
    base = BLOCK * block_of - LEFT
    info = jnp.clip(bounds[None, :] - base[:, None], 0, WIN)
    info = jnp.concatenate([valid.astype(jnp.int32)[:, None], info], axis=1)

    small = jnp.concatenate([kernel, norm_params, jnp.zeros((14, share), BF16)], axis=0)
    small_full = lax.all_to_all(
        jnp.broadcast_to(small[None], (16,) + small.shape), "zero", 0, 0, tiled=True
    )
    small_full = jnp.transpose(small_full, (1, 0, 2)).reshape(48, width).astype(F32)
    kern_full = small_full[:KER]
    send = pack(jnp.where(valid, block_of, -1), x)
    got = lax.all_to_all(send, "dp", 0, 0, tiled=True)

    w_t = lax.all_gather(w_out.T, "zero", axis=0, tiled=True)

    sums = stats(bounds, x, kern_full, send)
    for steps in ((1,), (2,), (4, 8, 12)):
        sums = add_from(sums, "zero", [zero_step(step) for step in steps])
    mine = (groups[None, :] == lax.axis_index("dp"))[..., None]
    info = jnp.where(mine, info[:, None, :], 0).astype(F32).reshape(1, 16 * 16 * 5)
    sums = jnp.concatenate([sums, jnp.pad(info, ((0, 0), (0, width - info.shape[1])))], axis=0)
    for row in (True, False):
        sums = add_from(sums, "dp", [dp_step(step, row) for step in (1, 2, 3)])
    info = sums[2, : 16 * 16 * 5].reshape(16, 80)
    info = lax.dynamic_index_in_dim(info, lax.axis_index("dp"), 0, False).astype(jnp.int32)
    frame_count = jnp.float32(BLOCKS * BLOCK * 256)
    mean = sums[0] / frame_count
    var = sums[1] / frame_count - mean * mean
    inverse = lax.rsqrt(var + EPS)
    norm = jnp.stack([mean, inverse, small_full[KER], small_full[KER + 1]])

    label = jnp.where(jnp.arange(NB * BLOCK) < end, seg, -1)
    padded = jnp.pad(label, (KER - 1 - LEFT, LEFT), constant_values=-1)
    meets = jnp.stack(
        [
            (padded[KER - 1 - k : KER - 1 - k + NB * BLOCK] == label) & (label >= 0)
            for k in range(KER)
        ]
    )
    x_sums = jnp.dot(meets.astype(BF16), x, preferred_element_type=F32)

    halves = cot.reshape(BLOCKS * BLOCK, 8, 2, share)
    cot_own = lax.dynamic_index_in_dim(halves, core, 2, False).reshape(-1, width // 2)
    cot_send = lax.dynamic_index_in_dim(halves, 1 - core, 2, False).reshape(-1, width // 2)
    swap = [(i, i ^ 1) for i in range(16)]
    cot_other = lax.ppermute(cot_send, "zero", swap)
    back = jnp.dot(cot, w_t, preferred_element_type=F32)

    h = hidden(info, got, kern_full, back, x_sums, cot_own, cot_other)
    a = (h - mean) * inverse * norm[2] + norm[3]
    sw = (a * jax.nn.sigmoid(a)).astype(BF16)
    sw_other = lax.ppermute(sw, "zero", swap)
    contract = (((0,), (0,)), ((), ()))
    term = lax.dot_general(sw, cot_own, contract, preferred_element_type=F32)
    term = term + lax.dot_general(sw_other, cot_other, contract, preferred_element_type=F32)
    term = term.astype(BF16).reshape(16, share, width // 2)
    term = lax.all_to_all(term, "dp", 0, 0, tiled=True)

    grads = terms(info, got, h, back, norm)
    out = lax.dot_general(
        sw, w_t, (((1,), (1,)), ((), ())), preferred_element_type=F32
    ).astype(BF16)

    grads = jnp.concatenate([grads, x_sums], axis=0).reshape(104, 8, 2, share)
    grads_other = lax.ppermute(
        lax.dynamic_index_in_dim(grads, 1 - core, 2, False), "zero", swap
    )
    grads = lax.dynamic_index_in_dim(grads, core, 2, False) + grads_other

    term = jnp.sum(term.astype(F32), axis=0).reshape(share, 8, share)
    both = jnp.transpose(jnp.concatenate([term, grads], axis=0), (1, 0, 2))
    both = lax.all_to_all(
        both,
        "zero",
        0,
        0,
        axis_index_groups=[[i for i in range(16) if i % 2 == c] for c in range(2)],
        tiled=True,
    )
    last = jnp.sum(both, axis=0)
    last = lax.all_to_all(
        jnp.broadcast_to(last[None], (16,) + last.shape), "dp", 0, 0, tiled=True
    )
    part_w = last[:, :share].reshape(width, share)
    grads = jnp.sum(last[:, share:], axis=0)

    own = lax.dynamic_slice_in_dim(norm, zero_id * share, share, 1)
    da_x, hat_x, x_k = grads[:KER], grads[KER : 2 * KER], grads[72 : 72 + KER]
    sum_x, sum_1 = grads[64], grads[65]
    part_k = (own[2] * own[1]) * (da_x - (sum_1 / frame_count) * x_k - (sum_x / frame_count) * hat_x)
    return out[None, None], part_w, part_k, jnp.stack([sum_x, sum_1])


def solution(mesh):
    return jax.shard_map(
        per_device,
        mesh=mesh,
        in_specs=(
            P("dp", "zero", None, None),
            P("dp", "zero", None),
            P("dp", "zero", None),
            P("dp", "zero", None, None),
            P(None, "zero"),
            P(None, "zero"),
            P(None, "zero"),
        ),
        out_specs=(P("dp", "zero", None, None), P(None, "zero"), P(None, "zero"), P(None, "zero")),
        check_vma=False,
    )
```

```python
import jax
import jax.numpy as jnp
from jax import lax
from jax.experimental import pallas as pl
from jax.experimental.pallas import tpu as pltpu
from jax.sharding import PartitionSpec as P

KER = 32
BLOCK = 64
BLOCKS = 8
NB = 12
LEFT = 16
WIN = 96
LANES = 128
EPS = 1e-05
F32 = jnp.float32
BF16 = jnp.bfloat16
SMEM_SPEC = pl.BlockSpec(memory_space=pltpu.SMEM)


def cost(microseconds):
    return pl.CostEstimate(
        flops=microseconds * 1_100_000_000, bytes_accessed=1_000_000, transcendentals=0
    )


def row_iota(rows):
    return lax.broadcasted_iota(jnp.int32, (rows, LANES), 0)


def spread_taps(kern_ref, taps):
    for k in range(KER):
        taps[pl.ds(8 * k, 8), :] = jnp.broadcast_to(kern_ref[pl.ds(k, 1), :], (8, LANES))


def row_of(v):
    return 8 * row_iota(8) + v


def shifted(window, w):
    return window[pl.ds(w, 8, stride=8), :]


def conv_block(window, taps):
    xs = [shifted(window, w) for w in range(7)]
    acc = [None] * 8
    for k in range(KER):
        xs.append(shifted(window, k + 7))
        tap = taps[pl.ds(8 * k, 8), :]
        for v in range(8):
            acc[v] = tap * xs[v] if k == 0 else acc[v] + tap * xs[v]
        xs.pop(0)
    return acc


def utterances(first, second, row):
    low = (first <= row).astype(jnp.int32) + (second <= row).astype(jnp.int32)
    top = row + BLOCK - 1
    high = (first <= top).astype(jnp.int32) + (second <= top).astype(jnp.int32)
    return low, high + 1


def pack_kernel(target_ref, x_ref, out_ref):
    for i in range(4):
        group = 4 * pl.program_id(0) + i
        b = jnp.int32(-1)
        for slot in range(NB):
            b = jnp.where(target_ref[slot] == group, slot, b)

        @pl.when(b >= 0)
        def _():
            before = pl.multiple_of(jnp.maximum(b * BLOCK - LEFT, 0), 16)
            start = pl.multiple_of(b * BLOCK, 16)
            after = pl.multiple_of(jnp.minimum((b + 1) * BLOCK, NB * BLOCK - 16), 16)
            out_ref[i, pl.ds(0, 16), :] = x_ref[pl.ds(before, 16), :]
            out_ref[i, pl.ds(16, 64), :] = x_ref[pl.ds(start, 64), :]
            out_ref[i, pl.ds(80, 16), :] = x_ref[pl.ds(after, 16), :]

        @pl.when(b < 0)
        def _():
            out_ref[i] = jnp.zeros_like(out_ref[i])


def pack(target_row, x):
    rows, width = x.shape
    return pl.pallas_call(
        pack_kernel,
        grid=(4,),
        out_shape=jax.ShapeDtypeStruct((16, WIN, width), BF16),
        in_specs=[SMEM_SPEC, pl.BlockSpec((rows, width), lambda r: (0, 0))],
        out_specs=pl.BlockSpec((4, WIN, width), lambda r: (r, 0, 0)),
        cost_estimate=cost(4),
        compiler_params=pltpu.CompilerParams(vmem_limit_bytes=32 * 1024 * 1024),
        name="pack",
    )(target_row, x)


def stats_kernel(bounds_ref, x_ref, kern_ref, _, out_ref, window, taps, sums):
    spread_taps(kern_ref, taps)
    sums[...] = jnp.zeros_like(sums)
    first, second, end = bounds_ref[1], bounds_ref[2], bounds_ref[3]

    def block(n, carry):
        row = n * BLOCK

        def part(u, inner):
            begin, stop = bounds_ref[u], bounds_ref[u + 1]
            before = jnp.maximum(row - LEFT, 0)
            after = jnp.minimum(row + BLOCK, NB * BLOCK - 16)
            for source, place, size in ((before, 0, 16), (row, 16, 64), (after, 80, 16)):
                rows = row_iota(size) + (row - LEFT + place)
                x = x_ref[pl.ds(pl.multiple_of(source, 16), size), :].astype(F32)
                window[pl.ds(place, size), :] = jnp.where((rows >= begin) & (rows < stop), x, 0.0)
            acc = conv_block(window, taps)
            total, square = sums[pl.ds(0, 8), :], sums[pl.ds(8, 8), :]
            for v in range(8):
                at = row_of(v) + row
                h = jnp.where((at >= begin) & (at < stop), acc[v], 0.0)
                total = total + h
                square = square + h * h
            sums[pl.ds(0, 8), :] = total
            sums[pl.ds(8, 8), :] = square
            return inner

        return lax.fori_loop(*utterances(first, second, row), part, carry)

    lax.fori_loop(0, end // BLOCK, block, 0)
    out_ref[pl.ds(0, 1), :] = jnp.sum(sums[pl.ds(0, 8), :], axis=0, keepdims=True)
    out_ref[pl.ds(1, 1), :] = jnp.sum(sums[pl.ds(8, 8), :], axis=0, keepdims=True)


def stats(bounds, x, kern, earlier):
    width = x.shape[1]
    return pl.pallas_call(
        stats_kernel,
        grid=(width // LANES,),
        out_shape=jax.ShapeDtypeStruct((2, width), F32),
        in_specs=[
            SMEM_SPEC,
            pl.BlockSpec((NB * BLOCK, LANES), lambda c: (0, c)),
            pl.BlockSpec((KER, LANES), lambda c: (0, c)),
            pl.BlockSpec(memory_space=pl.ANY),
        ],
        out_specs=pl.BlockSpec((2, LANES), lambda c: (0, c)),
        scratch_shapes=[
            pltpu.VMEM((WIN, LANES), F32),
            pltpu.VMEM((8 * KER, LANES), F32),
            pltpu.VMEM((16, LANES), F32),
        ],
        cost_estimate=cost(15),
        name="stats",
    )(bounds, x, kern, earlier)


def live_parts(info_ref, got_ref, window, per_part, per_block=None):
    def slot(s, n):
        valid = info_ref[5 * s] > 0

        @pl.when(valid)
        def _():
            def part(u, carry):
                begin, stop = info_ref[5 * s + 1 + u], info_ref[5 * s + 2 + u]
                rows = row_iota(WIN)
                source = got_ref[s].astype(F32)
                window[...] = jnp.where((rows >= begin) & (rows < stop), source, 0.0)
                per_part(pl.multiple_of(n * BLOCK, BLOCK), begin - LEFT, stop - LEFT)
                return carry

            lax.fori_loop(
                *utterances(info_ref[5 * s + 2], info_ref[5 * s + 3], LEFT), part, 0
            )
            if per_block is not None:
                per_block(pl.multiple_of(n * BLOCK, BLOCK))

        return n + valid.astype(jnp.int32)

    lax.fori_loop(0, 16, slot, 0)


def hidden_kernel(info_ref, got_ref, kern_ref, norm_ref, *rest):
    h_ref, sw_ref, window, taps = rest[-4:]
    spread_taps(kern_ref, taps)
    mean, inverse = norm_ref[pl.ds(0, 1), :], norm_ref[pl.ds(1, 1), :]
    scale, shift = norm_ref[pl.ds(2, 1), :], norm_ref[pl.ds(3, 1), :]

    def per_part(at, begin, stop):
        acc = conv_block(window, taps)
        for v in range(8):
            place = pl.ds(at + v, 8, stride=8)
            keep = (row_of(v) >= begin) & (row_of(v) < stop)
            h_ref[place, :] = jnp.where(keep, acc[v], h_ref[place, :])

    def per_block(at):
        a = (h_ref[pl.ds(at, BLOCK), :] - mean) * inverse * scale + shift
        sw_ref[pl.ds(at, BLOCK), :] = (a * jax.nn.sigmoid(a)).astype(BF16)

    live_parts(info_ref, got_ref, window, per_part, per_block)


def hidden(info, got, kern, norm, *earlier):
    width = got.shape[2]
    rows = BLOCKS * BLOCK
    return pl.pallas_call(
        hidden_kernel,
        grid=(width // LANES,),
        out_shape=(
            jax.ShapeDtypeStruct((rows, width), F32),
            jax.ShapeDtypeStruct((rows, width), BF16),
        ),
        in_specs=[
            SMEM_SPEC,
            pl.BlockSpec((16, WIN, LANES), lambda c: (0, 0, c)),
            pl.BlockSpec((KER, LANES), lambda c: (0, c)),
            pl.BlockSpec((4, LANES), lambda c: (0, c)),
        ]
        + [pl.BlockSpec(memory_space=pl.ANY)] * len(earlier),
        out_specs=(
            pl.BlockSpec((rows, LANES), lambda c: (0, c)),
            pl.BlockSpec((rows, LANES), lambda c: (0, c)),
        ),
        scratch_shapes=[pltpu.VMEM((WIN, LANES), F32), pltpu.VMEM((8 * KER, LANES), F32)],
        cost_estimate=cost(16),
        name="hidden",
    )(info, got, kern, norm, *earlier)


def terms_kernel(info_ref, got_ref, h_ref, back_ref, norm_ref, out_ref, window, acc_a, acc_x, sums):
    acc_a[...] = jnp.zeros_like(acc_a)
    acc_x[...] = jnp.zeros_like(acc_x)
    sums[...] = jnp.zeros_like(sums)
    mean, inverse = norm_ref[pl.ds(0, 1), :], norm_ref[pl.ds(1, 1), :]
    scale, shift = norm_ref[pl.ds(2, 1), :], norm_ref[pl.ds(3, 1), :]

    def per_part(at, begin, stop):
        das, hats = [], []
        sum_x, sum_1 = sums[pl.ds(0, 8), :], sums[pl.ds(8, 8), :]
        for v in range(8):
            place = pl.ds(at + v, 8, stride=8)
            keep = (row_of(v) >= begin) & (row_of(v) < stop)
            hat = (h_ref[place, :] - mean) * inverse
            a = hat * scale + shift
            sig = jax.nn.sigmoid(a)
            da = back_ref[place, :] * (sig * (1.0 + a * (1.0 - sig)))
            da = jnp.where(keep, da, 0.0)
            hat = jnp.where(keep, hat, 0.0)
            sum_x = sum_x + da * hat
            sum_1 = sum_1 + da
            das.append(da)
            hats.append(hat)
        sums[pl.ds(0, 8), :] = sum_x
        sums[pl.ds(8, 8), :] = sum_1
        xs = [shifted(window, w) for w in range(7)]
        for k in range(KER):
            xs.append(shifted(window, k + 7))
            place = pl.ds(8 * k, 8)
            for acc, rows in ((acc_a, das), (acc_x, hats)):
                terms_k = [rows[v] * xs[v] for v in range(8)]
                while len(terms_k) > 1:
                    terms_k = [p + q for p, q in zip(terms_k[::2], terms_k[1::2])]
                acc[place, :] += terms_k[0]
            xs.pop(0)

    live_parts(info_ref, got_ref, window, per_part)
    out_ref[pl.ds(0, 32), :] = jnp.sum(acc_a[...].reshape(KER, 8, LANES), axis=1)
    out_ref[pl.ds(32, 32), :] = jnp.sum(acc_x[...].reshape(KER, 8, LANES), axis=1)
    out_ref[pl.ds(64, 1), :] = jnp.sum(sums[pl.ds(0, 8), :], axis=0, keepdims=True)
    out_ref[pl.ds(65, 1), :] = jnp.sum(sums[pl.ds(8, 8), :], axis=0, keepdims=True)
    out_ref[pl.ds(66, 6), :] = jnp.zeros((6, LANES), F32)


def terms(info, got, h, back, norm):
    width = got.shape[2]
    return pl.pallas_call(
        terms_kernel,
        grid=(width // LANES,),
        out_shape=jax.ShapeDtypeStruct((72, width), F32),
        in_specs=[
            SMEM_SPEC,
            pl.BlockSpec((16, WIN, LANES), lambda c: (0, 0, c)),
            pl.BlockSpec((BLOCKS * BLOCK, LANES), lambda c: (0, c)),
            pl.BlockSpec((BLOCKS * BLOCK, LANES), lambda c: (0, c)),
            pl.BlockSpec((4, LANES), lambda c: (0, c)),
        ],
        out_specs=pl.BlockSpec((72, LANES), lambda c: (0, c)),
        scratch_shapes=[
            pltpu.VMEM((WIN, LANES), F32),
            pltpu.VMEM((8 * KER, LANES), F32),
            pltpu.VMEM((8 * KER, LANES), F32),
            pltpu.VMEM((16, LANES), F32),
        ],
        cost_estimate=cost(25),
        name="terms",
    )(info, got, h, back, norm)


def zero_step(step):
    if step < 4:
        return [(i, i ^ step) for i in range(16)]
    return [(i, (i + step) % 16) for i in range(16)]


def dp_step(step, row):
    if row:
        return [(i, 4 * (i // 4) + (i + step) % 4) for i in range(16)]
    return [(i, (i + 4 * step) % 16) for i in range(16)]


def add_from(x, axis, steps, *meanwhile):
    parts = [lax.ppermute(x, axis, step) for step in steps]
    parts, meanwhile = lax.optimization_barrier((parts, meanwhile))
    return sum(parts, x), meanwhile


def per_device(frames, segments, targets, cotangent, w_out, kernel, norm_params):
    x, seg, target_row, cot = frames[0, 0], segments[0, 0], targets[0, 0], cotangent[0, 0]
    width = x.shape[1]
    share = width // 16
    zero_id = lax.axis_index("zero")
    core = lax.rem(zero_id, 2)

    groups = jnp.arange(16, dtype=jnp.int32)
    hit = target_row[None, :] == groups[:, None]
    valid = jnp.any(hit, axis=1)
    block_of = jnp.sum(jnp.where(hit, jnp.arange(NB, dtype=jnp.int32)[None, :], 0), axis=1)
    end = BLOCK * jnp.sum((target_row >= 0).astype(jnp.int32))
    ends = [jnp.minimum(jnp.sum((seg < u).astype(jnp.int32)), end) for u in (1, 2)]
    bounds = jnp.stack([jnp.int32(0), ends[0], ends[1], end])
    base = BLOCK * block_of - LEFT
    info = jnp.clip(bounds[None, :] - base[:, None], 0, WIN)
    info = jnp.concatenate([valid.astype(jnp.int32)[:, None], info], axis=1)

    small = jnp.concatenate([kernel, norm_params, jnp.zeros((14, share), BF16)], axis=0)
    small_full = lax.all_to_all(
        jnp.broadcast_to(small[None], (16,) + small.shape), "zero", 0, 0, tiled=True
    )
    small_full = jnp.transpose(small_full, (1, 0, 2)).reshape(48, width).astype(F32)
    kern_full = small_full[:KER]
    send = pack(target_row, x)
    got = lax.all_to_all(send, "dp", 0, 0, tiled=True)

    w_t = lax.all_gather(w_out.T, "zero", axis=0, tiled=True)

    sums = stats(bounds, x, kern_full, send)
    for steps in ((1,), (2,), (4, 8, 12)):
        sums, _ = add_from(sums, "zero", [zero_step(step) for step in steps])
    mine = (groups[None, :] == lax.axis_index("dp"))[..., None]
    info = jnp.where(mine, info[:, None, :], 0).astype(F32).reshape(1, 16 * 16 * 5)
    sums = jnp.concatenate([sums, jnp.pad(info, ((0, 0), (0, width - info.shape[1])))], axis=0)
    back = jnp.dot(cot, w_t, preferred_element_type=F32)
    sums, _ = add_from(sums, "dp", [dp_step(step, True) for step in (1, 2, 3)])
    sums, (back,) = add_from(sums, "dp", [dp_step(step, False) for step in (1, 2, 3)], back)
    info = sums[2, : 16 * 16 * 5].reshape(16, 80)
    info = lax.dynamic_index_in_dim(info, lax.axis_index("dp"), 0, False).astype(jnp.int32)
    frame_count = jnp.float32(BLOCKS * BLOCK * 256)
    mean = sums[0] / frame_count
    var = sums[1] / frame_count - mean * mean
    inverse = lax.rsqrt(var + EPS)
    norm = jnp.stack([mean, inverse, small_full[KER], small_full[KER + 1]])

    frame = lax.broadcasted_iota(jnp.int32, (KER, NB * BLOCK), 1)
    centre = frame - lax.broadcasted_iota(jnp.int32, (KER, NB * BLOCK), 0) + LEFT
    meets = jnp.zeros((KER, NB * BLOCK), jnp.bool_)
    for u in range(3):
        begin, stop = bounds[u], bounds[u + 1]
        within = (jnp.minimum(frame, centre) >= begin) & (jnp.maximum(frame, centre) < stop)
        meets = meets | within
    x_sums = jnp.dot(meets.astype(BF16), x, preferred_element_type=F32)

    half = width // 2
    cot_own = lax.dynamic_slice_in_dim(cot, core * half, half, 1)
    cot_send = lax.dynamic_slice_in_dim(cot, (1 - core) * half, half, 1)
    swap = [(i, i ^ 1) for i in range(16)]
    cot_other = lax.ppermute(cot_send, "zero", swap)

    h, sw = hidden(info, got, kern_full, norm, back, x_sums)
    sw_other = lax.ppermute(sw, "zero", swap)
    contract = (((0,), (0,)), ((), ()))
    term = lax.dot_general(sw, cot_own, contract, preferred_element_type=F32)
    term = term + lax.dot_general(sw_other, cot_other, contract, preferred_element_type=F32)
    term = term.astype(BF16).reshape(16, share, half)
    term = lax.all_to_all(term, "dp", 0, 0, tiled=True)

    grads = terms(info, got, h, back, norm)
    out = lax.dot_general(
        sw, w_t, (((1,), (1,)), ((), ())), preferred_element_type=F32
    ).astype(BF16)

    grads = jnp.concatenate([grads, x_sums], axis=0)
    grads_other = lax.ppermute(
        lax.dynamic_slice_in_dim(grads, (1 - core) * half, half, 1), "zero", swap
    )
    grads = lax.dynamic_slice_in_dim(grads, core * half, half, 1) + grads_other

    term = jnp.sum(term.astype(F32), axis=0)
    both = jnp.concatenate([term, grads], axis=0).reshape(-1, 8, share)
    both = jnp.transpose(both, (1, 0, 2))
    both = lax.dynamic_slice_in_dim(jnp.concatenate([both, both], axis=0), zero_id // 2, 8, 0)
    last = jnp.zeros(both.shape[1:], F32)
    for i in range(8):
        to_owner = [(2 * z + c, 8 * c + (i + z) % 8) for z in range(8) for c in range(2)]
        last = last + lax.ppermute(both[i], "zero", to_owner)
    last = lax.all_to_all(
        jnp.broadcast_to(last[None], (16,) + last.shape), "dp", 0, 0, tiled=True
    )
    part_w = last[:, :share].reshape(width, share)
    grads = jnp.sum(last[:, share:], axis=0)

    own = lax.dynamic_slice_in_dim(norm, zero_id * share, share, 1)
    da_x, hat_x, x_k = grads[:KER], grads[KER : 2 * KER], grads[72 : 72 + KER]
    sum_x, sum_1 = grads[64], grads[65]
    part_k = (own[2] * own[1]) * (da_x - (sum_1 / frame_count) * x_k - (sum_x / frame_count) * hat_x)
    return out[None, None], part_w, part_k, jnp.stack([sum_x, sum_1])


def solution(mesh):
    return jax.shard_map(
        per_device,
        mesh=mesh,
        in_specs=(
            P("dp", "zero", None, None),
            P("dp", "zero", None),
            P("dp", "zero", None),
            P("dp", "zero", None, None),
            P(None, "zero"),
            P(None, "zero"),
            P(None, "zero"),
        ),
        out_specs=(P("dp", "zero", None, None), P(None, "zero"), P(None, "zero"), P(None, "zero")),
        check_vma=False,
    )
```

```python
import jax
import jax.numpy as jnp
from jax import lax
from jax.experimental import pallas as pl
from jax.experimental.pallas import tpu as pltpu
from jax.sharding import PartitionSpec as P

KER = 32
BLOCK = 64
BLOCKS = 8
NB = 12
LEFT = 16
WIN = 96
LANES = 128
EPS = 1e-05
F32 = jnp.float32
BF16 = jnp.bfloat16
SMEM_SPEC = pl.BlockSpec(memory_space=pltpu.SMEM)


def cost(microseconds):
    return pl.CostEstimate(
        flops=microseconds * 1_100_000_000, bytes_accessed=1_000_000, transcendentals=0
    )


def row_iota(rows):
    return lax.broadcasted_iota(jnp.int32, (rows, LANES), 0)


def spread_taps(kern_ref, taps):
    for k in range(KER):
        taps[pl.ds(8 * k, 8), :] = jnp.broadcast_to(kern_ref[pl.ds(k, 1), :], (8, LANES))


def row_of(v):
    return 8 * row_iota(8) + v


def shifted(window, w):
    return window[pl.ds(w, 8, stride=8), :]


def conv_block(window, taps):
    xs = [shifted(window, w) for w in range(7)]
    acc = [None] * 8
    for k in range(KER):
        xs.append(shifted(window, k + 7))
        tap = taps[pl.ds(8 * k, 8), :]
        for v in range(8):
            acc[v] = tap * xs[v] if k == 0 else acc[v] + tap * xs[v]
        xs.pop(0)
    return acc


def utterances(first, second, row):
    low = (first <= row).astype(jnp.int32) + (second <= row).astype(jnp.int32)
    top = row + BLOCK - 1
    high = (first <= top).astype(jnp.int32) + (second <= top).astype(jnp.int32)
    return low, high + 1


def places_kernel(target_ref, group_ref, segment_ref, bounds_ref, row_ref):
    live = jnp.int32(0)
    for slot in range(NB):
        live = live + (target_ref[slot] >= 0).astype(jnp.int32)
    segment = segment_ref[...]
    bounds = [jnp.int32(0)]
    for u in (1, 2):
        bounds.append(jnp.minimum(jnp.sum((segment < u).astype(jnp.int32)), BLOCK * live))
    bounds.append(BLOCK * live)
    for u in range(4):
        bounds_ref[u] = bounds[u]

    lane = lax.broadcasted_iota(jnp.int32, row_ref.shape, 1)
    group = sum((lane >= 96 * m).astype(jnp.int32) for m in range(1, 16))
    lane = lane - 96 * group
    source = sum((lane >= 5 * m).astype(jnp.int32) for m in range(1, 17))
    field = lane - 5 * source
    valid = jnp.zeros(row_ref.shape, jnp.int32)
    block = jnp.zeros(row_ref.shape, jnp.int32)
    for slot in range(NB):
        here = group == target_ref[slot]
        valid = jnp.where(here, 1, valid)
        block = jnp.where(here, slot, block)
    bound = jnp.zeros(row_ref.shape, jnp.int32)
    for u in range(4):
        bound = jnp.where(field == u + 1, bounds[u], bound)
    bound = jnp.clip(bound - (BLOCK * block - LEFT), 0, WIN)
    value = jnp.where(field == 0, valid, bound)
    row_ref[...] = jnp.where(source == group_ref[0], value, 0).astype(F32)


def places(target_row, group, segment, width):
    return pl.pallas_call(
        places_kernel,
        out_shape=(
            jax.ShapeDtypeStruct((4,), jnp.int32),
            jax.ShapeDtypeStruct((1, width), F32),
        ),
        in_specs=[SMEM_SPEC, SMEM_SPEC, pl.BlockSpec(memory_space=pltpu.VMEM)],
        out_specs=(SMEM_SPEC, pl.BlockSpec(memory_space=pltpu.VMEM)),
        cost_estimate=cost(1),
        name="places",
    )(target_row, group, segment)


def pack_kernel(target_ref, x_ref, out_ref):
    for i in range(4):
        group = 4 * pl.program_id(0) + i
        b = jnp.int32(-1)
        for slot in range(NB):
            b = jnp.where(target_ref[slot] == group, slot, b)

        @pl.when(b >= 0)
        def _():
            before = pl.multiple_of(jnp.maximum(b * BLOCK - LEFT, 0), 16)
            start = pl.multiple_of(b * BLOCK, 16)
            after = pl.multiple_of(jnp.minimum((b + 1) * BLOCK, NB * BLOCK - 16), 16)
            out_ref[i, pl.ds(0, 16), :] = x_ref[pl.ds(before, 16), :]
            out_ref[i, pl.ds(16, 64), :] = x_ref[pl.ds(start, 64), :]
            out_ref[i, pl.ds(80, 16), :] = x_ref[pl.ds(after, 16), :]

        @pl.when(b < 0)
        def _():
            out_ref[i] = jnp.zeros_like(out_ref[i])


def pack(target_row, x):
    rows, width = x.shape
    return pl.pallas_call(
        pack_kernel,
        grid=(4,),
        out_shape=jax.ShapeDtypeStruct((16, WIN, width), BF16),
        in_specs=[SMEM_SPEC, pl.BlockSpec((rows, width), lambda r: (0, 0))],
        out_specs=pl.BlockSpec((4, WIN, width), lambda r: (r, 0, 0)),
        cost_estimate=cost(4),
        compiler_params=pltpu.CompilerParams(vmem_limit_bytes=32 * 1024 * 1024),
        name="pack",
    )(target_row, x)


def stats_kernel(bounds_ref, x_ref, kern_ref, _, out_ref, window, taps, sums):
    spread_taps(kern_ref, taps)
    sums[...] = jnp.zeros_like(sums)
    first, second, end = bounds_ref[1], bounds_ref[2], bounds_ref[3]

    def block(n, carry):
        row = n * BLOCK

        def part(u, inner):
            begin, stop = bounds_ref[u], bounds_ref[u + 1]
            before = jnp.maximum(row - LEFT, 0)
            after = jnp.minimum(row + BLOCK, NB * BLOCK - 16)
            for source, place, size in ((before, 0, 16), (row, 16, 64), (after, 80, 16)):
                rows = row_iota(size) + (row - LEFT + place)
                x = x_ref[pl.ds(pl.multiple_of(source, 16), size), :].astype(F32)
                window[pl.ds(place, size), :] = jnp.where((rows >= begin) & (rows < stop), x, 0.0)
            acc = conv_block(window, taps)
            total, square = sums[pl.ds(0, 8), :], sums[pl.ds(8, 8), :]
            for v in range(8):
                at = row_of(v) + row
                h = jnp.where((at >= begin) & (at < stop), acc[v], 0.0)
                total = total + h
                square = square + h * h
            sums[pl.ds(0, 8), :] = total
            sums[pl.ds(8, 8), :] = square
            return inner

        return lax.fori_loop(*utterances(first, second, row), part, carry)

    lax.fori_loop(0, end // BLOCK, block, 0)
    out_ref[pl.ds(0, 1), :] = jnp.sum(sums[pl.ds(0, 8), :], axis=0, keepdims=True)
    out_ref[pl.ds(1, 1), :] = jnp.sum(sums[pl.ds(8, 8), :], axis=0, keepdims=True)


def stats(bounds, x, kern, earlier):
    width = x.shape[1]
    return pl.pallas_call(
        stats_kernel,
        grid=(width // LANES,),
        out_shape=jax.ShapeDtypeStruct((2, width), F32),
        in_specs=[
            SMEM_SPEC,
            pl.BlockSpec((NB * BLOCK, LANES), lambda c: (0, c)),
            pl.BlockSpec((KER, LANES), lambda c: (0, c)),
            pl.BlockSpec(memory_space=pl.ANY),
        ],
        out_specs=pl.BlockSpec((2, LANES), lambda c: (0, c)),
        scratch_shapes=[
            pltpu.VMEM((WIN, LANES), F32),
            pltpu.VMEM((8 * KER, LANES), F32),
            pltpu.VMEM((16, LANES), F32),
        ],
        cost_estimate=cost(15),
        name="stats",
    )(bounds, x, kern, earlier)


def live_parts(info_ref, got_ref, window, per_part, per_block=None):
    def slot(s, n):
        valid = info_ref[5 * s] > 0

        @pl.when(valid)
        def _():
            def part(u, carry):
                begin, stop = info_ref[5 * s + 1 + u], info_ref[5 * s + 2 + u]
                rows = row_iota(WIN)
                source = got_ref[s].astype(F32)
                window[...] = jnp.where((rows >= begin) & (rows < stop), source, 0.0)
                per_part(pl.multiple_of(n * BLOCK, BLOCK), begin - LEFT, stop - LEFT)
                return carry

            lax.fori_loop(
                *utterances(info_ref[5 * s + 2], info_ref[5 * s + 3], LEFT), part, 0
            )
            if per_block is not None:
                per_block(pl.multiple_of(n * BLOCK, BLOCK))

        return n + valid.astype(jnp.int32)

    lax.fori_loop(0, 16, slot, 0)


def hidden_kernel(info_ref, got_ref, kern_ref, norm_ref, *rest):
    h_ref, sw_ref, window, taps = rest[-4:]
    spread_taps(kern_ref, taps)
    mean, inverse = norm_ref[pl.ds(0, 1), :], norm_ref[pl.ds(1, 1), :]
    scale, shift = norm_ref[pl.ds(2, 1), :], norm_ref[pl.ds(3, 1), :]

    def per_part(at, begin, stop):
        acc = conv_block(window, taps)
        for v in range(8):
            place = pl.ds(at + v, 8, stride=8)
            keep = (row_of(v) >= begin) & (row_of(v) < stop)
            h_ref[place, :] = jnp.where(keep, acc[v], h_ref[place, :])

    def per_block(at):
        a = (h_ref[pl.ds(at, BLOCK), :] - mean) * inverse * scale + shift
        sw_ref[pl.ds(at, BLOCK), :] = (a * jax.nn.sigmoid(a)).astype(BF16)

    live_parts(info_ref, got_ref, window, per_part, per_block)


def hidden(info, got, kern, norm, *earlier):
    width = got.shape[2]
    rows = BLOCKS * BLOCK
    return pl.pallas_call(
        hidden_kernel,
        grid=(width // LANES,),
        out_shape=(
            jax.ShapeDtypeStruct((rows, width), F32),
            jax.ShapeDtypeStruct((rows, width), BF16),
        ),
        in_specs=[
            SMEM_SPEC,
            pl.BlockSpec((16, WIN, LANES), lambda c: (0, 0, c)),
            pl.BlockSpec((KER, LANES), lambda c: (0, c)),
            pl.BlockSpec((4, LANES), lambda c: (0, c)),
        ]
        + [pl.BlockSpec(memory_space=pl.ANY)] * len(earlier),
        out_specs=(
            pl.BlockSpec((rows, LANES), lambda c: (0, c)),
            pl.BlockSpec((rows, LANES), lambda c: (0, c)),
        ),
        scratch_shapes=[pltpu.VMEM((WIN, LANES), F32), pltpu.VMEM((8 * KER, LANES), F32)],
        cost_estimate=cost(16),
        name="hidden",
    )(info, got, kern, norm, *earlier)


def terms_kernel(info_ref, got_ref, h_ref, back_ref, norm_ref, out_ref, window, acc_a, acc_x, sums):
    acc_a[...] = jnp.zeros_like(acc_a)
    acc_x[...] = jnp.zeros_like(acc_x)
    sums[...] = jnp.zeros_like(sums)
    mean, inverse = norm_ref[pl.ds(0, 1), :], norm_ref[pl.ds(1, 1), :]
    scale, shift = norm_ref[pl.ds(2, 1), :], norm_ref[pl.ds(3, 1), :]

    def per_part(at, begin, stop):
        das, hats = [], []
        sum_x, sum_1 = sums[pl.ds(0, 8), :], sums[pl.ds(8, 8), :]
        for v in range(8):
            place = pl.ds(at + v, 8, stride=8)
            keep = (row_of(v) >= begin) & (row_of(v) < stop)
            hat = (h_ref[place, :] - mean) * inverse
            a = hat * scale + shift
            sig = jax.nn.sigmoid(a)
            da = back_ref[place, :] * (sig * (1.0 + a * (1.0 - sig)))
            da = jnp.where(keep, da, 0.0)
            hat = jnp.where(keep, hat, 0.0)
            sum_x = sum_x + da * hat
            sum_1 = sum_1 + da
            das.append(da)
            hats.append(hat)
        sums[pl.ds(0, 8), :] = sum_x
        sums[pl.ds(8, 8), :] = sum_1
        xs = [shifted(window, w) for w in range(7)]
        for k in range(KER):
            xs.append(shifted(window, k + 7))
            place = pl.ds(8 * k, 8)
            for acc, rows in ((acc_a, das), (acc_x, hats)):
                terms_k = [rows[v] * xs[v] for v in range(8)]
                while len(terms_k) > 1:
                    terms_k = [p + q for p, q in zip(terms_k[::2], terms_k[1::2])]
                acc[place, :] += terms_k[0]
            xs.pop(0)

    live_parts(info_ref, got_ref, window, per_part)
    out_ref[pl.ds(0, 32), :] = jnp.sum(acc_a[...].reshape(KER, 8, LANES), axis=1)
    out_ref[pl.ds(32, 32), :] = jnp.sum(acc_x[...].reshape(KER, 8, LANES), axis=1)
    out_ref[pl.ds(64, 1), :] = jnp.sum(sums[pl.ds(0, 8), :], axis=0, keepdims=True)
    out_ref[pl.ds(65, 1), :] = jnp.sum(sums[pl.ds(8, 8), :], axis=0, keepdims=True)
    out_ref[pl.ds(66, 6), :] = jnp.zeros((6, LANES), F32)


def terms(info, got, h, back, norm):
    width = got.shape[2]
    return pl.pallas_call(
        terms_kernel,
        grid=(width // LANES,),
        out_shape=jax.ShapeDtypeStruct((72, width), F32),
        in_specs=[
            SMEM_SPEC,
            pl.BlockSpec((16, WIN, LANES), lambda c: (0, 0, c)),
            pl.BlockSpec((BLOCKS * BLOCK, LANES), lambda c: (0, c)),
            pl.BlockSpec((BLOCKS * BLOCK, LANES), lambda c: (0, c)),
            pl.BlockSpec((4, LANES), lambda c: (0, c)),
        ],
        out_specs=pl.BlockSpec((72, LANES), lambda c: (0, c)),
        scratch_shapes=[
            pltpu.VMEM((WIN, LANES), F32),
            pltpu.VMEM((8 * KER, LANES), F32),
            pltpu.VMEM((8 * KER, LANES), F32),
            pltpu.VMEM((16, LANES), F32),
        ],
        cost_estimate=cost(25),
        name="terms",
    )(info, got, h, back, norm)


def zero_step(step):
    if step < 4:
        return [(i, i ^ step) for i in range(16)]
    return [(i, (i + step) % 16) for i in range(16)]


def dp_step(step, row):
    if row:
        return [(i, 4 * (i // 4) + (i + step) % 4) for i in range(16)]
    return [(i, (i + 4 * step) % 16) for i in range(16)]


def add_from(x, axis, steps, *meanwhile):
    parts = [lax.ppermute(x, axis, step) for step in steps]
    parts, meanwhile = lax.optimization_barrier((parts, meanwhile))
    return sum(parts, x), meanwhile


def per_device(frames, segments, targets, cotangent, w_out, kernel, norm_params):
    x, seg, target_row, cot = frames[0, 0], segments[0, 0], targets[0, 0], cotangent[0, 0]
    width = x.shape[1]
    share = width // 16
    zero_id = lax.axis_index("zero")
    core = lax.rem(zero_id, 2)

    bounds, info = places(
        target_row, lax.axis_index("dp").reshape(1), seg.reshape(NB // 2, 2 * BLOCK), width
    )
    send = pack(target_row, x)
    small = jnp.concatenate([kernel, norm_params, jnp.zeros((14, share), BF16)], axis=0)
    send, small = lax.optimization_barrier((send, small))
    got = lax.all_to_all(send, "dp", 0, 0, tiled=True)
    small_full = lax.all_gather(small, "zero", axis=0)
    small_full = jnp.transpose(small_full, (1, 0, 2)).reshape(48, width).astype(F32)
    kern_full = small_full[:KER]

    w_t = lax.all_gather(w_out.T, "zero", axis=0, tiled=True)

    frame = lax.broadcasted_iota(jnp.int32, (KER, NB * BLOCK), 1)
    centre = frame - lax.broadcasted_iota(jnp.int32, (KER, NB * BLOCK), 0) + LEFT
    meets = jnp.zeros((KER, NB * BLOCK), jnp.bool_)
    for u in range(3):
        begin, stop = bounds[u], bounds[u + 1]
        within = (jnp.minimum(frame, centre) >= begin) & (jnp.maximum(frame, centre) < stop)
        meets = meets | within

    half = width // 2
    column = lax.broadcasted_iota(jnp.int32, (width, half), 0)
    place = lax.broadcasted_iota(jnp.int32, (width, half), 1)
    even = column == place + share * (place // share)
    odd = column == place + share * (place // share) + share
    own_columns = jnp.where(core == 0, even, odd).astype(BF16)
    other_columns = jnp.where(core == 0, odd, even).astype(BF16)
    swap = [(i, i ^ 1) for i in range(16)]

    sums = stats(bounds, x, kern_full, send)
    for steps in ((1,), (2,), (4, 8, 12)):
        sums, _ = add_from(sums, "zero", [zero_step(step) for step in steps])
    sums = jnp.concatenate([sums, info], axis=0)
    sums, cot, x = lax.optimization_barrier((sums, cot, x))
    x_sums = jnp.dot(meets.astype(BF16), x, preferred_element_type=F32)
    cot_own = jnp.dot(cot, own_columns, preferred_element_type=F32).astype(BF16)
    cot_send = jnp.dot(cot, other_columns, preferred_element_type=F32).astype(BF16)
    back = jnp.dot(cot, w_t, preferred_element_type=F32)
    sums, (x_sums, cot_own, cot_send) = add_from(
        sums, "dp", [dp_step(step, True) for step in (1, 2, 3)], x_sums, cot_own, cot_send
    )
    cot_other = lax.ppermute(cot_send, "zero", swap)
    sums, (back,) = add_from(sums, "dp", [dp_step(step, False) for step in (1, 2, 3)], back)
    info = lax.dynamic_slice_in_dim(sums[2], lax.axis_index("dp") * 96, 80, 0).astype(jnp.int32)
    frame_count = jnp.float32(BLOCKS * BLOCK * 256)
    mean = sums[0] / frame_count
    var = sums[1] / frame_count - mean * mean
    inverse = lax.rsqrt(var + EPS)
    norm = jnp.stack([mean, inverse, small_full[KER], small_full[KER + 1]])

    h, sw = hidden(info, got, kern_full, norm, back, x_sums)
    sw_other = lax.ppermute(sw, "zero", swap)
    contract = (((0,), (0,)), ((), ()))
    term = lax.dot_general(sw, cot_own, contract, preferred_element_type=F32)
    term = term + lax.dot_general(sw_other, cot_other, contract, preferred_element_type=F32)
    term = term.astype(BF16).reshape(16, share, half)
    term = lax.all_to_all(term, "dp", 0, 0, tiled=True)

    grads = terms(info, got, h, back, norm)
    out = lax.dot_general(
        sw, w_t, (((1,), (1,)), ((), ())), preferred_element_type=F32
    ).astype(BF16)

    grads = jnp.concatenate([grads, x_sums], axis=0).reshape(104, 8, 2, share)
    grads = jnp.transpose(grads, (2, 1, 0, 3))
    grads_other = lax.ppermute(
        lax.dynamic_index_in_dim(grads, 1 - core, 0, False), "zero", swap
    )
    grads = lax.dynamic_index_in_dim(grads, core, 0, False) + grads_other

    term = jnp.sum(term.astype(F32), axis=0).reshape(share, 8, share)
    both = jnp.concatenate([jnp.transpose(term, (1, 0, 2)), grads], axis=1)
    both = lax.all_to_all(
        both,
        "zero",
        0,
        0,
        axis_index_groups=[[i for i in range(16) if i % 2 == c] for c in range(2)],
        tiled=True,
    )
    last = jnp.sum(both, axis=0)
    last = lax.all_to_all(
        jnp.broadcast_to(last[None], (16,) + last.shape), "dp", 0, 0, tiled=True
    )
    part_w = last[:, :share].reshape(width, share)
    grads = jnp.sum(last[:, share:], axis=0)

    own = lax.dynamic_slice_in_dim(norm, zero_id * share, share, 1)
    da_x, hat_x, x_k = grads[:KER], grads[KER : 2 * KER], grads[72 : 72 + KER]
    sum_x, sum_1 = grads[64], grads[65]
    part_k = (own[2] * own[1]) * (da_x - (sum_1 / frame_count) * x_k - (sum_x / frame_count) * hat_x)
    return out[None, None], part_w, part_k, jnp.stack([sum_x, sum_1])


def solution(mesh):
    return jax.shard_map(
        per_device,
        mesh=mesh,
        in_specs=(
            P("dp", "zero", None, None),
            P("dp", "zero", None),
            P("dp", "zero", None),
            P("dp", "zero", None, None),
            P(None, "zero"),
            P(None, "zero"),
            P(None, "zero"),
        ),
        out_specs=(P("dp", "zero", None, None), P(None, "zero"), P(None, "zero"), P(None, "zero")),
        check_vma=False,
    )
```

```python
import jax
import jax.numpy as jnp
from jax import lax
from jax.experimental import pallas as pl
from jax.experimental.pallas import tpu as pltpu
from jax.sharding import PartitionSpec as P

KER = 32
BLOCK = 64
BLOCKS = 8
NB = 12
LEFT = 16
WIN = 96
LANES = 128
TILES = 4
WIDE = TILES * LANES
EPS = 1e-05
F32 = jnp.float32
BF16 = jnp.bfloat16
SMEM_SPEC = pl.BlockSpec(memory_space=pltpu.SMEM)


def cost(microseconds):
    return pl.CostEstimate(
        flops=microseconds * 1_100_000_000, bytes_accessed=1_000_000, transcendentals=0
    )


def row_iota(rows):
    return lax.broadcasted_iota(jnp.int32, (rows, LANES), 0)


def tile(g):
    return pl.ds(LANES * g, LANES)


def spread_taps(kern_ref, taps):
    for g in range(TILES):
        for k in range(KER):
            row = kern_ref[pl.ds(k, 1), tile(g)]
            taps[g, pl.ds(8 * k, 8), :] = jnp.broadcast_to(row, (8, LANES))


def row_of(v):
    return 8 * row_iota(8) + v


def shifted(window, g, w):
    return window[g, pl.ds(w, 8, stride=8), :]


def conv_block(window, taps, g):
    xs = [shifted(window, g, w) for w in range(7)]
    acc = [None] * 8
    for k in range(KER):
        xs.append(shifted(window, g, k + 7))
        tap = taps[g, pl.ds(8 * k, 8), :]
        for v in range(8):
            acc[v] = tap * xs[v] if k == 0 else acc[v] + tap * xs[v]
        xs.pop(0)
    return acc


def utterances(first, second, row):
    low = (first <= row).astype(jnp.int32) + (second <= row).astype(jnp.int32)
    top = row + BLOCK - 1
    high = (first <= top).astype(jnp.int32) + (second <= top).astype(jnp.int32)
    return low, high + 1


def places_kernel(target_ref, group_ref, segment_ref, bounds_ref, row_ref):
    live = jnp.int32(0)
    for slot in range(NB):
        live = live + (target_ref[slot] >= 0).astype(jnp.int32)
    segment = segment_ref[...]
    bounds = [jnp.int32(0)]
    for u in (1, 2):
        bounds.append(jnp.minimum(jnp.sum((segment < u).astype(jnp.int32)), BLOCK * live))
    bounds.append(BLOCK * live)
    for u in range(4):
        bounds_ref[u] = bounds[u]

    lane = lax.broadcasted_iota(jnp.int32, row_ref.shape, 1)
    group = sum((lane >= 96 * m).astype(jnp.int32) for m in range(1, 16))
    lane = lane - 96 * group
    source = sum((lane >= 5 * m).astype(jnp.int32) for m in range(1, 17))
    field = lane - 5 * source
    valid = jnp.zeros(row_ref.shape, jnp.int32)
    block = jnp.zeros(row_ref.shape, jnp.int32)
    for slot in range(NB):
        here = group == target_ref[slot]
        valid = jnp.where(here, 1, valid)
        block = jnp.where(here, slot, block)
    bound = jnp.zeros(row_ref.shape, jnp.int32)
    for u in range(4):
        bound = jnp.where(field == u + 1, bounds[u], bound)
    bound = jnp.clip(bound - (BLOCK * block - LEFT), 0, WIN)
    value = jnp.where(field == 0, valid, bound)
    row_ref[...] = jnp.where(source == group_ref[0], value, 0).astype(F32)


def places(target_row, group, segment, width):
    return pl.pallas_call(
        places_kernel,
        out_shape=(
            jax.ShapeDtypeStruct((4,), jnp.int32),
            jax.ShapeDtypeStruct((1, width), F32),
        ),
        in_specs=[SMEM_SPEC, SMEM_SPEC, pl.BlockSpec(memory_space=pltpu.VMEM)],
        out_specs=(SMEM_SPEC, pl.BlockSpec(memory_space=pltpu.VMEM)),
        cost_estimate=cost(1),
        name="places",
    )(target_row, group, segment)


def pack_kernel(target_ref, x_ref, out_ref):
    for i in range(4):
        group = 4 * pl.program_id(0) + i
        b = jnp.int32(-1)
        for slot in range(NB):
            b = jnp.where(target_ref[slot] == group, slot, b)

        @pl.when(b >= 0)
        def _():
            before = pl.multiple_of(jnp.maximum(b * BLOCK - LEFT, 0), 16)
            start = pl.multiple_of(b * BLOCK, 16)
            after = pl.multiple_of(jnp.minimum((b + 1) * BLOCK, NB * BLOCK - 16), 16)
            out_ref[i, pl.ds(0, 16), :] = x_ref[pl.ds(before, 16), :]
            out_ref[i, pl.ds(16, 64), :] = x_ref[pl.ds(start, 64), :]
            out_ref[i, pl.ds(80, 16), :] = x_ref[pl.ds(after, 16), :]

        @pl.when(b < 0)
        def _():
            out_ref[i] = jnp.zeros_like(out_ref[i])


def pack(target_row, x):
    rows, width = x.shape
    return pl.pallas_call(
        pack_kernel,
        grid=(4,),
        out_shape=jax.ShapeDtypeStruct((16, WIN, width), BF16),
        in_specs=[SMEM_SPEC, pl.BlockSpec((rows, width), lambda r: (0, 0))],
        out_specs=pl.BlockSpec((4, WIN, width), lambda r: (r, 0, 0)),
        cost_estimate=cost(4),
        compiler_params=pltpu.CompilerParams(vmem_limit_bytes=32 * 1024 * 1024),
        name="pack",
    )(target_row, x)


def stats_kernel(bounds_ref, x_ref, kern_ref, _, out_ref, window, taps, sums):
    spread_taps(kern_ref, taps)
    sums[...] = jnp.zeros_like(sums)
    first, second, end = bounds_ref[1], bounds_ref[2], bounds_ref[3]

    def block(n, carry):
        row = n * BLOCK

        def part(u, inner):
            begin, stop = bounds_ref[u], bounds_ref[u + 1]
            before = jnp.maximum(row - LEFT, 0)
            after = jnp.minimum(row + BLOCK, NB * BLOCK - 16)
            for source, place, size in ((before, 0, 16), (row, 16, 64), (after, 80, 16)):
                rows = row_iota(size) + (row - LEFT + place)
                keep = (rows >= begin) & (rows < stop)
                for g in range(TILES):
                    x = x_ref[pl.ds(pl.multiple_of(source, 16), size), tile(g)].astype(F32)
                    window[g, pl.ds(place, size), :] = jnp.where(keep, x, 0.0)
            for g in range(TILES):
                acc = conv_block(window, taps, g)
                total, square = sums[g, pl.ds(0, 8), :], sums[g, pl.ds(8, 8), :]
                for v in range(8):
                    at = row_of(v) + row
                    h = jnp.where((at >= begin) & (at < stop), acc[v], 0.0)
                    total = total + h
                    square = square + h * h
                sums[g, pl.ds(0, 8), :] = total
                sums[g, pl.ds(8, 8), :] = square
            return inner

        return lax.fori_loop(*utterances(first, second, row), part, carry)

    lax.fori_loop(0, end // BLOCK, block, 0)
    for g in range(TILES):
        for i in range(2):
            part = sums[g, pl.ds(8 * i, 8), :]
            out_ref[pl.ds(i, 1), tile(g)] = jnp.sum(part, axis=0, keepdims=True)


def stats(bounds, x, kern, earlier):
    width = x.shape[1]
    return pl.pallas_call(
        stats_kernel,
        grid=(width // WIDE,),
        out_shape=jax.ShapeDtypeStruct((2, width), F32),
        in_specs=[
            SMEM_SPEC,
            pl.BlockSpec((NB * BLOCK, WIDE), lambda c: (0, c)),
            pl.BlockSpec((KER, WIDE), lambda c: (0, c)),
            pl.BlockSpec(memory_space=pl.ANY),
        ],
        out_specs=pl.BlockSpec((2, WIDE), lambda c: (0, c)),
        scratch_shapes=[
            pltpu.VMEM((TILES, WIN, LANES), F32),
            pltpu.VMEM((TILES, 8 * KER, LANES), F32),
            pltpu.VMEM((TILES, 16, LANES), F32),
        ],
        cost_estimate=cost(15),
        name="stats",
    )(bounds, x, kern, earlier)


def live_parts(info_ref, got_ref, window, per_part, per_block=None):
    def slot(s, n):
        valid = info_ref[5 * s] > 0

        @pl.when(valid)
        def _():
            def part(u, carry):
                begin, stop = info_ref[5 * s + 1 + u], info_ref[5 * s + 2 + u]
                rows = row_iota(WIN)
                keep = (rows >= begin) & (rows < stop)
                for g in range(TILES):
                    x = got_ref[s, :, tile(g)].astype(F32)
                    window[g] = jnp.where(keep, x, 0.0)
                per_part(pl.multiple_of(n * BLOCK, BLOCK), begin - LEFT, stop - LEFT)
                return carry

            lax.fori_loop(
                *utterances(info_ref[5 * s + 2], info_ref[5 * s + 3], LEFT), part, 0
            )
            if per_block is not None:
                per_block(pl.multiple_of(n * BLOCK, BLOCK))

        return n + valid.astype(jnp.int32)

    lax.fori_loop(0, 16, slot, 0)


def hidden_kernel(info_ref, got_ref, kern_ref, norm_ref, *rest):
    h_ref, sw_ref, window, taps = rest[-4:]
    spread_taps(kern_ref, taps)

    def per_part(at, begin, stop):
        for g in range(TILES):
            acc = conv_block(window, taps, g)
            for v in range(8):
                place = pl.ds(at + v, 8, stride=8)
                keep = (row_of(v) >= begin) & (row_of(v) < stop)
                h_ref[g, place, :] = jnp.where(keep, acc[v], h_ref[g, place, :])

    def per_block(at):
        for g in range(TILES):
            mean, inverse = norm_ref[pl.ds(0, 1), tile(g)], norm_ref[pl.ds(1, 1), tile(g)]
            scale, shift = norm_ref[pl.ds(2, 1), tile(g)], norm_ref[pl.ds(3, 1), tile(g)]
            a = (h_ref[g, pl.ds(at, BLOCK), :] - mean) * inverse * scale + shift
            sw_ref[pl.ds(at, BLOCK), tile(g)] = (a * jax.nn.sigmoid(a)).astype(BF16)

    live_parts(info_ref, got_ref, window, per_part, per_block)


def hidden(info, got, kern, norm, *earlier):
    width = got.shape[2]
    rows = BLOCKS * BLOCK
    return pl.pallas_call(
        hidden_kernel,
        grid=(width // WIDE,),
        out_shape=(
            jax.ShapeDtypeStruct((width // LANES, rows, LANES), F32),
            jax.ShapeDtypeStruct((rows, width), BF16),
        ),
        in_specs=[
            SMEM_SPEC,
            pl.BlockSpec((16, WIN, WIDE), lambda c: (0, 0, c)),
            pl.BlockSpec((KER, WIDE), lambda c: (0, c)),
            pl.BlockSpec((4, WIDE), lambda c: (0, c)),
        ]
        + [pl.BlockSpec(memory_space=pl.ANY)] * len(earlier),
        out_specs=(
            pl.BlockSpec((TILES, rows, LANES), lambda c: (c, 0, 0)),
            pl.BlockSpec((rows, WIDE), lambda c: (0, c)),
        ),
        scratch_shapes=[pltpu.VMEM((TILES, WIN, LANES), F32), pltpu.VMEM((TILES, 8 * KER, LANES), F32)],
        cost_estimate=cost(16),
        name="hidden",
    )(info, got, kern, norm, *earlier)


def terms_kernel(
    info_ref, got_ref, h_ref, wide_ref, norm_ref, out_ref, window, back_ref, acc_a, acc_x, sums
):
    for g in range(TILES):
        back_ref[g] = wide_ref[:, tile(g)]
    acc_a[...] = jnp.zeros_like(acc_a)
    acc_x[...] = jnp.zeros_like(acc_x)
    sums[...] = jnp.zeros_like(sums)

    def per_tile(g, at, begin, stop):
        mean, inverse = norm_ref[pl.ds(0, 1), tile(g)], norm_ref[pl.ds(1, 1), tile(g)]
        scale, shift = norm_ref[pl.ds(2, 1), tile(g)], norm_ref[pl.ds(3, 1), tile(g)]
        das, hats = [], []
        sum_x, sum_1 = sums[g, pl.ds(0, 8), :], sums[g, pl.ds(8, 8), :]
        for v in range(8):
            place = pl.ds(at + v, 8, stride=8)
            keep = (row_of(v) >= begin) & (row_of(v) < stop)
            hat = (h_ref[g, place, :] - mean) * inverse
            a = hat * scale + shift
            sig = jax.nn.sigmoid(a)
            da = back_ref[g, place, :] * (sig * (1.0 + a * (1.0 - sig)))
            da = jnp.where(keep, da, 0.0)
            hat = jnp.where(keep, hat, 0.0)
            sum_x = sum_x + da * hat
            sum_1 = sum_1 + da
            das.append(da)
            hats.append(hat)
        sums[g, pl.ds(0, 8), :] = sum_x
        sums[g, pl.ds(8, 8), :] = sum_1
        xs = [shifted(window, g, w) for w in range(7)]
        for k in range(KER):
            xs.append(shifted(window, g, k + 7))
            place = pl.ds(8 * k, 8)
            for acc, rows in ((acc_a, das), (acc_x, hats)):
                terms_k = [rows[v] * xs[v] for v in range(8)]
                while len(terms_k) > 1:
                    terms_k = [p + q for p, q in zip(terms_k[::2], terms_k[1::2])]
                acc[g, place, :] += terms_k[0]
            xs.pop(0)

    def per_part(at, begin, stop):
        for g in range(TILES):
            per_tile(g, at, begin, stop)

    live_parts(info_ref, got_ref, window, per_part)
    for g in range(TILES):
        for acc, first in ((acc_a, 0), (acc_x, KER)):
            rows = acc[g].reshape(KER, 8, LANES)
            out_ref[pl.ds(first, KER), tile(g)] = jnp.sum(rows, axis=1)
        for i in range(2):
            part = sums[g, pl.ds(8 * i, 8), :]
            out_ref[pl.ds(2 * KER + i, 1), tile(g)] = jnp.sum(part, axis=0, keepdims=True)
    out_ref[pl.ds(66, 6), :] = jnp.zeros((6, WIDE), F32)


def terms(info, got, h, back, norm):
    width = got.shape[2]
    return pl.pallas_call(
        terms_kernel,
        grid=(width // WIDE,),
        out_shape=jax.ShapeDtypeStruct((72, width), F32),
        in_specs=[
            SMEM_SPEC,
            pl.BlockSpec((16, WIN, WIDE), lambda c: (0, 0, c)),
            pl.BlockSpec((TILES, BLOCKS * BLOCK, LANES), lambda c: (c, 0, 0)),
            pl.BlockSpec((BLOCKS * BLOCK, WIDE), lambda c: (0, c)),
            pl.BlockSpec((4, WIDE), lambda c: (0, c)),
        ],
        out_specs=pl.BlockSpec((72, WIDE), lambda c: (0, c)),
        scratch_shapes=[
            pltpu.VMEM((TILES, WIN, LANES), F32),
            pltpu.VMEM((TILES, BLOCKS * BLOCK, LANES), F32),
            pltpu.VMEM((TILES, 8 * KER, LANES), F32),
            pltpu.VMEM((TILES, 8 * KER, LANES), F32),
            pltpu.VMEM((TILES, 16, LANES), F32),
        ],
        cost_estimate=cost(25),
        name="terms",
    )(info, got, h, back, norm)


def zero_step(step):
    if step < 4:
        return [(i, i ^ step) for i in range(16)]
    return [(i, (i + step) % 16) for i in range(16)]


def dp_step(step, row):
    if row:
        return [(i, 4 * (i // 4) + (i + step) % 4) for i in range(16)]
    return [(i, (i + 4 * step) % 16) for i in range(16)]


def add_from(x, axis, steps, *meanwhile):
    parts = [lax.ppermute(x, axis, step) for step in steps]
    parts, meanwhile = lax.optimization_barrier((parts, meanwhile))
    return sum(parts, x), meanwhile


def gather_small(x, zero_id, meanwhile):
    for step, first in ((1, zero_id % 2 == 0), (2, (zero_id // 2) % 2 == 0)):
        other = lax.ppermute(x, "zero", zero_step(step))
        other, meanwhile = lax.optimization_barrier((other, meanwhile))
        x = jnp.stack([jnp.where(first, x, other), jnp.where(first, other, x)])
    pairs = [x] + [lax.ppermute(x, "zero", zero_step(step)) for step in (4, 8, 12)]
    place = zero_id // 4
    parts = []
    for q in range(4):
        part = pairs[0]
        for s in range(1, 4):
            part = jnp.where((place - s) % 4 == q, pairs[s], part)
        parts.append(part)
    return jnp.stack(parts).reshape((16,) + x.shape[2:])


def per_device(frames, segments, targets, cotangent, w_out, kernel, norm_params):
    x, seg, target_row, cot = frames[0, 0], segments[0, 0], targets[0, 0], cotangent[0, 0]
    width = x.shape[1]
    share = width // 16
    zero_id = lax.axis_index("zero")
    core = lax.rem(zero_id, 2)

    bounds, info = places(
        target_row, lax.axis_index("dp").reshape(1), seg.reshape(NB // 2, 2 * BLOCK), width
    )
    send = pack(target_row, x)
    small = jnp.concatenate([kernel, norm_params, jnp.zeros((14, share), BF16)], axis=0)
    got = lax.all_to_all(send, "dp", 0, 0, tiled=True)
    small_full = gather_small(small, zero_id, send)
    small_full = jnp.transpose(small_full, (1, 0, 2)).reshape(48, width).astype(F32)
    kern_full = small_full[:KER]

    w_t = lax.all_gather(w_out.T, "zero", axis=0, tiled=True)

    frame = lax.broadcasted_iota(jnp.int32, (KER, NB * BLOCK), 1)
    centre = frame - lax.broadcasted_iota(jnp.int32, (KER, NB * BLOCK), 0) + LEFT
    meets = jnp.zeros((KER, NB * BLOCK), jnp.bool_)
    for u in range(3):
        begin, stop = bounds[u], bounds[u + 1]
        within = (jnp.minimum(frame, centre) >= begin) & (jnp.maximum(frame, centre) < stop)
        meets = meets | within

    half = width // 2
    column = lax.broadcasted_iota(jnp.int32, (width, half), 0)
    place = lax.broadcasted_iota(jnp.int32, (width, half), 1)
    even = column == place + share * (place // share)
    odd = column == place + share * (place // share) + share
    own_columns = jnp.where(core == 0, even, odd).astype(BF16)
    other_columns = jnp.where(core == 0, odd, even).astype(BF16)
    swap = [(i, i ^ 1) for i in range(16)]

    sums = stats(bounds, x, kern_full, send)
    for steps in ((1,), (2,), (4, 8, 12)):
        sums, _ = add_from(sums, "zero", [zero_step(step) for step in steps])
    sums = jnp.concatenate([sums, info], axis=0)
    sums, cot, x = lax.optimization_barrier((sums, cot, x))
    x_sums = jnp.dot(meets.astype(BF16), x, preferred_element_type=F32)
    cot_own = jnp.dot(cot, own_columns, preferred_element_type=F32).astype(BF16)
    cot_send = jnp.dot(cot, other_columns, preferred_element_type=F32).astype(BF16)
    back = jnp.dot(cot, w_t, preferred_element_type=F32)
    sums, (x_sums, cot_own, cot_send) = add_from(
        sums, "dp", [dp_step(step, True) for step in (1, 2, 3)], x_sums, cot_own, cot_send
    )
    cot_other = lax.ppermute(cot_send, "zero", swap)
    sums, (back,) = add_from(sums, "dp", [dp_step(step, False) for step in (1, 2, 3)], back)
    info = lax.dynamic_slice_in_dim(sums[2], lax.axis_index("dp") * 96, 80, 0).astype(jnp.int32)
    frame_count = jnp.float32(BLOCKS * BLOCK * 256)
    mean = sums[0] / frame_count
    var = sums[1] / frame_count - mean * mean
    inverse = lax.rsqrt(var + EPS)
    norm = jnp.stack([mean, inverse, small_full[KER], small_full[KER + 1]])

    h, sw = hidden(info, got, kern_full, norm, back, x_sums, cot_other)
    sw_other = lax.ppermute(sw, "zero", swap)
    contract = (((0,), (0,)), ((), ()))
    term = lax.dot_general(sw, cot_own, contract, preferred_element_type=F32)
    sw_other, term = lax.optimization_barrier((sw_other, term))
    term = term + lax.dot_general(sw_other, cot_other, contract, preferred_element_type=F32)
    term = term.astype(BF16).reshape(16, share, half)
    term = lax.all_to_all(term, "dp", 0, 0, tiled=True)

    grads = terms(info, got, h, back, norm)
    out = lax.dot_general(
        sw, w_t, (((1,), (1,)), ((), ())), preferred_element_type=F32
    ).astype(BF16)

    grads = jnp.concatenate([grads, x_sums], axis=0).reshape(104, 8, 2, share)
    grads = jnp.transpose(grads, (2, 1, 0, 3))
    grads_other = lax.ppermute(
        lax.dynamic_index_in_dim(grads, 1 - core, 0, False), "zero", swap
    )
    grads = lax.dynamic_index_in_dim(grads, core, 0, False) + grads_other

    term = jnp.sum(term.astype(F32), axis=0).reshape(share, 8, share)
    both = jnp.concatenate([jnp.transpose(term, (1, 0, 2)), grads], axis=1)
    both = lax.all_to_all(
        both,
        "zero",
        0,
        0,
        axis_index_groups=[[i for i in range(16) if i % 2 == c] for c in range(2)],
        tiled=True,
    )
    last = jnp.sum(both, axis=0)
    last = lax.all_to_all(
        jnp.broadcast_to(last[None], (16,) + last.shape), "dp", 0, 0, tiled=True
    )
    part_w = last[:, :share].reshape(width, share)
    grads = jnp.sum(last[:, share:], axis=0)

    own = lax.dynamic_slice_in_dim(norm, zero_id * share, share, 1)
    da_x, hat_x, x_k = grads[:KER], grads[KER : 2 * KER], grads[72 : 72 + KER]
    sum_x, sum_1 = grads[64], grads[65]
    part_k = (own[2] * own[1]) * (da_x - (sum_1 / frame_count) * x_k - (sum_x / frame_count) * hat_x)
    return out[None, None], part_w, part_k, jnp.stack([sum_x, sum_1])


def solution(mesh):
    return jax.shard_map(
        per_device,
        mesh=mesh,
        in_specs=(
            P("dp", "zero", None, None),
            P("dp", "zero", None),
            P("dp", "zero", None),
            P("dp", "zero", None, None),
            P(None, "zero"),
            P(None, "zero"),
            P(None, "zero"),
        ),
        out_specs=(P("dp", "zero", None, None), P(None, "zero"), P(None, "zero"), P(None, "zero")),
        check_vma=False,
    )
```

```python
import jax
import jax.numpy as jnp
from jax import lax
from jax.experimental import pallas as pl
from jax.experimental.pallas import tpu as pltpu
from jax.sharding import PartitionSpec as P

KER = 32
BLOCK = 64
BLOCKS = 8
NB = 12
LEFT = 16
WIN = 96
LANES = 128
TILES = 4
WIDE = TILES * LANES
EPS = 1e-05
F32 = jnp.float32
BF16 = jnp.bfloat16
SMEM_SPEC = pl.BlockSpec(memory_space=pltpu.SMEM)


def cost(microseconds):
    return pl.CostEstimate(
        flops=microseconds * 1_100_000_000, bytes_accessed=1_000_000, transcendentals=0
    )


def row_iota(rows):
    return lax.broadcasted_iota(jnp.int32, (rows, LANES), 0)


def tile(g):
    return pl.ds(LANES * g, LANES)


def spread_taps(kern_ref, taps):
    for g in range(TILES):
        for k in range(KER):
            row = kern_ref[pl.ds(k, 1), tile(g)]
            taps[g, pl.ds(8 * k, 8), :] = jnp.broadcast_to(row, (8, LANES))


def row_of(v):
    return 8 * row_iota(8) + v


def shifted(window, g, w):
    return window[g, pl.ds(w, 8, stride=8), :]


def conv_block(window, taps, g):
    xs = [shifted(window, g, w) for w in range(7)]
    acc = [None] * 8
    for k in range(KER):
        xs.append(shifted(window, g, k + 7))
        tap = taps[g, pl.ds(8 * k, 8), :]
        for v in range(8):
            acc[v] = tap * xs[v] if k == 0 else acc[v] + tap * xs[v]
        xs.pop(0)
    return acc


def utterances(first, second, row):
    low = (first <= row).astype(jnp.int32) + (second <= row).astype(jnp.int32)
    top = row + BLOCK - 1
    high = (first <= top).astype(jnp.int32) + (second <= top).astype(jnp.int32)
    return low, high + 1


def pack_kernel(target_ref, segment_ref, x_ref, out_ref, bounds_ref):
    @pl.when(pl.program_id(0) == 0)
    def _():
        live = jnp.int32(0)
        for slot in range(NB):
            live = live + (target_ref[slot] >= 0).astype(jnp.int32)
        segment = segment_ref[...]
        bounds_ref[0] = jnp.int32(0)
        for u in (1, 2):
            ended = jnp.sum((segment < u).astype(jnp.int32))
            bounds_ref[u] = jnp.minimum(ended, BLOCK * live)
        bounds_ref[3] = BLOCK * live

    row = lax.broadcasted_iota(jnp.int32, (16, LANES), 0)
    lane = lax.broadcasted_iota(jnp.int32, (16, LANES), 1)
    width = x_ref.shape[1]
    for i in range(4):
        group = 4 * pl.program_id(0) + i
        b = jnp.int32(-1)
        for slot in range(NB):
            b = jnp.where(target_ref[slot] == group, slot, b)

        @pl.when(b >= 0)
        def _():
            before = pl.multiple_of(jnp.maximum(b * BLOCK - LEFT, 0), 16)
            start = pl.multiple_of(b * BLOCK, 16)
            after = pl.multiple_of(jnp.minimum((b + 1) * BLOCK, NB * BLOCK - 16), 16)
            out_ref[i, pl.ds(0, 16), :] = x_ref[pl.ds(before, 16), :]
            out_ref[i, pl.ds(16, 64), :] = x_ref[pl.ds(start, 64), :]
            rest = pl.ds(LANES, width - LANES)
            out_ref[i, pl.ds(80, 16), rest] = x_ref[pl.ds(after, 16), rest]
            info = jnp.ones((16, LANES), jnp.int32)
            for u in range(4):
                end = jnp.clip(bounds_ref[u] - (b * BLOCK - LEFT), 0, WIN)
                info = jnp.where(lane == u + 1, end, info)
            tail = x_ref[pl.ds(after, 16), pl.ds(0, LANES)].astype(F32)
            tail = jnp.where(row == 15, info.astype(F32), tail)
            out_ref[i, pl.ds(80, 16), pl.ds(0, LANES)] = tail.astype(BF16)

        @pl.when(b < 0)
        def _():
            out_ref[i] = jnp.zeros_like(out_ref[i])


def pack(target_row, segment, x):
    rows, width = x.shape
    return pl.pallas_call(
        pack_kernel,
        grid=(4,),
        out_shape=(
            jax.ShapeDtypeStruct((16, WIN, width), BF16),
            jax.ShapeDtypeStruct((4,), jnp.int32),
        ),
        in_specs=[
            SMEM_SPEC,
            pl.BlockSpec((NB // 2, 2 * BLOCK), lambda r: (0, 0)),
            pl.BlockSpec((rows, width), lambda r: (0, 0)),
        ],
        out_specs=(pl.BlockSpec((4, WIN, width), lambda r: (r, 0, 0)), SMEM_SPEC),
        cost_estimate=cost(4),
        compiler_params=pltpu.CompilerParams(vmem_limit_bytes=32 * 1024 * 1024),
        name="pack",
    )(target_row, segment.reshape(NB // 2, 2 * BLOCK), x)


def stats_kernel(bounds_ref, x_ref, kern_ref, _, out_ref, window, taps, sums):
    spread_taps(kern_ref, taps)
    sums[...] = jnp.zeros_like(sums)
    first, second, end = bounds_ref[1], bounds_ref[2], bounds_ref[3]

    def block(n, carry):
        row = n * BLOCK

        def part(u, inner):
            begin, stop = bounds_ref[u], bounds_ref[u + 1]
            before = jnp.maximum(row - LEFT, 0)
            after = jnp.minimum(row + BLOCK, NB * BLOCK - 16)
            for source, place, size in ((before, 0, 16), (row, 16, 64), (after, 80, 16)):
                rows = row_iota(size) + (row - LEFT + place)
                keep = (rows >= begin) & (rows < stop)
                for g in range(TILES):
                    x = x_ref[pl.ds(pl.multiple_of(source, 16), size), tile(g)].astype(F32)
                    window[g, pl.ds(place, size), :] = jnp.where(keep, x, 0.0)
            for g in range(TILES):
                acc = conv_block(window, taps, g)
                total, square = sums[g, pl.ds(0, 8), :], sums[g, pl.ds(8, 8), :]
                for v in range(8):
                    at = row_of(v) + row
                    h = jnp.where((at >= begin) & (at < stop), acc[v], 0.0)
                    total = total + h
                    square = square + h * h
                sums[g, pl.ds(0, 8), :] = total
                sums[g, pl.ds(8, 8), :] = square
            return inner

        return lax.fori_loop(*utterances(first, second, row), part, carry)

    lax.fori_loop(0, end // BLOCK, block, 0)
    for g in range(TILES):
        for i in range(2):
            part = sums[g, pl.ds(8 * i, 8), :]
            out_ref[pl.ds(i, 1), tile(g)] = jnp.sum(part, axis=0, keepdims=True)


def stats(bounds, x, kern, earlier):
    width = x.shape[1]
    return pl.pallas_call(
        stats_kernel,
        grid=(width // WIDE,),
        out_shape=jax.ShapeDtypeStruct((2, width), F32),
        in_specs=[
            SMEM_SPEC,
            pl.BlockSpec((NB * BLOCK, WIDE), lambda c: (0, c)),
            pl.BlockSpec((KER, WIDE), lambda c: (0, c)),
            pl.BlockSpec(memory_space=pl.ANY),
        ],
        out_specs=pl.BlockSpec((2, WIDE), lambda c: (0, c)),
        scratch_shapes=[
            pltpu.VMEM((TILES, WIN, LANES), F32),
            pltpu.VMEM((TILES, 8 * KER, LANES), F32),
            pltpu.VMEM((TILES, 16, LANES), F32),
        ],
        cost_estimate=cost(15),
        name="stats",
    )(bounds, x, kern, earlier)


def live_parts(info_ref, got_ref, window, per_part):
    def slot(s, n):
        valid = info_ref[5 * s] > 0

        @pl.when(valid)
        def _():
            def part(u, carry):
                begin, stop = info_ref[5 * s + 1 + u], info_ref[5 * s + 2 + u]
                rows = row_iota(WIN)
                keep = (rows >= begin) & (rows < stop)
                for g in range(TILES):
                    x = got_ref[s, :, tile(g)].astype(F32)
                    window[g] = jnp.where(keep, x, 0.0)
                per_part(pl.multiple_of(n * BLOCK, BLOCK), begin - LEFT, stop - LEFT)
                return carry

            lax.fori_loop(
                *utterances(info_ref[5 * s + 2], info_ref[5 * s + 3], LEFT), part, 0
            )

        return n + valid.astype(jnp.int32)

    lax.fori_loop(0, 16, slot, 0)


def hidden_kernel(info_ref, got_ref, kern_ref, *rest):
    h_ref, window, taps = rest[-3:]
    spread_taps(kern_ref, taps)

    def per_part(at, begin, stop):
        for g in range(TILES):
            acc = conv_block(window, taps, g)
            for v in range(8):
                place = pl.ds(at + v, 8, stride=8)
                keep = (row_of(v) >= begin) & (row_of(v) < stop)
                h_ref[g, place, :] = jnp.where(keep, acc[v], h_ref[g, place, :])

    live_parts(info_ref, got_ref, window, per_part)


def hidden(info, got, kern, *earlier):
    width = got.shape[2]
    rows = BLOCKS * BLOCK
    return pl.pallas_call(
        hidden_kernel,
        grid=(width // WIDE,),
        out_shape=jax.ShapeDtypeStruct((width // LANES, rows, LANES), F32),
        in_specs=[
            SMEM_SPEC,
            pl.BlockSpec((16, WIN, WIDE), lambda c: (0, 0, c)),
            pl.BlockSpec((KER, WIDE), lambda c: (0, c)),
        ]
        + [pl.BlockSpec(memory_space=pl.ANY)] * len(earlier),
        out_specs=pl.BlockSpec((TILES, rows, LANES), lambda c: (c, 0, 0)),
        scratch_shapes=[
            pltpu.VMEM((TILES, WIN, LANES), F32),
            pltpu.VMEM((TILES, 8 * KER, LANES), F32),
        ],
        cost_estimate=cost(12),
        name="hidden",
    )(info, got, kern, *earlier)


def swish_kernel(h_ref, norm_ref, sw_ref):
    for g in range(TILES):
        mean, inverse = norm_ref[pl.ds(0, 1), tile(g)], norm_ref[pl.ds(1, 1), tile(g)]
        scale, shift = norm_ref[pl.ds(2, 1), tile(g)], norm_ref[pl.ds(3, 1), tile(g)]
        a = (h_ref[g] - mean) * inverse * scale + shift
        sw_ref[:, tile(g)] = (a * jax.nn.sigmoid(a)).astype(BF16)


def swish(h, norm):
    tiles, rows, _ = h.shape
    return pl.pallas_call(
        swish_kernel,
        grid=(tiles // TILES,),
        out_shape=jax.ShapeDtypeStruct((rows, tiles * LANES), BF16),
        in_specs=[
            pl.BlockSpec((TILES, rows, LANES), lambda c: (c, 0, 0)),
            pl.BlockSpec((4, WIDE), lambda c: (0, c)),
        ],
        out_specs=pl.BlockSpec((rows, WIDE), lambda c: (0, c)),
        cost_estimate=cost(3),
        name="swish",
    )(h, norm)


def terms_kernel(
    info_ref, got_ref, h_ref, wide_ref, norm_ref, out_ref, window, back_ref, acc_a, acc_x, sums
):
    for g in range(TILES):
        back_ref[g] = wide_ref[:, tile(g)]
    acc_a[...] = jnp.zeros_like(acc_a)
    acc_x[...] = jnp.zeros_like(acc_x)
    sums[...] = jnp.zeros_like(sums)

    def per_tile(g, at, begin, stop):
        mean, inverse = norm_ref[pl.ds(0, 1), tile(g)], norm_ref[pl.ds(1, 1), tile(g)]
        scale, shift = norm_ref[pl.ds(2, 1), tile(g)], norm_ref[pl.ds(3, 1), tile(g)]
        das, hats = [], []
        sum_x, sum_1 = sums[g, pl.ds(0, 8), :], sums[g, pl.ds(8, 8), :]
        for v in range(8):
            place = pl.ds(at + v, 8, stride=8)
            keep = (row_of(v) >= begin) & (row_of(v) < stop)
            hat = (h_ref[g, place, :] - mean) * inverse
            a = hat * scale + shift
            sig = jax.nn.sigmoid(a)
            da = back_ref[g, place, :] * (sig * (1.0 + a * (1.0 - sig)))
            da = jnp.where(keep, da, 0.0)
            hat = jnp.where(keep, hat, 0.0)
            sum_x = sum_x + da * hat
            sum_1 = sum_1 + da
            das.append(da)
            hats.append(hat)
        sums[g, pl.ds(0, 8), :] = sum_x
        sums[g, pl.ds(8, 8), :] = sum_1
        xs = [shifted(window, g, w) for w in range(7)]
        for k in range(KER):
            xs.append(shifted(window, g, k + 7))
            place = pl.ds(8 * k, 8)
            for acc, rows in ((acc_a, das), (acc_x, hats)):
                terms_k = [rows[v] * xs[v] for v in range(8)]
                while len(terms_k) > 1:
                    terms_k = [p + q for p, q in zip(terms_k[::2], terms_k[1::2])]
                acc[g, place, :] += terms_k[0]
            xs.pop(0)

    def per_part(at, begin, stop):
        for g in range(TILES):
            per_tile(g, at, begin, stop)

    live_parts(info_ref, got_ref, window, per_part)
    for g in range(TILES):
        for acc, first in ((acc_a, 0), (acc_x, KER)):
            rows = acc[g].reshape(KER, 8, LANES)
            out_ref[pl.ds(first, KER), tile(g)] = jnp.sum(rows, axis=1)
        for i in range(2):
            part = sums[g, pl.ds(8 * i, 8), :]
            out_ref[pl.ds(2 * KER + i, 1), tile(g)] = jnp.sum(part, axis=0, keepdims=True)
    out_ref[pl.ds(66, 14), :] = jnp.zeros((14, WIDE), F32)


def terms(info, got, h, back, norm):
    width = got.shape[2]
    return pl.pallas_call(
        terms_kernel,
        grid=(width // WIDE,),
        out_shape=jax.ShapeDtypeStruct((80, width), F32),
        in_specs=[
            SMEM_SPEC,
            pl.BlockSpec((16, WIN, WIDE), lambda c: (0, 0, c)),
            pl.BlockSpec((TILES, BLOCKS * BLOCK, LANES), lambda c: (c, 0, 0)),
            pl.BlockSpec((BLOCKS * BLOCK, WIDE), lambda c: (0, c)),
            pl.BlockSpec((4, WIDE), lambda c: (0, c)),
        ],
        out_specs=pl.BlockSpec((80, WIDE), lambda c: (0, c)),
        scratch_shapes=[
            pltpu.VMEM((TILES, WIN, LANES), F32),
            pltpu.VMEM((TILES, BLOCKS * BLOCK, LANES), F32),
            pltpu.VMEM((TILES, 8 * KER, LANES), F32),
            pltpu.VMEM((TILES, 8 * KER, LANES), F32),
            pltpu.VMEM((TILES, 16, LANES), F32),
        ],
        cost_estimate=cost(25),
        name="terms",
    )(info, got, h, back, norm)


def zero_step(step):
    if step < 4:
        return [(i, i ^ step) for i in range(16)]
    return [(i, (i + step) % 16) for i in range(16)]


def dp_step(step, row):
    if row:
        return [(i, 4 * (i // 4) + (i + step) % 4) for i in range(16)]
    return [(i, (i + 4 * step) % 16) for i in range(16)]


def add_from(x, axis, steps, *meanwhile):
    parts = [lax.ppermute(x, axis, step) for step in steps]
    parts, meanwhile = lax.optimization_barrier((parts, meanwhile))
    return sum(parts, x), meanwhile


def gather_small(x, zero_id, send):
    for step, first in ((1, zero_id % 2 == 0), (2, (zero_id // 2) % 2 == 0)):
        other = lax.ppermute(x, "zero", zero_step(step))
        other, send = lax.optimization_barrier((other, send))
        x = jnp.stack([jnp.where(first, x, other), jnp.where(first, other, x)])
    pairs = [x] + [lax.ppermute(x, "zero", zero_step(step)) for step in (4, 8, 12)]
    place = zero_id // 4

    def join(pairs):
        parts = []
        for q in range(4):
            part = pairs[0]
            for s in range(1, 4):
                part = jnp.where((place - s) % 4 == q, pairs[s], part)
            parts.append(part)
        return jnp.stack(parts).reshape((16,) + x.shape[2:])

    return pairs, join


def per_device(frames, segments, targets, cotangent, w_out, kernel, norm_params):
    x, seg, target_row, cot = frames[0, 0], segments[0, 0], targets[0, 0], cotangent[0, 0]
    width = x.shape[1]
    share, half = width // 16, width // 2
    zero_id = lax.axis_index("zero")
    core = lax.rem(zero_id, 2)
    swap = zero_step(1)

    small = jnp.concatenate([kernel, norm_params, jnp.zeros((14, share), BF16)], axis=0)
    small, target_row = lax.optimization_barrier((small, target_row))
    send, bounds = pack(target_row, seg, x)
    got = lax.all_to_all(send, "dp", 0, 0, tiled=True)
    w_t = lax.all_gather(w_out.T, "zero", axis=0, tiled=True)

    frame = lax.broadcasted_iota(jnp.int32, (KER, NB * BLOCK), 1)
    centre = frame - lax.broadcasted_iota(jnp.int32, (KER, NB * BLOCK), 0) + LEFT
    meets = jnp.zeros((KER, NB * BLOCK), jnp.bool_)
    for u in range(3):
        begin, stop = bounds[u], bounds[u + 1]
        within = (jnp.minimum(frame, centre) >= begin) & (jnp.maximum(frame, centre) < stop)
        meets = meets | within
    x_sums = jnp.dot(meets.astype(BF16), x, preferred_element_type=F32)

    pairs, join = gather_small(small, zero_id, send)
    pairs, x_sums = lax.optimization_barrier((pairs, x_sums))
    small_full = jnp.transpose(join(pairs), (1, 0, 2)).reshape(48, width).astype(F32)
    kern_full = small_full[:KER]

    sums = stats(bounds, x, kern_full, send)
    for steps in ((1,), (2,), (4, 8, 12)):
        sums, _ = add_from(sums, "zero", [zero_step(step) for step in steps])
    sums, cot_now = lax.optimization_barrier((sums, cot))
    back = jnp.dot(cot_now, w_t, preferred_element_type=F32)
    sums, (back,) = add_from(sums, "dp", [dp_step(step, True) for step in (1, 2, 3)], back)

    got, back = lax.optimization_barrier((got, back))
    info = got[:, WIN - 1, :5].astype(jnp.int32).reshape(80)
    cot_other = lax.ppermute(cot, "zero", swap)
    h = hidden(info, got, kern_full, cot_other)
    sums, (h,) = add_from(sums, "dp", [dp_step(step, False) for step in (1, 2, 3)], h)
    frame_count = jnp.float32(BLOCKS * BLOCK * 256)
    mean = sums[0] / frame_count
    var = sums[1] / frame_count - mean * mean
    inverse = lax.rsqrt(var + EPS)
    norm = jnp.stack([mean, inverse, small_full[KER], small_full[KER + 1]])
    sw = swish(h, norm)

    sw_other = lax.ppermute(
        lax.dynamic_slice_in_dim(sw, (1 - core) * half, half, 1), "zero", swap
    )
    contract = (((0,), (0,)), ((), ()))
    sw_own = lax.dynamic_slice_in_dim(sw, core * half, half, 1)
    term = lax.dot_general(sw_own, cot, contract, preferred_element_type=F32)
    sw_other, term = lax.optimization_barrier((sw_other, term))
    term = term + lax.dot_general(sw_other, cot_other, contract, preferred_element_type=F32)
    term = term.astype(BF16).reshape(16, share // 2, width)
    term = lax.all_to_all(term, "dp", 0, 0, tiled=True)

    grads = terms(info, got, h, back, norm)
    out = lax.dot_general(
        sw, w_t, (((1,), (1,)), ((), ())), preferred_element_type=F32
    ).astype(BF16)

    grads = jnp.concatenate([grads, x_sums], axis=0)
    grads_other = lax.ppermute(
        lax.dynamic_slice_in_dim(grads, (1 - core) * 56, 56, 0), "zero", swap
    )
    grads = lax.dynamic_slice_in_dim(grads, core * 56, 56, 0) + grads_other

    term = jnp.sum(term.astype(F32), axis=0)
    both = jnp.concatenate([term, grads], axis=0).reshape(-1, 16, share)
    both = lax.all_to_all(jnp.transpose(both, (1, 0, 2)), "zero", 0, 0, tiled=True)
    last = jnp.sum(both.reshape((8, 2) + both.shape[1:]), axis=0)
    last = lax.all_to_all(
        jnp.broadcast_to(last[None], (16,) + last.shape), "dp", 0, 0, tiled=True
    )
    part_w = jnp.transpose(last[:, :, : share // 2], (1, 0, 2, 3)).reshape(width, share)
    grads = jnp.sum(last[:, :, share // 2 :], axis=0).reshape(112, share)

    own = lax.dynamic_slice_in_dim(norm, zero_id * share, share, 1)
    da_x, hat_x, x_k = grads[:KER], grads[KER : 2 * KER], grads[80 : 80 + KER]
    sum_x, sum_1 = grads[64], grads[65]
    part_k = (own[2] * own[1]) * (da_x - (sum_1 / frame_count) * x_k - (sum_x / frame_count) * hat_x)
    return out[None, None], part_w, part_k, jnp.stack([sum_x, sum_1])


def solution(mesh):
    return jax.shard_map(
        per_device,
        mesh=mesh,
        in_specs=(
            P("dp", "zero", None, None),
            P("dp", "zero", None),
            P("dp", "zero", None),
            P("dp", "zero", None, None),
            P(None, "zero"),
            P(None, "zero"),
            P(None, "zero"),
        ),
        out_specs=(P("dp", "zero", None, None), P(None, "zero"), P(None, "zero"), P(None, "zero")),
        check_vma=False,
    )
```

```python
import jax
import jax.numpy as jnp
from jax import lax
from jax.experimental import pallas as pl
from jax.experimental.pallas import tpu as pltpu
from jax.sharding import PartitionSpec as P

KER = 32
BLOCK = 64
BLOCKS = 8
NB = 12
LEFT = 16
WIN = 96
LANES = 128
TILES = 4
WIDE = TILES * LANES
EPS = 1e-05
F32 = jnp.float32
BF16 = jnp.bfloat16
SMEM_SPEC = pl.BlockSpec(memory_space=pltpu.SMEM)


def cost(microseconds):
    return pl.CostEstimate(
        flops=microseconds * 1_100_000_000, bytes_accessed=1_000_000, transcendentals=0
    )


def row_iota(rows):
    return lax.broadcasted_iota(jnp.int32, (rows, LANES), 0)


def tile(g):
    return pl.ds(LANES * g, LANES)


def spread_taps(kern_ref, taps):
    for g in range(TILES):
        for k in range(KER):
            row = kern_ref[pl.ds(k, 1), tile(g)]
            taps[g, pl.ds(8 * k, 8), :] = jnp.broadcast_to(row, (8, LANES))


def row_of(v, n):
    return n * row_iota(8) + v


def shifted(window, g, w, n):
    return window[g, pl.ds(w, 8, stride=n), :]


def conv_rows(window, taps, g, base, n):
    xs = [shifted(window, g, base + w, n) for w in range(n - 1)]
    acc = [None] * n
    for k in range(KER):
        xs.append(shifted(window, g, base + k + n - 1, n))
        tap = taps[g, pl.ds(8 * k, 8), :]
        for v in range(n):
            acc[v] = tap * xs[v] if k == 0 else acc[v] + tap * xs[v]
        xs.pop(0)
    return acc


def in_rows(alone, begin, stop, per_rows):
    @pl.when(alone)
    def _():
        per_rows(0, 8)

    for base in (0, BLOCK // 2):
        meets = (begin < base + BLOCK // 2) & (stop > base)

        @pl.when(jnp.logical_not(alone) & meets)
        def _():
            per_rows(base, 4)


def utterances(first, second, row):
    low = (first <= row).astype(jnp.int32) + (second <= row).astype(jnp.int32)
    top = row + BLOCK - 1
    high = (first <= top).astype(jnp.int32) + (second <= top).astype(jnp.int32)
    return low, high + 1


def pack_kernel(target_ref, segment_ref, x_ref, out_ref, bounds_ref):
    @pl.when(pl.program_id(0) == 0)
    def _():
        live = jnp.int32(0)
        for slot in range(NB):
            live = live + (target_ref[slot] >= 0).astype(jnp.int32)
        segment = segment_ref[...]
        bounds_ref[0] = jnp.int32(0)
        for u in (1, 2):
            ended = jnp.sum((segment < u).astype(jnp.int32))
            bounds_ref[u] = jnp.minimum(ended, BLOCK * live)
        bounds_ref[3] = BLOCK * live

    row = lax.broadcasted_iota(jnp.int32, (16, LANES), 0)
    lane = lax.broadcasted_iota(jnp.int32, (16, LANES), 1)
    width = x_ref.shape[1]
    for i in range(4):
        group = 4 * pl.program_id(0) + i
        b = jnp.int32(-1)
        for slot in range(NB):
            b = jnp.where(target_ref[slot] == group, slot, b)

        @pl.when(b >= 0)
        def _():
            before = pl.multiple_of(jnp.maximum(b * BLOCK - LEFT, 0), 16)
            start = pl.multiple_of(b * BLOCK, 16)
            after = pl.multiple_of(jnp.minimum((b + 1) * BLOCK, NB * BLOCK - 16), 16)
            out_ref[i, pl.ds(0, 16), :] = x_ref[pl.ds(before, 16), :]
            out_ref[i, pl.ds(16, 64), :] = x_ref[pl.ds(start, 64), :]
            rest = pl.ds(LANES, width - LANES)
            out_ref[i, pl.ds(80, 16), rest] = x_ref[pl.ds(after, 16), rest]
            info = jnp.ones((16, LANES), jnp.int32)
            for u in range(4):
                end = jnp.clip(bounds_ref[u] - (b * BLOCK - LEFT), 0, WIN)
                info = jnp.where(lane == u + 1, end, info)
            tail = x_ref[pl.ds(after, 16), pl.ds(0, LANES)].astype(F32)
            tail = jnp.where(row == 15, info.astype(F32), tail)
            out_ref[i, pl.ds(80, 16), pl.ds(0, LANES)] = tail.astype(BF16)

        @pl.when(b < 0)
        def _():
            out_ref[i] = jnp.zeros_like(out_ref[i])


def pack(target_row, segment, x):
    rows, width = x.shape
    return pl.pallas_call(
        pack_kernel,
        grid=(4,),
        out_shape=(
            jax.ShapeDtypeStruct((16, WIN, width), BF16),
            jax.ShapeDtypeStruct((4,), jnp.int32),
        ),
        in_specs=[
            SMEM_SPEC,
            pl.BlockSpec((NB // 2, 2 * BLOCK), lambda r: (0, 0)),
            pl.BlockSpec((rows, width), lambda r: (0, 0)),
        ],
        out_specs=(pl.BlockSpec((4, WIN, width), lambda r: (r, 0, 0)), SMEM_SPEC),
        cost_estimate=cost(4),
        compiler_params=pltpu.CompilerParams(vmem_limit_bytes=32 * 1024 * 1024),
        name="pack",
    )(target_row, segment.reshape(NB // 2, 2 * BLOCK), x)


def stats_kernel(bounds_ref, x_ref, kern_ref, _, out_ref, x_sums_ref, window, taps, sums):
    spread_taps(kern_ref, taps)
    sums[...] = jnp.zeros_like(sums)
    first, second, end = bounds_ref[1], bounds_ref[2], bounds_ref[3]

    frame = lax.broadcasted_iota(jnp.int32, (KER, NB * BLOCK), 1)
    centre = frame - lax.broadcasted_iota(jnp.int32, (KER, NB * BLOCK), 0) + LEFT
    low, high = jnp.minimum(frame, centre), jnp.maximum(frame, centre)
    meets = jnp.zeros((KER, NB * BLOCK), F32)
    for u in range(3):
        meets = jnp.where((low >= bounds_ref[u]) & (high < bounds_ref[u + 1]), 1.0, meets)
    x_sums_ref[...] = jnp.dot(meets.astype(BF16), x_ref[...], preferred_element_type=F32)

    def block(n, carry):
        row = n * BLOCK
        low, high = utterances(first, second, row)

        def part(u, inner):
            begin, stop = bounds_ref[u], bounds_ref[u + 1]
            before = jnp.maximum(row - LEFT, 0)
            after = jnp.minimum(row + BLOCK, NB * BLOCK - 16)
            for source, place, size in ((before, 0, 16), (row, 16, 64), (after, 80, 16)):
                rows = row_iota(size) + (row - LEFT + place)
                keep = (rows >= begin) & (rows < stop)
                for g in range(TILES):
                    x = x_ref[pl.ds(pl.multiple_of(source, 16), size), tile(g)].astype(F32)
                    window[g, pl.ds(place, size), :] = jnp.where(keep, x, 0.0)

            def per_rows(base, n):
                for g in range(TILES):
                    acc = conv_rows(window, taps, g, base, n)
                    total, square = sums[g, pl.ds(0, 8), :], sums[g, pl.ds(8, 8), :]
                    for v in range(n):
                        at = row_of(v, n) + (row + base)
                        h = jnp.where((at >= begin) & (at < stop), acc[v], 0.0)
                        total = total + h
                        square = square + h * h
                    sums[g, pl.ds(0, 8), :] = total
                    sums[g, pl.ds(8, 8), :] = square

            in_rows(low + 1 == high, begin - row, stop - row, per_rows)
            return inner

        return lax.fori_loop(low, high, part, carry)

    lax.fori_loop(0, end // BLOCK, block, 0)
    for g in range(TILES):
        for i in range(2):
            part = sums[g, pl.ds(8 * i, 8), :]
            out_ref[pl.ds(i, 1), tile(g)] = jnp.sum(part, axis=0, keepdims=True)


def stats(bounds, x, kern, earlier):
    width = x.shape[1]
    return pl.pallas_call(
        stats_kernel,
        grid=(width // WIDE,),
        out_shape=(
            jax.ShapeDtypeStruct((2, width), F32),
            jax.ShapeDtypeStruct((KER, width), F32),
        ),
        in_specs=[
            SMEM_SPEC,
            pl.BlockSpec((NB * BLOCK, WIDE), lambda c: (0, c)),
            pl.BlockSpec((KER, WIDE), lambda c: (0, c)),
            pl.BlockSpec(memory_space=pl.ANY),
        ],
        out_specs=(
            pl.BlockSpec((2, WIDE), lambda c: (0, c)),
            pl.BlockSpec((KER, WIDE), lambda c: (0, c)),
        ),
        scratch_shapes=[
            pltpu.VMEM((TILES, WIN, LANES), F32),
            pltpu.VMEM((TILES, 8 * KER, LANES), F32),
            pltpu.VMEM((TILES, 16, LANES), F32),
        ],
        cost_estimate=cost(15),
        name="stats",
    )(bounds, x, kern, earlier)


def live_parts(info_ref, got_ref, window, per_part, per_block=None):
    def slot(s, n):
        valid = info_ref[5 * s] > 0

        @pl.when(valid)
        def _():
            at = pl.multiple_of(n * BLOCK, BLOCK)
            low, high = utterances(info_ref[5 * s + 2], info_ref[5 * s + 3], LEFT)

            def part(u, carry):
                begin, stop = info_ref[5 * s + 1 + u], info_ref[5 * s + 2 + u]
                rows = row_iota(WIN)
                keep = (rows >= begin) & (rows < stop)
                for g in range(TILES):
                    x = got_ref[s, :, tile(g)].astype(F32)
                    window[g] = jnp.where(keep, x, 0.0)
                begin, stop = begin - LEFT, stop - LEFT

                def per_rows(base, groups):
                    per_part(at + base, begin - base, stop - base, base, groups)

                in_rows(low + 1 == high, begin, stop, per_rows)
                return carry

            lax.fori_loop(low, high, part, 0)
            if per_block is not None:
                per_block(at)

        return n + valid.astype(jnp.int32)

    lax.fori_loop(0, 16, slot, 0)


def hidden_kernel(info_ref, got_ref, kern_ref, *rest):
    h_ref, window, rows, taps = rest[-4:]
    spread_taps(kern_ref, taps)

    def per_part(at, begin, stop, base, n):
        for g in range(TILES):
            acc = conv_rows(window, taps, g, base, n)
            for v in range(n):
                place = pl.ds(base + v, 8, stride=n)
                keep = (row_of(v, n) >= begin) & (row_of(v, n) < stop)
                rows[g, place, :] = jnp.where(keep, acc[v], rows[g, place, :])

    def per_block(at):
        for g in range(TILES):
            h_ref[pl.ds(at, BLOCK), tile(g)] = rows[g]

    live_parts(info_ref, got_ref, window, per_part, per_block)


def hidden(info, got, kern, *earlier):
    width = got.shape[2]
    rows = BLOCKS * BLOCK
    return pl.pallas_call(
        hidden_kernel,
        grid=(width // WIDE,),
        out_shape=jax.ShapeDtypeStruct((rows, width), F32),
        in_specs=[
            SMEM_SPEC,
            pl.BlockSpec((16, WIN, WIDE), lambda c: (0, 0, c)),
            pl.BlockSpec((KER, WIDE), lambda c: (0, c)),
        ]
        + [pl.BlockSpec(memory_space=pl.ANY)] * len(earlier),
        out_specs=pl.BlockSpec((rows, WIDE), lambda c: (0, c)),
        scratch_shapes=[
            pltpu.VMEM((TILES, WIN, LANES), F32),
            pltpu.VMEM((TILES, BLOCK, LANES), F32),
            pltpu.VMEM((TILES, 8 * KER, LANES), F32),
        ],
        cost_estimate=cost(12),
        name="hidden",
    )(info, got, kern, *earlier)


def terms_kernel(
    info_ref, got_ref, wide_h, wide_back, norm_ref, out_ref, window, h_ref, back_ref, acc_a, acc_x, sums
):
    for g in range(TILES):
        h_ref[g] = wide_h[:, tile(g)]
        back_ref[g] = wide_back[:, tile(g)]
    acc_a[...] = jnp.zeros_like(acc_a)
    acc_x[...] = jnp.zeros_like(acc_x)
    sums[...] = jnp.zeros_like(sums)

    def per_tile(g, at, begin, stop, base, n):
        mean, inverse = norm_ref[pl.ds(0, 1), tile(g)], norm_ref[pl.ds(1, 1), tile(g)]
        scale, shift = norm_ref[pl.ds(2, 1), tile(g)], norm_ref[pl.ds(3, 1), tile(g)]
        das, hats = [], []
        sum_x, sum_1 = sums[g, pl.ds(0, 8), :], sums[g, pl.ds(8, 8), :]
        for v in range(n):
            place = pl.ds(at + v, 8, stride=n)
            keep = (row_of(v, n) >= begin) & (row_of(v, n) < stop)
            hat = (h_ref[g, place, :] - mean) * inverse
            a = hat * scale + shift
            sig = jax.nn.sigmoid(a)
            da = back_ref[g, place, :] * (sig * (1.0 + a * (1.0 - sig)))
            da = jnp.where(keep, da, 0.0)
            hat = jnp.where(keep, hat, 0.0)
            sum_x = sum_x + da * hat
            sum_1 = sum_1 + da
            das.append(da)
            hats.append(hat)
        sums[g, pl.ds(0, 8), :] = sum_x
        sums[g, pl.ds(8, 8), :] = sum_1
        xs = [shifted(window, g, base + w, n) for w in range(n - 1)]
        for k in range(KER):
            xs.append(shifted(window, g, base + k + n - 1, n))
            place = pl.ds(8 * k, 8)
            for acc, rows in ((acc_a, das), (acc_x, hats)):
                terms_k = [rows[v] * xs[v] for v in range(n)]
                while len(terms_k) > 1:
                    terms_k = [p + q for p, q in zip(terms_k[::2], terms_k[1::2])]
                acc[g, place, :] += terms_k[0]
            xs.pop(0)

    def per_part(at, begin, stop, base, n):
        for g in range(TILES):
            per_tile(g, at, begin, stop, base, n)

    live_parts(info_ref, got_ref, window, per_part)
    for g in range(TILES):
        for acc, first in ((acc_a, 0), (acc_x, KER)):
            rows = acc[g].reshape(KER, 8, LANES)
            out_ref[pl.ds(first, KER), tile(g)] = jnp.sum(rows, axis=1)
        for i in range(2):
            part = sums[g, pl.ds(8 * i, 8), :]
            out_ref[pl.ds(2 * KER + i, 1), tile(g)] = jnp.sum(part, axis=0, keepdims=True)
    out_ref[pl.ds(66, 6), :] = jnp.zeros((6, WIDE), F32)


def terms(info, got, h, back, norm):
    width = got.shape[2]
    return pl.pallas_call(
        terms_kernel,
        grid=(width // WIDE,),
        out_shape=jax.ShapeDtypeStruct((72, width), F32),
        in_specs=[
            SMEM_SPEC,
            pl.BlockSpec((16, WIN, WIDE), lambda c: (0, 0, c)),
            pl.BlockSpec((BLOCKS * BLOCK, WIDE), lambda c: (0, c)),
            pl.BlockSpec((BLOCKS * BLOCK, WIDE), lambda c: (0, c)),
            pl.BlockSpec((4, WIDE), lambda c: (0, c)),
        ],
        out_specs=pl.BlockSpec((72, WIDE), lambda c: (0, c)),
        scratch_shapes=[
            pltpu.VMEM((TILES, WIN, LANES), F32),
            pltpu.VMEM((TILES, BLOCKS * BLOCK, LANES), F32),
            pltpu.VMEM((TILES, BLOCKS * BLOCK, LANES), F32),
            pltpu.VMEM((TILES, 8 * KER, LANES), F32),
            pltpu.VMEM((TILES, 8 * KER, LANES), F32),
            pltpu.VMEM((TILES, 16, LANES), F32),
        ],
        cost_estimate=cost(25),
        name="terms",
    )(info, got, h, back, norm)


def zero_step(step):
    if step < 4:
        return [(i, i ^ step) for i in range(16)]
    return [(i, (i + step) % 16) for i in range(16)]


def dp_step(step, row):
    if row:
        return [(i, 4 * (i // 4) + (i + step) % 4) for i in range(16)]
    return [(i, (i + 4 * step) % 16) for i in range(16)]


def add_from(x, axis, steps, *meanwhile):
    parts = [lax.ppermute(x, axis, step) for step in steps]
    parts, meanwhile = lax.optimization_barrier((parts, meanwhile))
    return sum(parts, x), meanwhile


def gather_small(x, zero_id, send):
    for step, first in ((1, zero_id % 2 == 0), (2, (zero_id // 2) % 2 == 0)):
        other = lax.ppermute(x, "zero", zero_step(step))
        other, send = lax.optimization_barrier((other, send))
        x = jnp.stack([jnp.where(first, x, other), jnp.where(first, other, x)])
    pairs = [x] + [lax.ppermute(x, "zero", zero_step(step)) for step in (4, 8, 12)]
    place = zero_id // 4

    def join(pairs):
        parts = []
        for q in range(4):
            part = pairs[0]
            for s in range(1, 4):
                part = jnp.where((place - s) % 4 == q, pairs[s], part)
            parts.append(part)
        return jnp.stack(parts).reshape((16,) + x.shape[2:])

    return pairs, join


def per_device(frames, segments, targets, cotangent, w_out, kernel, norm_params):
    x, seg, target_row, cot = frames[0, 0], segments[0, 0], targets[0, 0], cotangent[0, 0]
    width = x.shape[1]
    share, half = width // 16, width // 2
    zero_id = lax.axis_index("zero")
    core = lax.rem(zero_id, 2)
    swap = zero_step(1)

    small = jnp.concatenate([kernel, norm_params, jnp.zeros((14, share), BF16)], axis=0)
    small, target_row = lax.optimization_barrier((small, target_row))
    send, bounds = pack(target_row, seg, x)
    got = lax.all_to_all(send, "dp", 0, 0, tiled=True)
    w_t = lax.all_gather(w_out.T, "zero", axis=0, tiled=True)

    column = lax.broadcasted_iota(jnp.int32, (width, half), 0)
    place = lax.broadcasted_iota(jnp.int32, (width, half), 1)
    even = column == place + share * (place // share)
    odd = column == place + share * (place // share) + share
    own_columns = jnp.where(core == 0, even, odd).astype(BF16)
    other_columns = jnp.where(core == 0, odd, even).astype(BF16)

    pairs, join = gather_small(small, zero_id, send)
    cot_own = jnp.dot(cot, own_columns, preferred_element_type=F32).astype(BF16)
    cot_send = jnp.dot(cot, other_columns, preferred_element_type=F32).astype(BF16)
    pairs, cot_own, cot_send = lax.optimization_barrier((pairs, cot_own, cot_send))
    small_full = jnp.transpose(join(pairs), (1, 0, 2)).reshape(48, width).astype(F32)
    kern_full = small_full[:KER]

    sums, x_sums = stats(bounds, x, kern_full, send)
    for steps in ((1,), (2,), (4, 8, 12)):
        sums, _ = add_from(sums, "zero", [zero_step(step) for step in steps])
    sums, cot_now = lax.optimization_barrier((sums, cot))
    back = jnp.dot(cot_now, w_t, preferred_element_type=F32)
    sums, (back,) = add_from(sums, "dp", [dp_step(step, True) for step in (1, 2, 3)], back)

    got, back = lax.optimization_barrier((got, back))
    info = got[:, WIN - 1, :5].astype(jnp.int32).reshape(80)
    cot_other = lax.ppermute(cot_send, "zero", swap)
    h = hidden(info, got, kern_full, cot_other)
    sums, (h,) = add_from(sums, "dp", [dp_step(step, False) for step in (1, 2, 3)], h)
    frame_count = jnp.float32(BLOCKS * BLOCK * 256)
    mean = sums[0] / frame_count
    var = sums[1] / frame_count - mean * mean
    inverse = lax.rsqrt(var + EPS)
    norm = jnp.stack([mean, inverse, small_full[KER], small_full[KER + 1]])
    a = (h - mean) * inverse * norm[2] + norm[3]
    sw = (a * jax.nn.sigmoid(a)).astype(BF16)
    sw_other = lax.ppermute(sw, "zero", swap)
    contract = (((0,), (0,)), ((), ()))
    term = lax.dot_general(sw, cot_own, contract, preferred_element_type=F32)
    sw_other, term = lax.optimization_barrier((sw_other, term))
    term = term + lax.dot_general(sw_other, cot_other, contract, preferred_element_type=F32)
    term = term.astype(BF16).reshape(16, share, half)
    term = lax.all_to_all(term, "dp", 0, 0, tiled=True)

    grads = terms(info, got, h, back, norm)
    out = lax.dot_general(
        sw, w_t, (((1,), (1,)), ((), ())), preferred_element_type=F32
    ).astype(BF16)

    grads = jnp.concatenate([grads, x_sums], axis=0).reshape(104, 8, 2, share)
    grads = jnp.transpose(grads, (2, 1, 0, 3))
    grads_other = lax.ppermute(
        lax.dynamic_index_in_dim(grads, 1 - core, 0, False), "zero", swap
    )
    grads = lax.dynamic_index_in_dim(grads, core, 0, False) + grads_other

    term = jnp.sum(term.astype(F32), axis=0).reshape(share, 8, share)
    both = jnp.concatenate([jnp.transpose(term, (1, 0, 2)), grads], axis=1)
    both = lax.all_to_all(
        both,
        "zero",
        0,
        0,
        axis_index_groups=[[i for i in range(16) if i % 2 == c] for c in range(2)],
        tiled=True,
    )
    last = jnp.sum(both, axis=0)
    last = lax.all_to_all(
        jnp.broadcast_to(last[None], (16,) + last.shape), "dp", 0, 0, tiled=True
    )
    part_w = last[:, :share].reshape(width, share)
    grads = jnp.sum(last[:, share:], axis=0)

    own = lax.dynamic_slice_in_dim(norm, zero_id * share, share, 1)
    da_x, hat_x, x_k = grads[:KER], grads[KER : 2 * KER], grads[72 : 72 + KER]
    sum_x, sum_1 = grads[64], grads[65]
    part_k = (own[2] * own[1]) * (da_x - (sum_1 / frame_count) * x_k - (sum_x / frame_count) * hat_x)
    return out[None, None], part_w, part_k, jnp.stack([sum_x, sum_1])


def solution(mesh):
    return jax.shard_map(
        per_device,
        mesh=mesh,
        in_specs=(
            P("dp", "zero", None, None),
            P("dp", "zero", None),
            P("dp", "zero", None),
            P("dp", "zero", None, None),
            P(None, "zero"),
            P(None, "zero"),
            P(None, "zero"),
        ),
        out_specs=(P("dp", "zero", None, None), P(None, "zero"), P(None, "zero"), P(None, "zero")),
        check_vma=False,
    )
```

```python
import jax
import jax.numpy as jnp
from jax import lax
from jax.experimental import pallas as pl
from jax.experimental.pallas import tpu as pltpu
from jax.sharding import PartitionSpec as P

KER = 32
BLOCK = 64
BLOCKS = 8
NB = 12
LEFT = 16
WIN = 96
LANES = 128
TILES = 4
WIDE = TILES * LANES
EPS = 1e-05
F32 = jnp.float32
BF16 = jnp.bfloat16
SMEM_SPEC = pl.BlockSpec(memory_space=pltpu.SMEM)


def cost(microseconds):
    return pl.CostEstimate(
        flops=microseconds * 1_100_000_000, bytes_accessed=1_000_000, transcendentals=0
    )


def row_iota(rows):
    return lax.broadcasted_iota(jnp.int32, (rows, LANES), 0)


def tile(g):
    return pl.ds(LANES * g, LANES)


def spread_taps(kern_ref, taps):
    for g in range(TILES):
        for k in range(KER):
            row = kern_ref[pl.ds(k, 1), tile(g)]
            taps[g, pl.ds(8 * k, 8), :] = jnp.broadcast_to(row, (8, LANES))


def row_of(v, n):
    return n * row_iota(8) + v


def shifted(window, g, w, n):
    return window[g, pl.ds(w, 8, stride=n), :]


def conv_rows(window, taps, g, base, n):
    xs = [shifted(window, g, base + w, n) for w in range(n - 1)]
    acc = [None] * n
    for k in range(KER):
        xs.append(shifted(window, g, base + k + n - 1, n))
        tap = taps[g, pl.ds(8 * k, 8), :]
        for v in range(n):
            acc[v] = tap * xs[v] if k == 0 else acc[v] + tap * xs[v]
        xs.pop(0)
    return acc


def in_rows(alone, begin, stop, per_rows):
    @pl.when(alone)
    def _():
        per_rows(0, 8)

    for base in (0, BLOCK // 2):
        meets = (begin < base + BLOCK // 2) & (stop > base)

        @pl.when(jnp.logical_not(alone) & meets)
        def _():
            per_rows(base, 4)


def utterances(first, second, row):
    low = (first <= row).astype(jnp.int32) + (second <= row).astype(jnp.int32)
    top = row + BLOCK - 1
    high = (first <= top).astype(jnp.int32) + (second <= top).astype(jnp.int32)
    return low, high + 1


def places_kernel(target_ref, group_ref, segment_ref, bounds_ref, row_ref):
    live = jnp.int32(0)
    for slot in range(NB):
        live = live + (target_ref[slot] >= 0).astype(jnp.int32)
    segment = segment_ref[...]
    bounds = [jnp.int32(0)]
    for u in (1, 2):
        bounds.append(jnp.minimum(jnp.sum((segment < u).astype(jnp.int32)), BLOCK * live))
    bounds.append(BLOCK * live)
    for u in range(4):
        bounds_ref[u] = bounds[u]

    lane = lax.broadcasted_iota(jnp.int32, row_ref.shape, 1)
    group = sum((lane >= 96 * m).astype(jnp.int32) for m in range(1, 16))
    lane = lane - 96 * group
    source = sum((lane >= 5 * m).astype(jnp.int32) for m in range(1, 17))
    field = lane - 5 * source
    valid = jnp.zeros(row_ref.shape, jnp.int32)
    block = jnp.zeros(row_ref.shape, jnp.int32)
    for slot in range(NB):
        here = group == target_ref[slot]
        valid = jnp.where(here, 1, valid)
        block = jnp.where(here, slot, block)
    bound = jnp.zeros(row_ref.shape, jnp.int32)
    for u in range(4):
        bound = jnp.where(field == u + 1, bounds[u], bound)
    bound = jnp.clip(bound - (BLOCK * block - LEFT), 0, WIN)
    value = jnp.where(field == 0, valid, bound)
    row_ref[...] = jnp.where(source == group_ref[0], value, 0).astype(F32)


def places(target_row, group, segment, width):
    return pl.pallas_call(
        places_kernel,
        out_shape=(
            jax.ShapeDtypeStruct((4,), jnp.int32),
            jax.ShapeDtypeStruct((1, width), F32),
        ),
        in_specs=[SMEM_SPEC, SMEM_SPEC, pl.BlockSpec(memory_space=pltpu.VMEM)],
        out_specs=(SMEM_SPEC, pl.BlockSpec(memory_space=pltpu.VMEM)),
        cost_estimate=cost(1),
        name="places",
    )(target_row, group, segment)


def pack_kernel(target_ref, x_ref, out_ref):
    for i in range(4):
        group = 4 * pl.program_id(0) + i
        b = jnp.int32(-1)
        for slot in range(NB):
            b = jnp.where(target_ref[slot] == group, slot, b)

        @pl.when(b >= 0)
        def _():
            before = pl.multiple_of(jnp.maximum(b * BLOCK - LEFT, 0), 16)
            start = pl.multiple_of(b * BLOCK, 16)
            after = pl.multiple_of(jnp.minimum((b + 1) * BLOCK, NB * BLOCK - 16), 16)
            out_ref[i, pl.ds(0, 16), :] = x_ref[pl.ds(before, 16), :]
            out_ref[i, pl.ds(16, 64), :] = x_ref[pl.ds(start, 64), :]
            out_ref[i, pl.ds(80, 16), :] = x_ref[pl.ds(after, 16), :]

        @pl.when(b < 0)
        def _():
            out_ref[i] = jnp.zeros_like(out_ref[i])


def pack(target_row, x):
    rows, width = x.shape
    return pl.pallas_call(
        pack_kernel,
        grid=(4,),
        out_shape=jax.ShapeDtypeStruct((16, WIN, width), BF16),
        in_specs=[SMEM_SPEC, pl.BlockSpec((rows, width), lambda r: (0, 0))],
        out_specs=pl.BlockSpec((4, WIN, width), lambda r: (r, 0, 0)),
        cost_estimate=cost(4),
        compiler_params=pltpu.CompilerParams(vmem_limit_bytes=32 * 1024 * 1024),
        name="pack",
    )(target_row, x)


def stats_kernel(bounds_ref, x_ref, kern_ref, _, out_ref, x_sums_ref, window, taps, sums):
    spread_taps(kern_ref, taps)
    sums[...] = jnp.zeros_like(sums)
    first, second, end = bounds_ref[1], bounds_ref[2], bounds_ref[3]

    frame = lax.broadcasted_iota(jnp.int32, (KER, NB * BLOCK), 1)
    centre = frame - lax.broadcasted_iota(jnp.int32, (KER, NB * BLOCK), 0) + LEFT
    low, high = jnp.minimum(frame, centre), jnp.maximum(frame, centre)
    meets = jnp.zeros((KER, NB * BLOCK), F32)
    for u in range(3):
        meets = jnp.where((low >= bounds_ref[u]) & (high < bounds_ref[u + 1]), 1.0, meets)
    x_sums_ref[...] = jnp.dot(meets.astype(BF16), x_ref[...], preferred_element_type=F32)

    def block(n, carry):
        row = n * BLOCK
        low, high = utterances(first, second, row)

        def part(u, inner):
            begin, stop = bounds_ref[u], bounds_ref[u + 1]
            before = jnp.maximum(row - LEFT, 0)
            after = jnp.minimum(row + BLOCK, NB * BLOCK - 16)
            for source, place, size in ((before, 0, 16), (row, 16, 64), (after, 80, 16)):
                rows = row_iota(size) + (row - LEFT + place)
                keep = (rows >= begin) & (rows < stop)
                for g in range(TILES):
                    x = x_ref[pl.ds(pl.multiple_of(source, 16), size), tile(g)].astype(F32)
                    window[g, pl.ds(place, size), :] = jnp.where(keep, x, 0.0)

            def per_rows(base, n):
                for g in range(TILES):
                    acc = conv_rows(window, taps, g, base, n)
                    total, square = sums[g, pl.ds(0, 8), :], sums[g, pl.ds(8, 8), :]
                    for v in range(n):
                        at = row_of(v, n) + (row + base)
                        h = jnp.where((at >= begin) & (at < stop), acc[v], 0.0)
                        total = total + h
                        square = square + h * h
                    sums[g, pl.ds(0, 8), :] = total
                    sums[g, pl.ds(8, 8), :] = square

            in_rows(low + 1 == high, begin - row, stop - row, per_rows)
            return inner

        return lax.fori_loop(low, high, part, carry)

    lax.fori_loop(0, end // BLOCK, block, 0)
    for g in range(TILES):
        for i in range(2):
            part = sums[g, pl.ds(8 * i, 8), :]
            out_ref[pl.ds(i, 1), tile(g)] = jnp.sum(part, axis=0, keepdims=True)


def stats(bounds, x, kern, earlier):
    width = x.shape[1]
    return pl.pallas_call(
        stats_kernel,
        grid=(width // WIDE,),
        out_shape=(
            jax.ShapeDtypeStruct((2, width), F32),
            jax.ShapeDtypeStruct((KER, width), F32),
        ),
        in_specs=[
            SMEM_SPEC,
            pl.BlockSpec((NB * BLOCK, WIDE), lambda c: (0, c)),
            pl.BlockSpec((KER, WIDE), lambda c: (0, c)),
            pl.BlockSpec(memory_space=pl.ANY),
        ],
        out_specs=(
            pl.BlockSpec((2, WIDE), lambda c: (0, c)),
            pl.BlockSpec((KER, WIDE), lambda c: (0, c)),
        ),
        scratch_shapes=[
            pltpu.VMEM((TILES, WIN, LANES), F32),
            pltpu.VMEM((TILES, 8 * KER, LANES), F32),
            pltpu.VMEM((TILES, 16, LANES), F32),
        ],
        cost_estimate=cost(15),
        name="stats",
    )(bounds, x, kern, earlier)


def live_parts(info_ref, got_ref, window, per_part, per_block=None):
    def slot(s, n):
        valid = info_ref[5 * s] > 0

        @pl.when(valid)
        def _():
            at = pl.multiple_of(n * BLOCK, BLOCK)
            low, high = utterances(info_ref[5 * s + 2], info_ref[5 * s + 3], LEFT)

            def part(u, carry):
                begin, stop = info_ref[5 * s + 1 + u], info_ref[5 * s + 2 + u]
                rows = row_iota(WIN)
                keep = (rows >= begin) & (rows < stop)
                for g in range(TILES):
                    x = got_ref[s, :, tile(g)].astype(F32)
                    window[g] = jnp.where(keep, x, 0.0)
                begin, stop = begin - LEFT, stop - LEFT

                def per_rows(base, groups):
                    per_part(at + base, begin - base, stop - base, base, groups)

                in_rows(low + 1 == high, begin, stop, per_rows)
                return carry

            lax.fori_loop(low, high, part, 0)
            if per_block is not None:
                per_block(at)

        return n + valid.astype(jnp.int32)

    lax.fori_loop(0, 16, slot, 0)


def hidden_kernel(info_ref, got_ref, kern_ref, norm_ref, *rest):
    h_ref, sw_ref, window, taps = rest[-4:]
    spread_taps(kern_ref, taps)

    def per_part(at, begin, stop, base, n):
        for g in range(TILES):
            acc = conv_rows(window, taps, g, base, n)
            for v in range(n):
                place = pl.ds(at + v, 8, stride=n)
                keep = (row_of(v, n) >= begin) & (row_of(v, n) < stop)
                h_ref[g, place, :] = jnp.where(keep, acc[v], h_ref[g, place, :])

    def per_block(at):
        for g in range(TILES):
            mean, inverse = norm_ref[pl.ds(0, 1), tile(g)], norm_ref[pl.ds(1, 1), tile(g)]
            scale, shift = norm_ref[pl.ds(2, 1), tile(g)], norm_ref[pl.ds(3, 1), tile(g)]
            a = (h_ref[g, pl.ds(at, BLOCK), :] - mean) * inverse * scale + shift
            sw_ref[pl.ds(at, BLOCK), tile(g)] = (a * jax.nn.sigmoid(a)).astype(BF16)

    live_parts(info_ref, got_ref, window, per_part, per_block)


def hidden(info, got, kern, norm, *earlier):
    width = got.shape[2]
    rows = BLOCKS * BLOCK
    return pl.pallas_call(
        hidden_kernel,
        grid=(width // WIDE,),
        out_shape=(
            jax.ShapeDtypeStruct((width // LANES, rows, LANES), F32),
            jax.ShapeDtypeStruct((rows, width), BF16),
        ),
        in_specs=[
            SMEM_SPEC,
            pl.BlockSpec((16, WIN, WIDE), lambda c: (0, 0, c)),
            pl.BlockSpec((KER, WIDE), lambda c: (0, c)),
            pl.BlockSpec((4, WIDE), lambda c: (0, c)),
        ]
        + [pl.BlockSpec(memory_space=pl.ANY)] * len(earlier),
        out_specs=(
            pl.BlockSpec((TILES, rows, LANES), lambda c: (c, 0, 0)),
            pl.BlockSpec((rows, WIDE), lambda c: (0, c)),
        ),
        scratch_shapes=[pltpu.VMEM((TILES, WIN, LANES), F32), pltpu.VMEM((TILES, 8 * KER, LANES), F32)],
        cost_estimate=cost(16),
        name="hidden",
    )(info, got, kern, norm, *earlier)


def terms_kernel(
    info_ref, got_ref, h_ref, wide_back, norm_ref, out_ref, window, back_ref, acc_a, acc_x, sums
):
    for g in range(TILES):
        back_ref[g] = wide_back[:, tile(g)]
    acc_a[...] = jnp.zeros_like(acc_a)
    acc_x[...] = jnp.zeros_like(acc_x)
    sums[...] = jnp.zeros_like(sums)

    def per_tile(g, at, begin, stop, base, n):
        mean, inverse = norm_ref[pl.ds(0, 1), tile(g)], norm_ref[pl.ds(1, 1), tile(g)]
        scale, shift = norm_ref[pl.ds(2, 1), tile(g)], norm_ref[pl.ds(3, 1), tile(g)]
        das, hats = [], []
        sum_x, sum_1 = sums[g, pl.ds(0, 8), :], sums[g, pl.ds(8, 8), :]
        for v in range(n):
            place = pl.ds(at + v, 8, stride=n)
            keep = (row_of(v, n) >= begin) & (row_of(v, n) < stop)
            hat = (h_ref[g, place, :] - mean) * inverse
            a = hat * scale + shift
            sig = jax.nn.sigmoid(a)
            da = back_ref[g, place, :] * (sig * (1.0 + a * (1.0 - sig)))
            da = jnp.where(keep, da, 0.0)
            hat = jnp.where(keep, hat, 0.0)
            sum_x = sum_x + da * hat
            sum_1 = sum_1 + da
            das.append(da)
            hats.append(hat)
        sums[g, pl.ds(0, 8), :] = sum_x
        sums[g, pl.ds(8, 8), :] = sum_1
        xs = [shifted(window, g, base + w, n) for w in range(n - 1)]
        for k in range(KER):
            xs.append(shifted(window, g, base + k + n - 1, n))
            place = pl.ds(8 * k, 8)
            for acc, rows in ((acc_a, das), (acc_x, hats)):
                terms_k = [rows[v] * xs[v] for v in range(n)]
                while len(terms_k) > 1:
                    terms_k = [p + q for p, q in zip(terms_k[::2], terms_k[1::2])]
                acc[g, place, :] += terms_k[0]
            xs.pop(0)

    def per_part(at, begin, stop, base, n):
        for g in range(TILES):
            per_tile(g, at, begin, stop, base, n)

    live_parts(info_ref, got_ref, window, per_part)
    for g in range(TILES):
        for acc, first in ((acc_a, 0), (acc_x, KER)):
            rows = acc[g].reshape(KER, 8, LANES)
            out_ref[pl.ds(first, KER), tile(g)] = jnp.sum(rows, axis=1)
        for i in range(2):
            part = sums[g, pl.ds(8 * i, 8), :]
            out_ref[pl.ds(2 * KER + i, 1), tile(g)] = jnp.sum(part, axis=0, keepdims=True)
    out_ref[pl.ds(66, 6), :] = jnp.zeros((6, WIDE), F32)


def terms(info, got, h, back, norm):
    width = got.shape[2]
    return pl.pallas_call(
        terms_kernel,
        grid=(width // WIDE,),
        out_shape=jax.ShapeDtypeStruct((72, width), F32),
        in_specs=[
            SMEM_SPEC,
            pl.BlockSpec((16, WIN, WIDE), lambda c: (0, 0, c)),
            pl.BlockSpec((TILES, BLOCKS * BLOCK, LANES), lambda c: (c, 0, 0)),
            pl.BlockSpec((BLOCKS * BLOCK, WIDE), lambda c: (0, c)),
            pl.BlockSpec((4, WIDE), lambda c: (0, c)),
        ],
        out_specs=pl.BlockSpec((72, WIDE), lambda c: (0, c)),
        scratch_shapes=[
            pltpu.VMEM((TILES, WIN, LANES), F32),
            pltpu.VMEM((TILES, BLOCKS * BLOCK, LANES), F32),
            pltpu.VMEM((TILES, 8 * KER, LANES), F32),
            pltpu.VMEM((TILES, 8 * KER, LANES), F32),
            pltpu.VMEM((TILES, 16, LANES), F32),
        ],
        cost_estimate=cost(25),
        name="terms",
    )(info, got, h, back, norm)


def zero_step(step):
    if step < 4:
        return [(i, i ^ step) for i in range(16)]
    return [(i, (i + step) % 16) for i in range(16)]


def dp_step(step, row):
    if row:
        return [(i, 4 * (i // 4) + (i + step) % 4) for i in range(16)]
    return [(i, (i + 4 * step) % 16) for i in range(16)]


def add_from(x, axis, steps, *meanwhile):
    parts = [lax.ppermute(x, axis, step) for step in steps]
    parts, meanwhile = lax.optimization_barrier((parts, meanwhile))
    return sum(parts, x), meanwhile


def gather_small(x, zero_id, meanwhile):
    for step, first in ((1, zero_id % 2 == 0), (2, (zero_id // 2) % 2 == 0)):
        other = lax.ppermute(x, "zero", zero_step(step))
        other, meanwhile = lax.optimization_barrier((other, meanwhile))
        x = jnp.stack([jnp.where(first, x, other), jnp.where(first, other, x)])
    pairs = [x] + [lax.ppermute(x, "zero", zero_step(step)) for step in (4, 8, 12)]
    place = zero_id // 4
    parts = []
    for q in range(4):
        part = pairs[0]
        for s in range(1, 4):
            part = jnp.where((place - s) % 4 == q, pairs[s], part)
        parts.append(part)
    return jnp.stack(parts).reshape((16,) + x.shape[2:])


def per_device(frames, segments, targets, cotangent, w_out, kernel, norm_params):
    x, seg, target_row, cot = frames[0, 0], segments[0, 0], targets[0, 0], cotangent[0, 0]
    width = x.shape[1]
    share = width // 16
    zero_id = lax.axis_index("zero")
    core = lax.rem(zero_id, 2)

    bounds, info = places(
        target_row, lax.axis_index("dp").reshape(1), seg.reshape(NB // 2, 2 * BLOCK), width
    )
    send = pack(target_row, x)
    small = jnp.concatenate([kernel, norm_params, jnp.zeros((14, share), BF16)], axis=0)
    got = lax.all_to_all(send, "dp", 0, 0, tiled=True)
    small_full = gather_small(small, zero_id, send)
    small_full = jnp.transpose(small_full, (1, 0, 2)).reshape(48, width).astype(F32)
    kern_full = small_full[:KER]

    w_t = lax.all_gather(w_out.T, "zero", axis=0, tiled=True)

    half = width // 2
    column = lax.broadcasted_iota(jnp.int32, (width, half), 0)
    place = lax.broadcasted_iota(jnp.int32, (width, half), 1)
    even = column == place + share * (place // share)
    odd = column == place + share * (place // share) + share
    own_columns = jnp.where(core == 0, even, odd).astype(BF16)
    other_columns = jnp.where(core == 0, odd, even).astype(BF16)
    swap = [(i, i ^ 1) for i in range(16)]

    sums, x_sums = stats(bounds, x, kern_full, send)
    for steps in ((1,), (2,), (4, 8, 12)):
        sums, _ = add_from(sums, "zero", [zero_step(step) for step in steps])
    sums = jnp.concatenate([sums, info], axis=0)
    sums, cot = lax.optimization_barrier((sums, cot))
    cot_own = jnp.dot(cot, own_columns, preferred_element_type=F32).astype(BF16)
    cot_send = jnp.dot(cot, other_columns, preferred_element_type=F32).astype(BF16)
    back = jnp.dot(cot, w_t, preferred_element_type=F32)
    sums, (back, cot_own, cot_send) = add_from(
        sums, "dp", [dp_step(step, True) for step in (1, 2, 3)], back, cot_own, cot_send
    )
    cot_other = lax.ppermute(cot_send, "zero", swap)
    sums, _ = add_from(sums, "dp", [dp_step(step, False) for step in (1, 2, 3)])
    info = lax.dynamic_slice_in_dim(sums[2], lax.axis_index("dp") * 96, 80, 0).astype(jnp.int32)
    frame_count = jnp.float32(BLOCKS * BLOCK * 256)
    mean = sums[0] / frame_count
    var = sums[1] / frame_count - mean * mean
    inverse = lax.rsqrt(var + EPS)
    norm = jnp.stack([mean, inverse, small_full[KER], small_full[KER + 1]])

    h, sw = hidden(info, got, kern_full, norm, back, cot_other)
    sw_other = lax.ppermute(sw, "zero", swap)
    contract = (((0,), (0,)), ((), ()))
    term = lax.dot_general(sw, cot_own, contract, preferred_element_type=F32)
    sw_other, term = lax.optimization_barrier((sw_other, term))
    term = term + lax.dot_general(sw_other, cot_other, contract, preferred_element_type=F32)
    term = term.astype(BF16).reshape(16, share, half)
    term = lax.all_to_all(term, "dp", 0, 0, tiled=True)

    grads = terms(info, got, h, back, norm)
    out = lax.dot_general(
        sw, w_t, (((1,), (1,)), ((), ())), preferred_element_type=F32
    ).astype(BF16)

    grads = jnp.concatenate([grads, x_sums], axis=0).reshape(104, 8, 2, share)
    grads = jnp.transpose(grads, (2, 1, 0, 3))
    grads_other = lax.ppermute(
        lax.dynamic_index_in_dim(grads, 1 - core, 0, False), "zero", swap
    )
    grads = lax.dynamic_index_in_dim(grads, core, 0, False) + grads_other

    term = jnp.sum(term.astype(F32), axis=0).reshape(share, 8, share)
    both = jnp.concatenate([jnp.transpose(term, (1, 0, 2)), grads], axis=1)
    both = lax.all_to_all(
        both,
        "zero",
        0,
        0,
        axis_index_groups=[[i for i in range(16) if i % 2 == c] for c in range(2)],
        tiled=True,
    )
    last = jnp.sum(both, axis=0)
    last = lax.all_to_all(
        jnp.broadcast_to(last[None], (16,) + last.shape), "dp", 0, 0, tiled=True
    )
    part_w = last[:, :share].reshape(width, share)
    grads = jnp.sum(last[:, share:], axis=0)

    own = lax.dynamic_slice_in_dim(norm, zero_id * share, share, 1)
    da_x, hat_x, x_k = grads[:KER], grads[KER : 2 * KER], grads[72 : 72 + KER]
    sum_x, sum_1 = grads[64], grads[65]
    part_k = (own[2] * own[1]) * (da_x - (sum_1 / frame_count) * x_k - (sum_x / frame_count) * hat_x)
    return out[None, None], part_w, part_k, jnp.stack([sum_x, sum_1])


def solution(mesh):
    return jax.shard_map(
        per_device,
        mesh=mesh,
        in_specs=(
            P("dp", "zero", None, None),
            P("dp", "zero", None),
            P("dp", "zero", None),
            P("dp", "zero", None, None),
            P(None, "zero"),
            P(None, "zero"),
            P(None, "zero"),
        ),
        out_specs=(P("dp", "zero", None, None), P(None, "zero"), P(None, "zero"), P(None, "zero")),
        check_vma=False,
    )
```

```python
import jax
import jax.numpy as jnp
from jax import lax
from jax.experimental import pallas as pl
from jax.experimental.pallas import tpu as pltpu
from jax.sharding import PartitionSpec as P

KER = 32
BLOCK = 64
BLOCKS = 8
NB = 12
LEFT = 16
WIN = 96
LANES = 128
TILES = 4
WIDE = TILES * LANES
EPS = 1e-05
F32 = jnp.float32
BF16 = jnp.bfloat16
SMEM_SPEC = pl.BlockSpec(memory_space=pltpu.SMEM)


def cost(microseconds):
    return pl.CostEstimate(
        flops=microseconds * 1_100_000_000, bytes_accessed=1_000_000, transcendentals=0
    )


def row_iota(rows):
    return lax.broadcasted_iota(jnp.int32, (rows, LANES), 0)


def tile(g):
    return pl.ds(LANES * g, LANES)


def spread_taps(kern_ref, taps):
    for g in range(TILES):
        for k in range(KER):
            row = kern_ref[pl.ds(k, 1), tile(g)]
            taps[g, pl.ds(8 * k, 8), :] = jnp.broadcast_to(row, (8, LANES))


def row_of(v, n):
    return n * row_iota(8) + v


def shifted(window, g, w, n):
    return window[g, pl.ds(w, 8, stride=n), :]


def conv_rows(window, taps, g, base, n):
    xs = [shifted(window, g, base + w, n) for w in range(n - 1)]
    acc = [None] * n
    for k in range(KER):
        xs.append(shifted(window, g, base + k + n - 1, n))
        tap = taps[g, pl.ds(8 * k, 8), :]
        for v in range(n):
            acc[v] = tap * xs[v] if k == 0 else acc[v] + tap * xs[v]
        xs.pop(0)
    return acc


def in_rows(alone, begin, stop, per_rows):
    @pl.when(alone)
    def _():
        per_rows(0, 8)

    for base in (0, BLOCK // 2):
        meets = (begin < base + BLOCK // 2) & (stop > base)

        @pl.when(jnp.logical_not(alone) & meets)
        def _():
            per_rows(base, 4)


def utterances(first, second, row):
    low = (first <= row).astype(jnp.int32) + (second <= row).astype(jnp.int32)
    top = row + BLOCK - 1
    high = (first <= top).astype(jnp.int32) + (second <= top).astype(jnp.int32)
    return low, high + 1


def places_kernel(target_ref, group_ref, segment_ref, bounds_ref, row_ref):
    live = jnp.int32(0)
    for slot in range(NB):
        live = live + (target_ref[slot] >= 0).astype(jnp.int32)
    segment = segment_ref[...]
    bounds = [jnp.int32(0)]
    for u in (1, 2):
        bounds.append(jnp.minimum(jnp.sum((segment < u).astype(jnp.int32)), BLOCK * live))
    bounds.append(BLOCK * live)
    for u in range(4):
        bounds_ref[u] = bounds[u]

    lane = lax.broadcasted_iota(jnp.int32, row_ref.shape, 1)
    group = sum((lane >= 96 * m).astype(jnp.int32) for m in range(1, 16))
    lane = lane - 96 * group
    source = sum((lane >= 5 * m).astype(jnp.int32) for m in range(1, 17))
    field = lane - 5 * source
    valid = jnp.zeros(row_ref.shape, jnp.int32)
    block = jnp.zeros(row_ref.shape, jnp.int32)
    for slot in range(NB):
        here = group == target_ref[slot]
        valid = jnp.where(here, 1, valid)
        block = jnp.where(here, slot, block)
    bound = jnp.zeros(row_ref.shape, jnp.int32)
    for u in range(4):
        bound = jnp.where(field == u + 1, bounds[u], bound)
    bound = jnp.clip(bound - (BLOCK * block - LEFT), 0, WIN)
    value = jnp.where(field == 0, valid, bound)
    row_ref[...] = jnp.where(source == group_ref[0], value, 0).astype(F32)


def places(target_row, group, segment, width):
    return pl.pallas_call(
        places_kernel,
        out_shape=(
            jax.ShapeDtypeStruct((4,), jnp.int32),
            jax.ShapeDtypeStruct((1, width), F32),
        ),
        in_specs=[SMEM_SPEC, SMEM_SPEC, pl.BlockSpec(memory_space=pltpu.VMEM)],
        out_specs=(SMEM_SPEC, pl.BlockSpec(memory_space=pltpu.VMEM)),
        cost_estimate=cost(1),
        name="places",
    )(target_row, group, segment)


def pack_kernel(target_ref, x_ref, out_ref):
    for i in range(4):
        group = 4 * pl.program_id(0) + i
        b = jnp.int32(-1)
        for slot in range(NB):
            b = jnp.where(target_ref[slot] == group, slot, b)

        @pl.when(b >= 0)
        def _():
            before = pl.multiple_of(jnp.maximum(b * BLOCK - LEFT, 0), 16)
            start = pl.multiple_of(b * BLOCK, 16)
            after = pl.multiple_of(jnp.minimum((b + 1) * BLOCK, NB * BLOCK - 16), 16)
            out_ref[i, pl.ds(0, 16), :] = x_ref[pl.ds(before, 16), :]
            out_ref[i, pl.ds(16, 64), :] = x_ref[pl.ds(start, 64), :]
            out_ref[i, pl.ds(80, 16), :] = x_ref[pl.ds(after, 16), :]

        @pl.when(b < 0)
        def _():
            out_ref[i] = jnp.zeros_like(out_ref[i])


def pack(target_row, x):
    rows, width = x.shape
    return pl.pallas_call(
        pack_kernel,
        grid=(4,),
        out_shape=jax.ShapeDtypeStruct((16, WIN, width), BF16),
        in_specs=[SMEM_SPEC, pl.BlockSpec((rows, width), lambda r: (0, 0))],
        out_specs=pl.BlockSpec((4, WIN, width), lambda r: (r, 0, 0)),
        cost_estimate=cost(4),
        compiler_params=pltpu.CompilerParams(vmem_limit_bytes=32 * 1024 * 1024),
        name="pack",
    )(target_row, x)


def stats_kernel(bounds_ref, x_ref, kern_ref, _, out_ref, x_sums_ref, window, taps, sums):
    spread_taps(kern_ref, taps)
    sums[...] = jnp.zeros_like(sums)
    first, second, end = bounds_ref[1], bounds_ref[2], bounds_ref[3]

    frame = lax.broadcasted_iota(jnp.int32, (KER, NB * BLOCK), 1)
    centre = frame - lax.broadcasted_iota(jnp.int32, (KER, NB * BLOCK), 0) + LEFT
    low, high = jnp.minimum(frame, centre), jnp.maximum(frame, centre)
    meets = jnp.zeros((KER, NB * BLOCK), F32)
    for u in range(3):
        meets = jnp.where((low >= bounds_ref[u]) & (high < bounds_ref[u + 1]), 1.0, meets)
    x_sums_ref[...] = jnp.dot(meets.astype(BF16), x_ref[...], preferred_element_type=F32)

    def block(n, carry):
        row = n * BLOCK
        low, high = utterances(first, second, row)

        def part(u, inner):
            begin, stop = bounds_ref[u], bounds_ref[u + 1]
            before = jnp.maximum(row - LEFT, 0)
            after = jnp.minimum(row + BLOCK, NB * BLOCK - 16)
            for source, place, size in ((before, 0, 16), (row, 16, 64), (after, 80, 16)):
                rows = row_iota(size) + (row - LEFT + place)
                keep = (rows >= begin) & (rows < stop)
                for g in range(TILES):
                    x = x_ref[pl.ds(pl.multiple_of(source, 16), size), tile(g)].astype(F32)
                    window[g, pl.ds(place, size), :] = jnp.where(keep, x, 0.0)

            def per_rows(base, n):
                for g in range(TILES):
                    acc = conv_rows(window, taps, g, base, n)
                    total, square = sums[g, pl.ds(0, 8), :], sums[g, pl.ds(8, 8), :]
                    for v in range(n):
                        at = row_of(v, n) + (row + base)
                        h = jnp.where((at >= begin) & (at < stop), acc[v], 0.0)
                        total = total + h
                        square = square + h * h
                    sums[g, pl.ds(0, 8), :] = total
                    sums[g, pl.ds(8, 8), :] = square

            in_rows(low + 1 == high, begin - row, stop - row, per_rows)
            return inner

        return lax.fori_loop(low, high, part, carry)

    lax.fori_loop(0, end // BLOCK, block, 0)
    for g in range(TILES):
        for i in range(2):
            part = sums[g, pl.ds(8 * i, 8), :]
            out_ref[pl.ds(i, 1), tile(g)] = jnp.sum(part, axis=0, keepdims=True)


def stats(bounds, x, kern, earlier):
    width = x.shape[1]
    return pl.pallas_call(
        stats_kernel,
        grid=(width // WIDE,),
        out_shape=(
            jax.ShapeDtypeStruct((2, width), F32),
            jax.ShapeDtypeStruct((KER, width), F32),
        ),
        in_specs=[
            SMEM_SPEC,
            pl.BlockSpec((NB * BLOCK, WIDE), lambda c: (0, c)),
            pl.BlockSpec((KER, WIDE), lambda c: (0, c)),
            pl.BlockSpec(memory_space=pl.ANY),
        ],
        out_specs=(
            pl.BlockSpec((2, WIDE), lambda c: (0, c)),
            pl.BlockSpec((KER, WIDE), lambda c: (0, c)),
        ),
        scratch_shapes=[
            pltpu.VMEM((TILES, WIN, LANES), F32),
            pltpu.VMEM((TILES, 8 * KER, LANES), F32),
            pltpu.VMEM((TILES, 16, LANES), F32),
        ],
        cost_estimate=cost(15),
        name="stats",
    )(bounds, x, kern, earlier)


def live_parts(info_ref, got_ref, window, per_part, per_block=None):
    def slot(s, n):
        valid = info_ref[5 * s] > 0

        @pl.when(valid)
        def _():
            at = pl.multiple_of(n * BLOCK, BLOCK)
            low, high = utterances(info_ref[5 * s + 2], info_ref[5 * s + 3], LEFT)

            def part(u, carry):
                begin, stop = info_ref[5 * s + 1 + u], info_ref[5 * s + 2 + u]
                rows = row_iota(WIN)
                keep = (rows >= begin) & (rows < stop)
                for g in range(TILES):
                    x = got_ref[s, :, tile(g)].astype(F32)
                    window[g] = jnp.where(keep, x, 0.0)
                begin, stop = begin - LEFT, stop - LEFT

                def per_rows(base, groups):
                    per_part(at + base, begin - base, stop - base, base, groups)

                in_rows(low + 1 == high, begin, stop, per_rows)
                return carry

            lax.fori_loop(low, high, part, 0)
            if per_block is not None:
                per_block(at)

        return n + valid.astype(jnp.int32)

    lax.fori_loop(0, 16, slot, 0)


def hidden_kernel(info_ref, got_ref, kern_ref, norm_ref, *rest):
    h_ref, sw_ref, window, taps = rest[-4:]
    spread_taps(kern_ref, taps)

    def per_part(at, begin, stop, base, n):
        for g in range(TILES):
            acc = conv_rows(window, taps, g, base, n)
            for v in range(n):
                place = pl.ds(at + v, 8, stride=n)
                keep = (row_of(v, n) >= begin) & (row_of(v, n) < stop)
                h_ref[g, place, :] = jnp.where(keep, acc[v], h_ref[g, place, :])

    def per_block(at):
        for g in range(TILES):
            mean, inverse = norm_ref[pl.ds(0, 1), tile(g)], norm_ref[pl.ds(1, 1), tile(g)]
            scale, shift = norm_ref[pl.ds(2, 1), tile(g)], norm_ref[pl.ds(3, 1), tile(g)]
            a = (h_ref[g, pl.ds(at, BLOCK), :] - mean) * inverse * scale + shift
            sw_ref[pl.ds(at, BLOCK), tile(g)] = (a * jax.nn.sigmoid(a)).astype(BF16)

    live_parts(info_ref, got_ref, window, per_part, per_block)


def hidden(info, got, kern, norm, *earlier):
    width = got.shape[2]
    rows = BLOCKS * BLOCK
    return pl.pallas_call(
        hidden_kernel,
        grid=(width // WIDE,),
        out_shape=(
            jax.ShapeDtypeStruct((width // LANES, rows, LANES), F32),
            jax.ShapeDtypeStruct((rows, width), BF16),
        ),
        in_specs=[
            SMEM_SPEC,
            pl.BlockSpec((16, WIN, WIDE), lambda c: (0, 0, c)),
            pl.BlockSpec((KER, WIDE), lambda c: (0, c)),
            pl.BlockSpec((4, WIDE), lambda c: (0, c)),
        ]
        + [pl.BlockSpec(memory_space=pl.ANY)] * len(earlier),
        out_specs=(
            pl.BlockSpec((TILES, rows, LANES), lambda c: (c, 0, 0)),
            pl.BlockSpec((rows, WIDE), lambda c: (0, c)),
        ),
        scratch_shapes=[pltpu.VMEM((TILES, WIN, LANES), F32), pltpu.VMEM((TILES, 8 * KER, LANES), F32)],
        cost_estimate=cost(16),
        name="hidden",
    )(info, got, kern, norm, *earlier)


def terms_kernel(
    info_ref, got_ref, h_ref, wide_back, norm_ref, out_ref, window, back_ref, acc_a, acc_x, sums
):
    for g in range(TILES):
        back_ref[g] = wide_back[:, tile(g)]
    acc_a[...] = jnp.zeros_like(acc_a)
    acc_x[...] = jnp.zeros_like(acc_x)
    sums[...] = jnp.zeros_like(sums)

    def per_tile(g, at, begin, stop, base, n):
        mean, inverse = norm_ref[pl.ds(0, 1), tile(g)], norm_ref[pl.ds(1, 1), tile(g)]
        scale, shift = norm_ref[pl.ds(2, 1), tile(g)], norm_ref[pl.ds(3, 1), tile(g)]
        das, hats = [], []
        sum_x, sum_1 = sums[g, pl.ds(0, 8), :], sums[g, pl.ds(8, 8), :]
        for v in range(n):
            place = pl.ds(at + v, 8, stride=n)
            keep = (row_of(v, n) >= begin) & (row_of(v, n) < stop)
            hat = (h_ref[g, place, :] - mean) * inverse
            a = hat * scale + shift
            sig = jax.nn.sigmoid(a)
            da = back_ref[g, place, :] * (sig * (1.0 + a * (1.0 - sig)))
            da = jnp.where(keep, da, 0.0)
            hat = jnp.where(keep, hat, 0.0)
            sum_x = sum_x + da * hat
            sum_1 = sum_1 + da
            das.append(da)
            hats.append(hat)
        sums[g, pl.ds(0, 8), :] = sum_x
        sums[g, pl.ds(8, 8), :] = sum_1
        xs = [shifted(window, g, base + w, n) for w in range(n - 1)]
        for k in range(KER):
            xs.append(shifted(window, g, base + k + n - 1, n))
            place = pl.ds(8 * k, 8)
            for acc, rows in ((acc_a, das), (acc_x, hats)):
                terms_k = [rows[v] * xs[v] for v in range(n)]
                while len(terms_k) > 1:
                    terms_k = [p + q for p, q in zip(terms_k[::2], terms_k[1::2])]
                acc[g, place, :] += terms_k[0]
            xs.pop(0)

    def per_part(at, begin, stop, base, n):
        for g in range(TILES):
            per_tile(g, at, begin, stop, base, n)

    live_parts(info_ref, got_ref, window, per_part)
    for g in range(TILES):
        for acc, first in ((acc_a, 0), (acc_x, KER)):
            rows = acc[g].reshape(KER, 8, LANES)
            out_ref[pl.ds(first, KER), tile(g)] = jnp.sum(rows, axis=1)
        for i in range(2):
            part = sums[g, pl.ds(8 * i, 8), :]
            out_ref[pl.ds(2 * KER + i, 1), tile(g)] = jnp.sum(part, axis=0, keepdims=True)
    out_ref[pl.ds(66, 6), :] = jnp.zeros((6, WIDE), F32)


def terms(info, got, h, back, norm):
    width = got.shape[2]
    return pl.pallas_call(
        terms_kernel,
        grid=(width // WIDE,),
        out_shape=jax.ShapeDtypeStruct((72, width), F32),
        in_specs=[
            SMEM_SPEC,
            pl.BlockSpec((16, WIN, WIDE), lambda c: (0, 0, c)),
            pl.BlockSpec((TILES, BLOCKS * BLOCK, LANES), lambda c: (c, 0, 0)),
            pl.BlockSpec((BLOCKS * BLOCK, WIDE), lambda c: (0, c)),
            pl.BlockSpec((4, WIDE), lambda c: (0, c)),
        ],
        out_specs=pl.BlockSpec((72, WIDE), lambda c: (0, c)),
        scratch_shapes=[
            pltpu.VMEM((TILES, WIN, LANES), F32),
            pltpu.VMEM((TILES, BLOCKS * BLOCK, LANES), F32),
            pltpu.VMEM((TILES, 8 * KER, LANES), F32),
            pltpu.VMEM((TILES, 8 * KER, LANES), F32),
            pltpu.VMEM((TILES, 16, LANES), F32),
        ],
        cost_estimate=cost(25),
        name="terms",
    )(info, got, h, back, norm)


def zero_step(step):
    if step < 4:
        return [(i, i ^ step) for i in range(16)]
    return [(i, (i + step) % 16) for i in range(16)]


def dp_step(step, row):
    if row:
        return [(i, 4 * (i // 4) + (i + step) % 4) for i in range(16)]
    return [(i, (i + 4 * step) % 16) for i in range(16)]


def add_from(x, axis, steps, *meanwhile):
    parts = [lax.ppermute(x, axis, step) for step in steps]
    parts, meanwhile = lax.optimization_barrier((parts, meanwhile))
    return sum(parts, x), meanwhile


def gather_small(x, zero_id, meanwhile):
    for step, first in ((1, zero_id % 2 == 0), (2, (zero_id // 2) % 2 == 0)):
        other = lax.ppermute(x, "zero", zero_step(step))
        other, meanwhile = lax.optimization_barrier((other, meanwhile))
        x = jnp.stack([jnp.where(first, x, other), jnp.where(first, other, x)])
    pairs = [x] + [lax.ppermute(x, "zero", zero_step(step)) for step in (4, 8, 12)]
    place = zero_id // 4
    parts = []
    for q in range(4):
        part = pairs[0]
        for s in range(1, 4):
            part = jnp.where((place - s) % 4 == q, pairs[s], part)
        parts.append(part)
    return jnp.stack(parts).reshape((16,) + x.shape[2:])


def per_device(frames, segments, targets, cotangent, w_out, kernel, norm_params):
    x, seg, target_row, cot = frames[0, 0], segments[0, 0], targets[0, 0], cotangent[0, 0]
    width = x.shape[1]
    share = width // 16
    zero_id = lax.axis_index("zero")
    core = lax.rem(zero_id, 2)

    bounds, info = places(
        target_row, lax.axis_index("dp").reshape(1), seg.reshape(NB // 2, 2 * BLOCK), width
    )
    send = pack(target_row, x)
    small = jnp.concatenate([kernel, norm_params, jnp.zeros((14, share), BF16)], axis=0)
    got = lax.all_to_all(send, "dp", 0, 0, tiled=True)
    small_full = gather_small(small, zero_id, send)
    small_full = jnp.transpose(small_full, (1, 0, 2)).reshape(48, width).astype(F32)
    kern_full = small_full[:KER]

    w_t = lax.all_gather(w_out.T, "zero", axis=0, tiled=True)

    half = width // 2
    column = lax.broadcasted_iota(jnp.int32, (width, half), 0)
    place = lax.broadcasted_iota(jnp.int32, (width, half), 1)
    even = column == place + share * (place // share)
    odd = column == place + share * (place // share) + share
    own_columns = jnp.where(core == 0, even, odd).astype(BF16)
    other_columns = jnp.where(core == 0, odd, even).astype(BF16)
    swap = [(i, i ^ 1) for i in range(16)]

    sums, x_sums = stats(bounds, x, kern_full, send)
    for steps in ((1,), (2,), (4, 8, 12)):
        sums, _ = add_from(sums, "zero", [zero_step(step) for step in steps])
    sums = jnp.concatenate([sums, info], axis=0)
    sums, cot = lax.optimization_barrier((sums, cot))
    cot_own = jnp.dot(cot, own_columns, preferred_element_type=F32).astype(BF16)
    cot_send = jnp.dot(cot, other_columns, preferred_element_type=F32).astype(BF16)
    back = jnp.dot(cot, w_t, preferred_element_type=F32)
    sums, (back, cot_own, cot_send) = add_from(
        sums, "dp", [dp_step(step, True) for step in (1, 2, 3)], back, cot_own, cot_send
    )
    cot_other = lax.ppermute(cot_send, "zero", swap)
    sums, _ = add_from(sums, "dp", [dp_step(step, False) for step in (1, 2, 3)])
    info = lax.dynamic_slice_in_dim(sums[2], lax.axis_index("dp") * 96, 80, 0).astype(jnp.int32)
    frame_count = jnp.float32(BLOCKS * BLOCK * 256)
    mean = sums[0] / frame_count
    var = sums[1] / frame_count - mean * mean
    inverse = lax.rsqrt(var + EPS)
    norm = jnp.stack([mean, inverse, small_full[KER], small_full[KER + 1]])

    h, sw = hidden(info, got, kern_full, norm, back, cot_other)
    sw_other = lax.ppermute(sw, "zero", swap)
    contract = (((0,), (0,)), ((), ()))
    term = lax.dot_general(sw, cot_own, contract, preferred_element_type=F32)
    sw_other, term = lax.optimization_barrier((sw_other, term))
    term = term + lax.dot_general(sw_other, cot_other, contract, preferred_element_type=F32)
    term = term.astype(BF16).reshape(16, share, half)
    term = lax.all_to_all(term, "dp", 0, 0, tiled=True)

    grads = terms(info, got, h, back, norm)
    out = lax.dot_general(
        sw, w_t, (((1,), (1,)), ((), ())), preferred_element_type=F32
    ).astype(BF16)

    grads = jnp.concatenate([grads, x_sums], axis=0).reshape(104, 8, 2, share)
    grads = jnp.transpose(grads, (2, 1, 0, 3))
    grads_other = lax.ppermute(
        lax.dynamic_index_in_dim(grads, 1 - core, 0, False), "zero", swap
    )
    grads = lax.dynamic_index_in_dim(grads, core, 0, False) + grads_other

    term = jnp.sum(term.astype(F32), axis=0).reshape(share, 8, share)
    both = jnp.concatenate([jnp.transpose(term, (1, 0, 2)), grads], axis=1).reshape(8, 150, LANES)
    both = lax.all_to_all(
        both,
        "zero",
        0,
        0,
        axis_index_groups=[[i for i in range(16) if i % 2 == c] for c in range(2)],
        tiled=True,
    )
    last = jnp.sum(both, axis=0)
    last = lax.all_to_all(
        jnp.broadcast_to(last[None], (16,) + last.shape), "dp", 0, 0, tiled=True
    )
    part_w = last[:, :72].reshape(width, share)
    grads = jnp.sum(last[:, 72:], axis=0).reshape(104, share)

    own = lax.dynamic_slice_in_dim(norm, zero_id * share, share, 1)
    da_x, hat_x, x_k = grads[:KER], grads[KER : 2 * KER], grads[72 : 72 + KER]
    sum_x, sum_1 = grads[64], grads[65]
    part_k = (own[2] * own[1]) * (da_x - (sum_1 / frame_count) * x_k - (sum_x / frame_count) * hat_x)
    return out[None, None], part_w, part_k, jnp.stack([sum_x, sum_1])


def solution(mesh):
    return jax.shard_map(
        per_device,
        mesh=mesh,
        in_specs=(
            P("dp", "zero", None, None),
            P("dp", "zero", None),
            P("dp", "zero", None),
            P("dp", "zero", None, None),
            P(None, "zero"),
            P(None, "zero"),
            P(None, "zero"),
        ),
        out_specs=(P("dp", "zero", None, None), P(None, "zero"), P(None, "zero"), P(None, "zero")),
        check_vma=False,
    )
```

```python
import jax
import jax.numpy as jnp
from jax import lax
from jax.experimental import pallas as pl
from jax.experimental.pallas import tpu as pltpu
from jax.sharding import PartitionSpec as P

KER = 32
BLOCK = 64
BLOCKS = 8
NB = 12
LEFT = 16
WIN = 96
LANES = 128
TILES = 4
WIDE = TILES * LANES
EPS = 1e-05
F32 = jnp.float32
BF16 = jnp.bfloat16
SMEM_SPEC = pl.BlockSpec(memory_space=pltpu.SMEM)


def cost(microseconds):
    return pl.CostEstimate(
        flops=microseconds * 1_100_000_000, bytes_accessed=1_000_000, transcendentals=0
    )


def row_iota(rows):
    return lax.broadcasted_iota(jnp.int32, (rows, LANES), 0)


def tile(g):
    return pl.ds(LANES * g, LANES)


def spread_taps(kern_ref, taps):
    for g in range(TILES):
        for k in range(KER):
            row = kern_ref[pl.ds(k, 1), tile(g)]
            taps[g, pl.ds(8 * k, 8), :] = jnp.broadcast_to(row, (8, LANES))


def row_of(v, n):
    return n * row_iota(8) + v


def shifted(window, g, w, n):
    return window[g, pl.ds(w, 8, stride=n), :]


def conv_rows(window, taps, g, base, n):
    xs = [shifted(window, g, base + w, n) for w in range(n - 1)]
    acc = [None] * n
    for k in range(KER):
        xs.append(shifted(window, g, base + k + n - 1, n))
        tap = taps[g, pl.ds(8 * k, 8), :]
        for v in range(n):
            acc[v] = tap * xs[v] if k == 0 else acc[v] + tap * xs[v]
        xs.pop(0)
    return acc


def in_rows(alone, begin, stop, per_rows):
    @pl.when(alone)
    def _():
        per_rows(0, 8)

    for base in (0, BLOCK // 2):
        meets = (begin < base + BLOCK // 2) & (stop > base)

        @pl.when(jnp.logical_not(alone) & meets)
        def _():
            per_rows(base, 4)


def utterances(first, second, row):
    low = (first <= row).astype(jnp.int32) + (second <= row).astype(jnp.int32)
    top = row + BLOCK - 1
    high = (first <= top).astype(jnp.int32) + (second <= top).astype(jnp.int32)
    return low, high + 1


def places_kernel(target_ref, group_ref, segment_ref, bounds_ref, row_ref):
    live = jnp.int32(0)
    for slot in range(NB):
        live = live + (target_ref[slot] >= 0).astype(jnp.int32)
    segment = segment_ref[...]
    bounds = [jnp.int32(0)]
    for u in (1, 2):
        bounds.append(jnp.minimum(jnp.sum((segment < u).astype(jnp.int32)), BLOCK * live))
    bounds.append(BLOCK * live)
    for u in range(4):
        bounds_ref[u] = bounds[u]

    lane = lax.broadcasted_iota(jnp.int32, row_ref.shape, 1)
    group = sum((lane >= 96 * m).astype(jnp.int32) for m in range(1, 16))
    lane = lane - 96 * group
    source = sum((lane >= 5 * m).astype(jnp.int32) for m in range(1, 17))
    field = lane - 5 * source
    valid = jnp.zeros(row_ref.shape, jnp.int32)
    block = jnp.zeros(row_ref.shape, jnp.int32)
    for slot in range(NB):
        here = group == target_ref[slot]
        valid = jnp.where(here, 1, valid)
        block = jnp.where(here, slot, block)
    bound = jnp.zeros(row_ref.shape, jnp.int32)
    for u in range(4):
        bound = jnp.where(field == u + 1, bounds[u], bound)
    bound = jnp.clip(bound - (BLOCK * block - LEFT), 0, WIN)
    value = jnp.where(field == 0, valid, bound)
    row_ref[...] = jnp.where(source == group_ref[0], value, 0).astype(F32)


def places(target_row, group, segment, width):
    return pl.pallas_call(
        places_kernel,
        out_shape=(
            jax.ShapeDtypeStruct((4,), jnp.int32),
            jax.ShapeDtypeStruct((1, width), F32),
        ),
        in_specs=[SMEM_SPEC, SMEM_SPEC, pl.BlockSpec(memory_space=pltpu.VMEM)],
        out_specs=(SMEM_SPEC, pl.BlockSpec(memory_space=pltpu.VMEM)),
        cost_estimate=cost(1),
        name="places",
    )(target_row, group, segment)


def pack_kernel(target_ref, x_ref, out_ref):
    for i in range(4):
        group = 4 * pl.program_id(0) + i
        b = jnp.int32(-1)
        for slot in range(NB):
            b = jnp.where(target_ref[slot] == group, slot, b)

        @pl.when(b >= 0)
        def _():
            before = pl.multiple_of(jnp.maximum(b * BLOCK - LEFT, 0), 16)
            start = pl.multiple_of(b * BLOCK, 16)
            after = pl.multiple_of(jnp.minimum((b + 1) * BLOCK, NB * BLOCK - 16), 16)
            out_ref[i, pl.ds(0, 16), :] = x_ref[pl.ds(before, 16), :]
            out_ref[i, pl.ds(16, 64), :] = x_ref[pl.ds(start, 64), :]
            out_ref[i, pl.ds(80, 16), :] = x_ref[pl.ds(after, 16), :]

        @pl.when(b < 0)
        def _():
            out_ref[i] = jnp.zeros_like(out_ref[i])


def pack(target_row, x):
    rows, width = x.shape
    return pl.pallas_call(
        pack_kernel,
        grid=(4,),
        out_shape=jax.ShapeDtypeStruct((16, WIN, width), BF16),
        in_specs=[SMEM_SPEC, pl.BlockSpec((rows, width), lambda r: (0, 0))],
        out_specs=pl.BlockSpec((4, WIN, width), lambda r: (r, 0, 0)),
        cost_estimate=cost(4),
        compiler_params=pltpu.CompilerParams(vmem_limit_bytes=32 * 1024 * 1024),
        name="pack",
    )(target_row, x)


def stats_kernel(bounds_ref, x_ref, kern_ref, _, out_ref, x_sums_ref, window, taps, sums):
    spread_taps(kern_ref, taps)
    sums[...] = jnp.zeros_like(sums)
    first, second, end = bounds_ref[1], bounds_ref[2], bounds_ref[3]

    frame = lax.broadcasted_iota(jnp.int32, (KER, NB * BLOCK), 1)
    centre = frame - lax.broadcasted_iota(jnp.int32, (KER, NB * BLOCK), 0) + LEFT
    low, high = jnp.minimum(frame, centre), jnp.maximum(frame, centre)
    meets = jnp.zeros((KER, NB * BLOCK), F32)
    for u in range(3):
        meets = jnp.where((low >= bounds_ref[u]) & (high < bounds_ref[u + 1]), 1.0, meets)
    x_sums_ref[...] = jnp.dot(meets.astype(BF16), x_ref[...], preferred_element_type=F32)

    def block(n, carry):
        row = n * BLOCK
        low, high = utterances(first, second, row)

        def part(u, inner):
            begin, stop = bounds_ref[u], bounds_ref[u + 1]
            before = jnp.maximum(row - LEFT, 0)
            after = jnp.minimum(row + BLOCK, NB * BLOCK - 16)
            for source, place, size in ((before, 0, 16), (row, 16, 64), (after, 80, 16)):
                rows = row_iota(size) + (row - LEFT + place)
                keep = (rows >= begin) & (rows < stop)
                for g in range(TILES):
                    x = x_ref[pl.ds(pl.multiple_of(source, 16), size), tile(g)].astype(F32)
                    window[g, pl.ds(place, size), :] = jnp.where(keep, x, 0.0)

            def per_rows(base, n):
                for g in range(TILES):
                    acc = conv_rows(window, taps, g, base, n)
                    total, square = sums[g, pl.ds(0, 8), :], sums[g, pl.ds(8, 8), :]
                    for v in range(n):
                        at = row_of(v, n) + (row + base)
                        h = jnp.where((at >= begin) & (at < stop), acc[v], 0.0)
                        total = total + h
                        square = square + h * h
                    sums[g, pl.ds(0, 8), :] = total
                    sums[g, pl.ds(8, 8), :] = square

            in_rows(low + 1 == high, begin - row, stop - row, per_rows)
            return inner

        return lax.fori_loop(low, high, part, carry)

    lax.fori_loop(0, end // BLOCK, block, 0)
    for g in range(TILES):
        for i in range(2):
            part = sums[g, pl.ds(8 * i, 8), :]
            out_ref[pl.ds(i, 1), tile(g)] = jnp.sum(part, axis=0, keepdims=True)


def stats(bounds, x, kern, earlier):
    width = x.shape[1]
    return pl.pallas_call(
        stats_kernel,
        grid=(width // WIDE,),
        out_shape=(
            jax.ShapeDtypeStruct((2, width), F32),
            jax.ShapeDtypeStruct((KER, width), F32),
        ),
        in_specs=[
            SMEM_SPEC,
            pl.BlockSpec((NB * BLOCK, WIDE), lambda c: (0, c)),
            pl.BlockSpec((KER, WIDE), lambda c: (0, c)),
            pl.BlockSpec(memory_space=pl.ANY),
        ],
        out_specs=(
            pl.BlockSpec((2, WIDE), lambda c: (0, c)),
            pl.BlockSpec((KER, WIDE), lambda c: (0, c)),
        ),
        scratch_shapes=[
            pltpu.VMEM((TILES, WIN, LANES), F32),
            pltpu.VMEM((TILES, 8 * KER, LANES), F32),
            pltpu.VMEM((TILES, 16, LANES), F32),
        ],
        cost_estimate=cost(15),
        name="stats",
    )(bounds, x, kern, earlier)


def live_parts(info_ref, got_ref, window, per_part, per_block=None):
    def slot(s, n):
        valid = info_ref[5 * s] > 0

        @pl.when(valid)
        def _():
            at = pl.multiple_of(n * BLOCK, BLOCK)
            low, high = utterances(info_ref[5 * s + 2], info_ref[5 * s + 3], LEFT)

            def part(u, carry):
                begin, stop = info_ref[5 * s + 1 + u], info_ref[5 * s + 2 + u]
                rows = row_iota(WIN)
                keep = (rows >= begin) & (rows < stop)
                for g in range(TILES):
                    x = got_ref[s, :, tile(g)].astype(F32)
                    window[g] = jnp.where(keep, x, 0.0)
                begin, stop = begin - LEFT, stop - LEFT

                def per_rows(base, groups):
                    per_part(at + base, begin - base, stop - base, base, groups)

                in_rows(low + 1 == high, begin, stop, per_rows)
                return carry

            lax.fori_loop(low, high, part, 0)
            if per_block is not None:
                per_block(at)

        return n + valid.astype(jnp.int32)

    lax.fori_loop(0, 16, slot, 0)


def hidden_kernel(info_ref, got_ref, kern_ref, norm_ref, *rest):
    h_ref, sw_ref, window, taps = rest[-4:]
    spread_taps(kern_ref, taps)

    def per_part(at, begin, stop, base, n):
        for g in range(TILES):
            acc = conv_rows(window, taps, g, base, n)
            for v in range(n):
                place = pl.ds(at + v, 8, stride=n)
                keep = (row_of(v, n) >= begin) & (row_of(v, n) < stop)
                h_ref[g, place, :] = jnp.where(keep, acc[v], h_ref[g, place, :])

    def per_block(at):
        for g in range(TILES):
            mean, inverse = norm_ref[pl.ds(0, 1), tile(g)], norm_ref[pl.ds(1, 1), tile(g)]
            scale, shift = norm_ref[pl.ds(2, 1), tile(g)], norm_ref[pl.ds(3, 1), tile(g)]
            a = (h_ref[g, pl.ds(at, BLOCK), :] - mean) * inverse * scale + shift
            sw_ref[pl.ds(at, BLOCK), tile(g)] = (a * jax.nn.sigmoid(a)).astype(BF16)

    live_parts(info_ref, got_ref, window, per_part, per_block)


def hidden(info, got, kern, norm, *earlier):
    width = got.shape[2]
    rows = BLOCKS * BLOCK
    return pl.pallas_call(
        hidden_kernel,
        grid=(width // WIDE,),
        out_shape=(
            jax.ShapeDtypeStruct((width // LANES, rows, LANES), F32),
            jax.ShapeDtypeStruct((rows, width), BF16),
        ),
        in_specs=[
            SMEM_SPEC,
            pl.BlockSpec((16, WIN, WIDE), lambda c: (0, 0, c)),
            pl.BlockSpec((KER, WIDE), lambda c: (0, c)),
            pl.BlockSpec((4, WIDE), lambda c: (0, c)),
        ]
        + [pl.BlockSpec(memory_space=pl.ANY)] * len(earlier),
        out_specs=(
            pl.BlockSpec((TILES, rows, LANES), lambda c: (c, 0, 0)),
            pl.BlockSpec((rows, WIDE), lambda c: (0, c)),
        ),
        scratch_shapes=[pltpu.VMEM((TILES, WIN, LANES), F32), pltpu.VMEM((TILES, 8 * KER, LANES), F32)],
        cost_estimate=cost(16),
        name="hidden",
    )(info, got, kern, norm, *earlier)


def terms_kernel(
    info_ref, got_ref, h_ref, wide_back, norm_ref, out_ref, window, back_ref, acc_a, acc_x, sums
):
    for g in range(TILES):
        back_ref[g] = wide_back[:, tile(g)]
    acc_a[...] = jnp.zeros_like(acc_a)
    acc_x[...] = jnp.zeros_like(acc_x)
    sums[...] = jnp.zeros_like(sums)

    def per_tile(g, at, begin, stop, base, n):
        mean, inverse = norm_ref[pl.ds(0, 1), tile(g)], norm_ref[pl.ds(1, 1), tile(g)]
        scale, shift = norm_ref[pl.ds(2, 1), tile(g)], norm_ref[pl.ds(3, 1), tile(g)]
        das, hats = [], []
        sum_x, sum_1 = sums[g, pl.ds(0, 8), :], sums[g, pl.ds(8, 8), :]
        for v in range(n):
            place = pl.ds(at + v, 8, stride=n)
            keep = (row_of(v, n) >= begin) & (row_of(v, n) < stop)
            hat = (h_ref[g, place, :] - mean) * inverse
            a = hat * scale + shift
            sig = jax.nn.sigmoid(a)
            da = back_ref[g, place, :] * (sig * (1.0 + a * (1.0 - sig)))
            da = jnp.where(keep, da, 0.0)
            hat = jnp.where(keep, hat, 0.0)
            sum_x = sum_x + da * hat
            sum_1 = sum_1 + da
            das.append(da)
            hats.append(hat)
        sums[g, pl.ds(0, 8), :] = sum_x
        sums[g, pl.ds(8, 8), :] = sum_1
        xs = [shifted(window, g, base + w, n) for w in range(n - 1)]
        for k in range(KER):
            xs.append(shifted(window, g, base + k + n - 1, n))
            place = pl.ds(8 * k, 8)
            for acc, rows in ((acc_a, das), (acc_x, hats)):
                terms_k = [rows[v] * xs[v] for v in range(n)]
                while len(terms_k) > 1:
                    terms_k = [p + q for p, q in zip(terms_k[::2], terms_k[1::2])]
                acc[g, place, :] += terms_k[0]
            xs.pop(0)

    def per_part(at, begin, stop, base, n):
        for g in range(TILES):
            per_tile(g, at, begin, stop, base, n)

    live_parts(info_ref, got_ref, window, per_part)
    for g in range(TILES):
        for acc, first in ((acc_a, 0), (acc_x, KER)):
            rows = acc[g].reshape(KER, 8, LANES)
            out_ref[pl.ds(first, KER), tile(g)] = jnp.sum(rows, axis=1)
        for i in range(2):
            part = sums[g, pl.ds(8 * i, 8), :]
            out_ref[pl.ds(2 * KER + i, 1), tile(g)] = jnp.sum(part, axis=0, keepdims=True)
    out_ref[pl.ds(66, 6), :] = jnp.zeros((6, WIDE), F32)


def terms(info, got, h, back, norm):
    width = got.shape[2]
    return pl.pallas_call(
        terms_kernel,
        grid=(width // WIDE,),
        out_shape=jax.ShapeDtypeStruct((72, width), F32),
        in_specs=[
            SMEM_SPEC,
            pl.BlockSpec((16, WIN, WIDE), lambda c: (0, 0, c)),
            pl.BlockSpec((TILES, BLOCKS * BLOCK, LANES), lambda c: (c, 0, 0)),
            pl.BlockSpec((BLOCKS * BLOCK, WIDE), lambda c: (0, c)),
            pl.BlockSpec((4, WIDE), lambda c: (0, c)),
        ],
        out_specs=pl.BlockSpec((72, WIDE), lambda c: (0, c)),
        scratch_shapes=[
            pltpu.VMEM((TILES, WIN, LANES), F32),
            pltpu.VMEM((TILES, BLOCKS * BLOCK, LANES), F32),
            pltpu.VMEM((TILES, 8 * KER, LANES), F32),
            pltpu.VMEM((TILES, 8 * KER, LANES), F32),
            pltpu.VMEM((TILES, 16, LANES), F32),
        ],
        cost_estimate=cost(25),
        name="terms",
    )(info, got, h, back, norm)


def zero_step(step):
    if step < 4:
        return [(i, i ^ step) for i in range(16)]
    return [(i, (i + step) % 16) for i in range(16)]


def dp_step(step, row):
    if row:
        return [(i, 4 * (i // 4) + (i + step) % 4) for i in range(16)]
    return [(i, (i + 4 * step) % 16) for i in range(16)]


def add_from(x, axis, steps, *meanwhile):
    parts = [lax.ppermute(x, axis, step) for step in steps]
    parts, meanwhile = lax.optimization_barrier((parts, meanwhile))
    return sum(parts, x), meanwhile


def gather_small(x, zero_id, meanwhile):
    for step, first in ((1, zero_id % 2 == 0), (2, (zero_id // 2) % 2 == 0)):
        other = lax.ppermute(x, "zero", zero_step(step))
        other, meanwhile = lax.optimization_barrier((other, meanwhile))
        x = jnp.stack([jnp.where(first, x, other), jnp.where(first, other, x)])
    pairs = [x] + [lax.ppermute(x, "zero", zero_step(step)) for step in (4, 8, 12)]
    place = zero_id // 4
    parts = []
    for q in range(4):
        part = pairs[0]
        for s in range(1, 4):
            part = jnp.where((place - s) % 4 == q, pairs[s], part)
        parts.append(part)
    return jnp.stack(parts).reshape((16,) + x.shape[2:])


def per_device(frames, segments, targets, cotangent, w_out, kernel, norm_params):
    x, seg, target_row, cot = frames[0, 0], segments[0, 0], targets[0, 0], cotangent[0, 0]
    width = x.shape[1]
    share = width // 16
    zero_id = lax.axis_index("zero")
    core = lax.rem(zero_id, 2)

    bounds, info = places(
        target_row, lax.axis_index("dp").reshape(1), seg.reshape(NB // 2, 2 * BLOCK), width
    )
    send = pack(target_row, x)
    small = jnp.concatenate([kernel, norm_params, jnp.zeros((14, share), BF16)], axis=0)
    got = lax.all_to_all(send, "dp", 0, 0, tiled=True)
    small_full = gather_small(small, zero_id, send)
    small_full = jnp.transpose(small_full, (1, 0, 2)).reshape(48, width).astype(F32)
    kern_full = small_full[:KER]

    w_t = lax.all_gather(w_out.T, "zero", axis=0, tiled=True)

    half = width // 2
    column = lax.broadcasted_iota(jnp.int32, (width, half), 0)
    place = lax.broadcasted_iota(jnp.int32, (width, half), 1)
    even = column == place + share * (place // share)
    odd = column == place + share * (place // share) + share
    own_columns = jnp.where(core == 0, even, odd).astype(BF16)
    other_columns = jnp.where(core == 0, odd, even).astype(BF16)
    swap = [(i, i ^ 1) for i in range(16)]

    sums, x_sums = stats(bounds, x, kern_full, send)
    for steps in ((1,), (2,), (4, 8, 12)):
        sums, _ = add_from(sums, "zero", [zero_step(step) for step in steps])
    sums = jnp.concatenate([sums, info], axis=0)
    sums, cot = lax.optimization_barrier((sums, cot))
    cot_own = jnp.dot(cot, own_columns, preferred_element_type=F32).astype(BF16)
    cot_send = jnp.dot(cot, other_columns, preferred_element_type=F32).astype(BF16)
    back = jnp.dot(cot, w_t, preferred_element_type=F32)
    sums, (back, cot_own, cot_send) = add_from(
        sums, "dp", [dp_step(step, True) for step in (1, 2, 3)], back, cot_own, cot_send
    )
    cot_other = lax.ppermute(cot_send, "zero", swap)
    sums, _ = add_from(sums, "dp", [dp_step(step, False) for step in (1, 2, 3)])
    info = lax.dynamic_slice_in_dim(sums[2], lax.axis_index("dp") * 96, 80, 0).astype(jnp.int32)
    frame_count = jnp.float32(BLOCKS * BLOCK * 256)
    mean = sums[0] / frame_count
    var = sums[1] / frame_count - mean * mean
    inverse = lax.rsqrt(var + EPS)
    norm = jnp.stack([mean, inverse, small_full[KER], small_full[KER + 1]])

    h, sw = hidden(info, got, kern_full, norm, back, cot_other)
    sw_other = lax.ppermute(sw, "zero", swap)
    contract = (((0,), (0,)), ((), ()))
    term = lax.dot_general(sw, cot_own, contract, preferred_element_type=F32)
    sw_other, term = lax.optimization_barrier((sw_other, term))
    term = term + lax.dot_general(sw_other, cot_other, contract, preferred_element_type=F32)
    term = term.astype(BF16).reshape(16, share, half)
    term = lax.all_to_all(term, "dp", 0, 0, tiled=True)

    grads = terms(info, got, h, back, norm)
    out = lax.dot_general(
        sw, w_t, (((1,), (1,)), ((), ())), preferred_element_type=F32
    ).astype(BF16)

    grads = jnp.concatenate([grads, x_sums], axis=0).reshape(104, 8, 2, share)
    grads = jnp.transpose(grads, (2, 1, 0, 3))
    grads_other = lax.ppermute(
        lax.dynamic_index_in_dim(grads, 1 - core, 0, False), "zero", swap
    )
    grads = lax.dynamic_index_in_dim(grads, core, 0, False) + grads_other
    grads = grads.reshape(8, 78, LANES)
    term, grads = lax.optimization_barrier((term, grads))

    term = jnp.sum(term.astype(F32), axis=0).reshape(share, 8, share)
    term = jnp.transpose(term, (1, 0, 2)).reshape(8, 72, LANES)
    both = jnp.concatenate([term, grads], axis=1)
    both = lax.all_to_all(
        both,
        "zero",
        0,
        0,
        axis_index_groups=[[i for i in range(16) if i % 2 == c] for c in range(2)],
        tiled=True,
    )
    last = jnp.sum(both, axis=0)
    last = lax.all_to_all(
        jnp.broadcast_to(last[None], (16,) + last.shape), "dp", 0, 0, tiled=True
    )
    part_w = last[:, :72].reshape(width, share)
    grads = jnp.sum(last[:, 72:], axis=0).reshape(104, share)

    own = lax.dynamic_slice_in_dim(norm, zero_id * share, share, 1)
    da_x, hat_x, x_k = grads[:KER], grads[KER : 2 * KER], grads[72 : 72 + KER]
    sum_x, sum_1 = grads[64], grads[65]
    part_k = (own[2] * own[1]) * (da_x - (sum_1 / frame_count) * x_k - (sum_x / frame_count) * hat_x)
    return out[None, None], part_w, part_k, jnp.stack([sum_x, sum_1])


def solution(mesh):
    return jax.shard_map(
        per_device,
        mesh=mesh,
        in_specs=(
            P("dp", "zero", None, None),
            P("dp", "zero", None),
            P("dp", "zero", None),
            P("dp", "zero", None, None),
            P(None, "zero"),
            P(None, "zero"),
            P(None, "zero"),
        ),
        out_specs=(P("dp", "zero", None, None), P(None, "zero"), P(None, "zero"), P(None, "zero")),
        check_vma=False,
    )
```
